32 devices in a mesh: row: 8 (over z, y), col: 4 (over x, core).
Axes of the slice: x: 2, y: 2, z: 4, core: 2. Of those that a mesh axis runs over, the one named last changes fastest.
Arguments:
- delta: bfloat16 [16384, 7168], P('row', 'col'), may hold values from -0.0625 to 0.0625
- omega: bfloat16 [7168, 256], P('col'), may hold values from -6 to 6
Outputs:
- sketch: float32 [16384, 256], P('row')
- corange: float32 [7168, 256], P('col', 'row')
The draws below stay inside these ranges and needn't reach their ends.
All inputs are finite; a program needn't handle non-finite values.
Results may differ from the reference program's by a relative error of at most 0.0016.
Values sent between devices are 32-bit elements; how exact they have to be, the bound alone decides.
No kernel may reach another device: no remote copies, remote signals or barrier semaphores. Data moves between devices by JAX's collectives and lax.ppermute only.
A program may use at most 64 MiB of HBM per device.

```python
import jax
import jax.numpy as jnp
from jax import lax

D = 7168
K = 256
ROWS_DEV = 2048
ROWS = 16384
N_ROW = 8


def steps_of(rng, dims, shards, smallest, high):
    loudness, own = 1.0, jax.random.fold_in(rng, 6)
    for position, blocks in shards:
        heights = jnp.exp(jax.random.uniform(jax.random.fold_in(own, position), (blocks,), jnp.float32, smallest / len(shards), high / len(shards)))
        loudness = loudness * jnp.repeat(heights, dims[position] // blocks).reshape([-1 if axis == position else 1 for axis in range(len(dims))])
    return loudness


def gaussian(key, dims, spread, bound, cuts=(), held_as=jnp.bfloat16):
    values = spread * jax.random.normal(key, dims, jnp.float32)
    if cuts:
        values = values * steps_of(key, dims, cuts, -0.22, 0.18)
    return jnp.clip(values, -bound, bound).astype(held_as)


def setup_inputs(seed: int = 0) -> dict:
    key_of = jax.random.split(jax.random.key(seed), 3)
    return {
        "delta": gaussian(key_of[0], (ROWS, D), (D ** -0.5), 0.0625, ((0, 8), (1, 4))),
        "omega": gaussian(key_of[1], (D, K), 1.0, 6.0, ((0, 4),)),
    }


def reference(delta, omega):
    blocks = delta.reshape(N_ROW, ROWS_DEV, D)
    omega_wide = omega.astype(jnp.float32)

    def step(total, block):
        block_wide = block.astype(jnp.float32)
        partial_value = jnp.dot(block_wide, omega_wide, precision=lax.Precision.HIGHEST, preferred_element_type=jnp.float32)
        rounded = partial_value.astype(jnp.bfloat16).astype(jnp.float32)
        total = total + jnp.dot(block_wide.T, rounded, precision=lax.Precision.HIGHEST, preferred_element_type=jnp.float32)
        return total, partial_value

    corange, sketch = lax.scan(step, jnp.zeros((D, K), jnp.float32), blocks)
    return sketch.reshape(ROWS, K), corange
```

```python
import functools

import jax
import jax.numpy as jnp
from jax import lax
from jax.experimental import pallas as pl
from jax.experimental.pallas import tpu as pltpu
from jax.sharding import PartitionSpec as P

CHUNKS = 4
BLOCK = 256
F32 = jnp.float32
BF16 = jnp.bfloat16
NT = (((1,), (1,)), ((), ()))
NN = (((1,), (0,)), ((), ()))


def vmem(shape, dtype=F32):
    return pltpu.VMEM(shape, dtype)


def call(body, ins, outs, scratch=(), flops=0, moved=0, limit=16):
    spec = {"v": pl.BlockSpec(memory_space=pltpu.VMEM), "a": pl.BlockSpec(memory_space=pl.ANY)}
    return pl.pallas_call(
        body,
        out_shape=[vmem(*shape) for shape in outs],
        in_specs=[spec[kind] for kind in ins],
        out_specs=[spec["v"]] * len(outs),
        scratch_shapes=list(scratch),
        cost_estimate=pl.CostEstimate(flops=flops, bytes_accessed=moved, transcendentals=0),
        compiler_params=pltpu.CompilerParams(vmem_limit_bytes=limit << 20),
    )


def column_of(position, k, chunks, n_row):
    width = k // chunks
    mine = k // n_row
    piece = mine // chunks
    chunk, rest = position // width, position % width
    low, rest = rest // (width // 2), rest % (width // 2)
    high, j = rest // piece, rest % piece
    return (2 * high + low) * mine + chunk * piece + j


def stream_half(delta, held, sem, first, rows):
    copies = []
    for b in range(rows // BLOCK):
        copies.append(
            pltpu.make_async_copy(
                delta.at[pl.ds(pl.multiple_of(first + b * BLOCK, BLOCK), BLOCK), :],
                held.at[pl.ds(b * BLOCK, BLOCK), :],
                sem.at[b],
            )
        )
        copies[-1].start()
    return copies


def send_half_body(n_row, delta, omega, held, omega_t, out, omega_v, sem, omega_sem):
    rows, k = held.shape[0], omega_t.shape[0]
    other = 1 - lax.rem(lax.axis_index("col"), 2)
    fetch = pltpu.make_async_copy(omega, omega_v, omega_sem)
    fetch.start()
    copies = stream_half(delta, held, sem, other * rows, rows)
    position = lax.broadcasted_iota(jnp.int32, (k, k), 0)
    column = lax.broadcasted_iota(jnp.int32, (k, k), 1)
    pick = jnp.where(column_of(position, k, CHUNKS, n_row) == column, 1.0, 0.0).astype(BF16)
    fetch.wait()
    omega_t[...] = lax.dot_general(pick, omega_v[...], NT, preferred_element_type=F32).astype(BF16)
    for b, copy in enumerate(copies):
        copy.wait()
        block = pl.ds(b * BLOCK, BLOCK)
        out[:, block] = lax.dot_general(omega_t[...], held[block, :], NT, preferred_element_type=F32)


def keep_half_body(delta, omega_t, held, out, sem):
    rows = held.shape[0]
    copies = stream_half(delta, held, sem, lax.rem(lax.axis_index("col"), 2) * rows, rows)
    for b, copy in enumerate(copies):
        copy.wait()
        block = pl.ds(b * BLOCK, BLOCK)
        out[:, block] = lax.dot_general(omega_t[...], held[block, :], NT, preferred_element_type=F32)


def add_chunks_body(kept, received, *outs):
    width = outs[0].shape[0]
    for c, out in enumerate(outs):
        part = pl.ds(c * width, width)
        out[...] = kept[part, :] + received[part, :]


def add_body(a, b, out):
    out[...] = a[...] + b[...]


def corange_body(own, other, held_own, held_other, send, keep):
    half = send.shape[0]
    low = lax.rem(lax.axis_index("row"), 2)
    theirs = pl.ds(pl.multiple_of((1 - low) * half, half), half)
    mine = pl.ds(pl.multiple_of(low * half, half), half)

    def ordered(ref):
        return jnp.concatenate([ref[theirs, :], ref[mine, :]], axis=0).astype(BF16)

    total = lax.dot_general(ordered(own), held_own[...], NN, preferred_element_type=F32)
    total += lax.dot_general(ordered(other), held_other[...], NN, preferred_element_type=F32)
    send[...] = total[:half]
    keep[...] = total[half:]


def split_high_body(n_high, kept, received, *outs):
    width = outs[0].shape[0]
    high = lax.axis_index("row") // 2
    for d, out in enumerate(outs):
        part = pl.ds(pl.multiple_of(lax.rem(high + d, n_high) * width, width), width)
        out[...] = kept[part, :] + received[part, :]


def final_corange_body(chunks, *refs):
    out = refs[-1]
    per = (len(refs) - 1) // chunks
    width = refs[0].shape[0]
    for c in range(chunks):
        parts = refs[c * per : (c + 1) * per]
        total = parts[0][...]
        for part in parts[1:]:
            total += part[...]
        out[pl.ds(c * width, width), :] = total


def final_sketch_body(chunks, n_row, *refs):
    out = refs[-1]
    rows = refs[0].shape[1]
    width = refs[0].shape[0]
    piece = width // n_row
    parity = lax.rem(lax.axis_index("col"), 2)
    for side in range(2):
        parts = refs[side * chunks : (side + 1) * chunks]
        first = (parity if side == 0 else 1 - parity) * rows
        for b in range(rows // 128):
            lanes = pl.ds(b * 128, 128)
            pieces = []
            for r in range(n_row):
                start = (r % 2) * (width // 2) + (r // 2) * piece
                for part in parts:
                    pieces.append(part[pl.ds(start, piece), lanes])
            block = jnp.concatenate(pieces, axis=0)
            out[pl.ds(pl.multiple_of(first + b * 128, 128), 128), :] = block.T


def swap(x, axis, size, bit):
    return lax.ppermute(x, axis, [(i, i ^ bit) for i in range(size)])


def shards(n_row, n_col, delta, omega):
    rows, d = delta.shape
    k = omega.shape[1]
    half = rows // 2
    width = k // CHUNKS
    n_high = n_row // 2
    piece = width // n_row
    blocks = half // BLOCK
    mm = 2 * half * d * k

    held_other, omega_t, to_send = call(
        functools.partial(send_half_body, n_row),
        "aa",
        [((half, d), BF16), ((k, d), BF16), ((k, half),)],
        [pltpu.VMEM((d, k), BF16), pltpu.SemaphoreType.DMA((blocks,)), pltpu.SemaphoreType.DMA],
        mm,
        2 * half * d,
    )(delta, omega)
    received = swap(to_send, "col", n_col, 1)
    held_own, kept = call(
        keep_half_body,
        "av",
        [((half, d), BF16), ((k, half),)],
        [pltpu.SemaphoreType.DMA((blocks,))],
        mm,
        2 * half * d,
    )(delta, omega_t)
    partial = call(add_chunks_body, "vv", [((width, half),)] * CHUNKS, (), k * half, 12 * k * half)(kept, received)
    owns, others = [], []
    terms = []
    bit = 2
    while bit < n_col:
        moved = [swap(x, "col", n_col, bit) for x in partial]
        partial = [call(add_body, "vv", [((width, half),)], (), width * half, 12 * width * half)(a, b)[0] for a, b in zip(partial, moved)]
        bit *= 2
    for own in partial:
        other = swap(own, "col", n_col, 1)
        owns.append(own)
        others.append(other)
        send, keep = call(
            corange_body,
            "vvvv",
            [((width // 2, d),), ((width // 2, d),)],
            (),
            4 * half * d * width,
            4 * half * d,
        )(own, other, held_own, held_other)
        got = swap(send, "row", n_row, 1)
        if piece % 8 == 0:
            parts = call(
                functools.partial(split_high_body, n_high),
                "vv",
                [((piece, d),)] * n_high,
                (),
                width * d,
                6 * width * d,
            )(keep, got)
        else:
            total = keep + got
            high = lax.axis_index("row") // 2
            parts = [lax.dynamic_slice_in_dim(total, lax.rem(high + i, n_high) * piece, piece, 0) for i in range(n_high)]
        parts = list(parts)
        for shift in range(1, n_high):
            pairs = [(r, 2 * ((r // 2 + shift) % n_high) + r % 2) for r in range(n_row)]
            parts[shift] = lax.ppermute(parts[shift], "row", pairs)
        terms.append(parts)

    if piece % 8 == 0:
        flat = [x for parts in terms for x in parts]
        corange = pl.pallas_call(
            functools.partial(final_corange_body, CHUNKS),
            out_shape=jax.ShapeDtypeStruct((k // n_row, d), F32),
        )(*flat)
        sketch = pl.pallas_call(
            functools.partial(final_sketch_body, CHUNKS, n_row),
            out_shape=jax.ShapeDtypeStruct((rows, k), F32),
        )(*owns, *others)
    else:
        corange = jnp.concatenate([functools.reduce(jnp.add, parts) for parts in terms], axis=0)
        parity = lax.rem(lax.axis_index("col"), 2)

        def columns(parts):
            stacked = jnp.stack(parts).reshape(CHUNKS, 2, n_high, piece, half)
            return stacked.transpose(4, 2, 1, 0, 3).reshape(half, k)

        own, other = columns(owns), columns(others)
        sketch = jnp.where(parity == 0, jnp.concatenate([own, other]), jnp.concatenate([other, own]))
    return sketch, corange.T


def solution(mesh):
    body = functools.partial(shards, mesh.shape["row"], mesh.shape["col"])
    in_specs = (P("row", "col"), P("col", None))
    out_specs = (P("row", None), P("col", "row"))
    return jax.shard_map(body, mesh=mesh, in_specs=in_specs, out_specs=out_specs, check_vma=False)
```

```python
import functools

import jax
import jax.numpy as jnp
from jax import lax
from jax.experimental import pallas as pl
from jax.experimental.pallas import tpu as pltpu
from jax.sharding import PartitionSpec as P

CHUNKS = 4
WEIGHTS = (20000000000, 2000000000, 4000000000, 4000000000, 4000000000, 100000000, 2000000000, 1000000000, 10000000000)
BLOCK = 256
F32 = jnp.float32
BF16 = jnp.bfloat16
SPECS = {
    "v": pl.BlockSpec(memory_space=pltpu.VMEM),
    "h": pl.BlockSpec(memory_space=pltpu.HBM),
    "a": pl.BlockSpec(memory_space=pl.ANY),
}


def call(body, args, outs, kinds=None, after=(), scratch=(), results=0, weight=0):
    n = len(args)
    kinds = (kinds or "v" * n) + "a" * len(after)

    def run(*refs):
        body(*refs[:n], *refs[len(kinds) :])

    return pl.pallas_call(
        run,
        out_shape=[pltpu.VMEM(*o) if i >= results else jax.ShapeDtypeStruct(*o) for i, o in enumerate(outs)],
        in_specs=[SPECS[kind] for kind in kinds],
        out_specs=[SPECS["v"]] * len(outs),
        scratch_shapes=list(scratch),
        cost_estimate=pl.CostEstimate(flops=weight, bytes_accessed=0, transcendentals=0),
        compiler_params=pltpu.CompilerParams(vmem_limit_bytes=16 << 20),
    )(*args, *after)


def owner_at(index, n_row):
    owner, bit = 0, 1
    while bit < n_row:
        owner = 2 * owner + index % 2
        index //= 2
        bit *= 2
    return owner


def sketch_half_body(n_row, mine, delta, omega, held, out, omega_v, sem, omega_sem):
    rows, k = held.shape[0], out.shape[0]
    parity = lax.rem(lax.axis_index("col"), 2)
    first = (parity if mine else 1 - parity) * rows
    fetch = pltpu.make_async_copy(omega, omega_v, omega_sem)
    fetch.start()
    copies = []
    for b in range(rows // BLOCK):
        source = delta.at[pl.ds(pl.multiple_of(first + b * BLOCK, BLOCK), BLOCK), :]
        copies.append(pltpu.make_async_copy(source, held.at[pl.ds(b * BLOCK, BLOCK), :], sem.at[b]))
        copies[-1].start()
    fetch.wait()
    per_owner = k // n_row
    piece = per_owner // CHUNKS
    for b, copy in enumerate(copies):
        copy.wait()
        lanes = pl.ds(b * BLOCK, BLOCK)
        turned = jnp.dot(held[lanes, :], omega_v[...], preferred_element_type=F32).T
        for c in range(CHUNKS):
            for i in range(n_row):
                start = owner_at(i, n_row) * per_owner + c * piece
                out[pl.ds((c * n_row + i) * piece, piece), lanes] = turned[start : start + piece]


def add_chunks_body(kept, received, *outs):
    width = outs[0].shape[0]
    for c, out in enumerate(outs):
        part = pl.ds(c * width, width)
        out[...] = kept[part, :] + received[part, :]


def add_body(a, b, out):
    out[...] = a[...] + b[...]


def product_body(n_row, sketch, held, out):
    out[...] = jnp.dot(sketch[...].astype(BF16), held[...], preferred_element_type=F32)


def halves(bit, ref):
    half = ref.shape[0] // 2
    own = lax.rem(lax.axis_index("row") // bit, 2)
    if half % 8:
        low, high = ref[:half, :], ref[half:, :]
        return jnp.where(own == 0, high, low), jnp.where(own == 0, low, high)
    theirs = pl.ds(pl.multiple_of((1 - own) * half, half), half)
    mine = pl.ds(pl.multiple_of(own * half, half), half)
    return ref[theirs, :], ref[mine, :]


def product_send_body(sketch, held, before, send, keep):
    half = send.shape[0]
    ordered = jnp.concatenate(halves(1, sketch), axis=0).astype(BF16)
    total = jnp.dot(ordered, held[...], preferred_element_type=F32)
    theirs, mine = halves(1, before)
    send[...] = total[:half] + theirs
    keep[...] = total[half:] + mine


def add_send_body(bit, kept, received, send, keep):
    for out, a, b in zip((send, keep), halves(bit, kept), halves(bit, received)):
        out[...] = a + b


def final_corange_body(*refs):
    out = refs[-1]
    width = refs[0].shape[0]
    for c in range(len(refs) // 2):
        out[pl.ds(c * width, width), :] = refs[2 * c][...] + refs[2 * c + 1][...]


def final_sketch_body(n_row, *refs):
    out, done = refs[-2:]
    width, rows = refs[0].shape
    piece = width // n_row
    parity = lax.rem(lax.axis_index("col"), 2)
    for side in range(2):
        parts = refs[side * CHUNKS : (side + 1) * CHUNKS]
        first = (parity if side == 0 else 1 - parity) * rows
        for b in range(rows // 128):
            lanes = pl.ds(b * 128, 128)
            pieces = []
            for r in range(n_row):
                start = owner_at(r, n_row) * piece
                pieces.extend(part[pl.ds(start, piece), lanes] for part in parts)
            block = jnp.concatenate(pieces, axis=0)
            out[pl.ds(pl.multiple_of(first + b * 128, 128), 128), :] = block.T
    done[...] = jnp.zeros_like(done)


def swap(x, axis, size, bit):
    return lax.ppermute(x, axis, [(i, i ^ bit) for i in range(size)])


def shards(n_row, n_col, delta, omega):
    rows, d = delta.shape
    k = omega.shape[1]
    half = rows // 2
    width = k // CHUNKS
    piece = width // n_row

    def sketch_half(mine, after):
        return call(
            functools.partial(sketch_half_body, n_row, mine),
            (pltpu.with_memory_space_constraint(delta, pltpu.HBM), pltpu.with_memory_space_constraint(omega, pltpu.HBM)),
            [((half, d), BF16), ((k, half), F32)],
            "hh",
            after,
            [pltpu.VMEM((d, k), BF16), pltpu.SemaphoreType.DMA((half // BLOCK,)), pltpu.SemaphoreType.DMA],
            weight=WEIGHTS[0],
        )

    held_other, to_send = sketch_half(False, ())
    received = swap(to_send, "col", n_col, 1)
    held_own, kept = sketch_half(True, (to_send,))
    partial = call(add_chunks_body, (kept, received), [((width, half), F32)] * CHUNKS, weight=WEIGHTS[1])
    bit = 2
    while bit < n_col // 2:
        moved = [swap(x, "col", n_col, bit) for x in partial]
        partial = [call(add_body, pair, [((width, half), F32)])[0] for pair in zip(partial, moved)]
        bit *= 2
    moved = [swap(x, "col", n_col, bit) for x in partial]

    bits = [1 << i for i in range(n_row.bit_length() - 1)]
    stages = len(bits)
    owns, others = [], []
    pending = {}
    last = ()

    def reduce_step(c, s):
        nonlocal last
        kept, got = pending[c]
        wide = width >> (s + 2)
        send, keep = call(
            functools.partial(add_send_body, bits[s + 1]), (kept, got), [((wide, d), F32)] * 2, after=last, weight=WEIGHTS[5 + min(s, 1)]
        )
        last = (keep,)
        pending[c] = keep, swap(send, "row", n_row, bits[s + 1])

    for c in range(CHUNKS + stages - 1):
        if c < CHUNKS:
            own = call(add_body, (partial[c], moved[c]), [((width, half), F32)], after=last, weight=WEIGHTS[2])[0]
            other = swap(own, "col", n_col, 1)
            owns.append(own)
            others.append(other)
            before = call(functools.partial(product_body, n_row), (own, held_own), [((width, d), F32)], weight=WEIGHTS[3])[0]
            send, keep = call(product_send_body, (other, held_other, before), [((width // 2, d), F32)] * 2, weight=WEIGHTS[4])
            pending[c] = keep, swap(send, "row", n_row, bits[0])
            last = (keep,)
        if c == CHUNKS - 1:
            sketch, done = finish_sketch(n_row, k, owns, others, last)
            last = (done,)
        for s in range(stages - 1):
            if 0 <= c - 1 - s < CHUNKS:
                reduce_step(c - 1 - s, s)
    if piece % 8 == 0:
        flat = [x for c in range(CHUNKS) for x in pending[c]]
        corange = call(final_corange_body, flat, [((k // n_row, d), F32)], results=1, weight=WEIGHTS[8])[0]
    else:
        corange = jnp.concatenate([kept + got for kept, got in (pending[c] for c in range(CHUNKS))], axis=0)
    return sketch, corange.T


def finish_sketch(n_row, k, owns, others, after):
    width, half = owns[0].shape
    piece = width // n_row
    if piece % 8 == 0:
        body = functools.partial(final_sketch_body, n_row)
        return call(body, (*owns, *others), [((2 * half, k), F32), ((8, 128), F32)], after=after, results=1, weight=WEIGHTS[7])
    places = [owner_at(r, n_row) for r in range(n_row)]

    def columns(parts):
        stacked = jnp.stack(parts).reshape(CHUNKS, n_row, piece, half)[:, jnp.array(places)]
        return stacked.transpose(3, 1, 0, 2).reshape(half, k)

    own, other = columns(owns), columns(others)
    first = lax.rem(lax.axis_index("col"), 2) == 0
    return jnp.where(first, jnp.concatenate([own, other]), jnp.concatenate([other, own])), after[0]


def solution(mesh):
    body = functools.partial(shards, mesh.shape["row"], mesh.shape["col"])
    in_specs = (P("row", "col"), P("col", None))
    out_specs = (P("row", None), P("col", "row"))
    return jax.shard_map(body, mesh=mesh, in_specs=in_specs, out_specs=out_specs, check_vma=False)
```

```python
import functools

import jax
import jax.numpy as jnp
from jax import lax
from jax.experimental import pallas as pl
from jax.experimental.pallas import tpu as pltpu
from jax.sharding import PartitionSpec as P

CHUNKS = 4
LAG = 2
BLOCK = 256
F32 = jnp.float32
BF16 = jnp.bfloat16
SPECS = {
    "v": pl.BlockSpec(memory_space=pltpu.VMEM),
    "h": pl.BlockSpec(memory_space=pltpu.HBM),
    "a": pl.BlockSpec(memory_space=pl.ANY),
}


def call(body, args, outs, kinds=None, after=(), scratch=(), results=0):
    n = len(args)
    kinds = (kinds or "v" * n) + "a" * len(after)

    def run(*refs):
        body(*refs[:n], *refs[len(kinds) :])

    return pl.pallas_call(
        run,
        out_shape=[pltpu.VMEM(*o) if i >= results else jax.ShapeDtypeStruct(*o) for i, o in enumerate(outs)],
        in_specs=[SPECS[kind] for kind in kinds],
        out_specs=[SPECS["v"]] * len(outs),
        scratch_shapes=list(scratch),
        cost_estimate=pl.CostEstimate(flops=10**10, bytes_accessed=0, transcendentals=0),
        compiler_params=pltpu.CompilerParams(vmem_limit_bytes=16 << 20),
    )(*args, *after)


def owner_at(index, n_row):
    owner, bit = 0, 1
    while bit < n_row:
        owner = 2 * owner + index % 2
        index //= 2
        bit *= 2
    return owner


def sketch_half_body(n_row, mine, delta, omega, held, out, omega_v, sem, omega_sem):
    rows, k = held.shape[0], out.shape[0]
    parity = lax.rem(lax.axis_index("col"), 2)
    first = (parity if mine else 1 - parity) * rows
    fetch = pltpu.make_async_copy(omega, omega_v, omega_sem)
    fetch.start()
    copies = []
    for b in range(rows // BLOCK):
        source = delta.at[pl.ds(pl.multiple_of(first + b * BLOCK, BLOCK), BLOCK), :]
        copies.append(pltpu.make_async_copy(source, held.at[pl.ds(b * BLOCK, BLOCK), :], sem.at[b]))
        copies[-1].start()
    fetch.wait()
    per_owner = k // n_row
    piece = per_owner // CHUNKS
    for b, copy in enumerate(copies):
        copy.wait()
        lanes = pl.ds(b * BLOCK, BLOCK)
        turned = jnp.dot(held[lanes, :], omega_v[...], preferred_element_type=F32).T
        for c in range(CHUNKS):
            for i in range(n_row):
                start = owner_at(i, n_row) * per_owner + c * piece
                out[pl.ds((c * n_row + i) * piece, piece), lanes] = turned[start : start + piece]


def add_chunks_body(kept, received, *outs):
    width = outs[0].shape[0]
    for c, out in enumerate(outs):
        part = pl.ds(c * width, width)
        out[...] = kept[part, :] + received[part, :]


def add_body(a, b, out):
    out[...] = a[...] + b[...]


def product_body(n_row, sketch, held, out):
    out[...] = jnp.dot(sketch[...].astype(BF16), held[...], preferred_element_type=F32)


def halves(bit, ref):
    half = ref.shape[0] // 2
    own = lax.rem(lax.axis_index("row") // bit, 2)
    if half % 8:
        low, high = ref[:half, :], ref[half:, :]
        return jnp.where(own == 0, high, low), jnp.where(own == 0, low, high)
    theirs = pl.ds(pl.multiple_of((1 - own) * half, half), half)
    mine = pl.ds(pl.multiple_of(own * half, half), half)
    return ref[theirs, :], ref[mine, :]


def product_send_body(sketch, held, before, send, keep):
    half = send.shape[0]
    ordered = jnp.concatenate(halves(1, sketch), axis=0).astype(BF16)
    total = jnp.dot(ordered, held[...], preferred_element_type=F32)
    theirs, mine = halves(1, before)
    send[...] = total[:half] + theirs
    keep[...] = total[half:] + mine


def add_send_body(bit, kept, received, send, keep):
    for out, a, b in zip((send, keep), halves(bit, kept), halves(bit, received)):
        out[...] = a + b


def final_corange_body(*refs):
    out = refs[-1]
    width = refs[0].shape[0]
    for c in range(len(refs) // 2):
        out[pl.ds(c * width, width), :] = refs[2 * c][...] + refs[2 * c + 1][...]


def final_sketch_body(n_row, *refs):
    out, done = refs[-2:]
    width, rows = refs[0].shape
    piece = width // n_row
    parity = lax.rem(lax.axis_index("col"), 2)
    for side in range(2):
        parts = refs[side * CHUNKS : (side + 1) * CHUNKS]
        first = (parity if side == 0 else 1 - parity) * rows
        for b in range(rows // 128):
            lanes = pl.ds(b * 128, 128)
            pieces = []
            for r in range(n_row):
                start = owner_at(r, n_row) * piece
                pieces.extend(part[pl.ds(start, piece), lanes] for part in parts)
            block = jnp.concatenate(pieces, axis=0)
            out[pl.ds(pl.multiple_of(first + b * 128, 128), 128), :] = block.T
    done[...] = jnp.zeros_like(done)


def swap(x, axis, size, bit):
    return lax.ppermute(x, axis, [(i, i ^ bit) for i in range(size)])


def shards(n_row, n_col, delta, omega):
    rows, d = delta.shape
    k = omega.shape[1]
    half = rows // 2
    width = k // CHUNKS
    piece = width // n_row

    def sketch_half(mine, after):
        return call(
            functools.partial(sketch_half_body, n_row, mine),
            (pltpu.with_memory_space_constraint(delta, pltpu.HBM), pltpu.with_memory_space_constraint(omega, pltpu.HBM)),
            [((half, d), BF16), ((k, half), F32)],
            "hh",
            after,
            [pltpu.VMEM((d, k), BF16), pltpu.SemaphoreType.DMA((half // BLOCK,)), pltpu.SemaphoreType.DMA],
        )

    held_other, to_send = sketch_half(False, ())
    received = swap(to_send, "col", n_col, 1)
    held_own, kept = sketch_half(True, (to_send,))
    partial = call(add_chunks_body, (kept, received), [((width, half), F32)] * CHUNKS)
    bit = 2
    while bit < n_col // 2:
        moved = [swap(x, "col", n_col, bit) for x in partial]
        partial = [call(add_body, pair, [((width, half), F32)])[0] for pair in zip(partial, moved)]
        bit *= 2
    moved = [swap(x, "col", n_col, bit) for x in partial]

    bits = [1 << i for i in range(n_row.bit_length() - 1)]
    stages = len(bits)
    owns, others = [], []
    pending = {}
    last = ()

    def reduce_step(c, s):
        nonlocal last
        kept, got = pending[c]
        wide = width >> (s + 2)
        send, keep = call(
            functools.partial(add_send_body, bits[s + 1]), (kept, got), [((wide, d), F32)] * 2, after=last
        )
        last = (keep,)
        pending[c] = keep, swap(send, "row", n_row, bits[s + 1])

    for c in range(CHUNKS + stages - 2 + LAG):
        if c < CHUNKS:
            own = call(add_body, (partial[c], moved[c]), [((width, half), F32)], after=last)[0]
            other = swap(own, "col", n_col, 1)
            owns.append(own)
            others.append(other)
            before = call(functools.partial(product_body, n_row), (own, held_own), [((width, d), F32)])[0]
            send, keep = call(product_send_body, (other, held_other, before), [((width // 2, d), F32)] * 2)
            pending[c] = keep, swap(send, "row", n_row, bits[0])
            last = (keep,)
        if c == CHUNKS - 1:
            sketch, done = finish_sketch(n_row, k, owns, others, last)
            last = (done,)
        for s in range(stages - 1):
            if 0 <= c - LAG - s < CHUNKS:
                reduce_step(c - LAG - s, s)
    if piece % 8 == 0:
        flat = [x for c in range(CHUNKS) for x in pending[c]]
        corange = call(final_corange_body, flat, [((k // n_row, d), F32)], results=1)[0]
    else:
        corange = jnp.concatenate([kept + got for kept, got in (pending[c] for c in range(CHUNKS))], axis=0)
    return sketch, corange.T


def finish_sketch(n_row, k, owns, others, after):
    width, half = owns[0].shape
    piece = width // n_row
    if piece % 8 == 0:
        body = functools.partial(final_sketch_body, n_row)
        return call(body, (*owns, *others), [((2 * half, k), F32), ((8, 128), F32)], after=after, results=1)
    places = [owner_at(r, n_row) for r in range(n_row)]

    def columns(parts):
        stacked = jnp.stack(parts).reshape(CHUNKS, n_row, piece, half)[:, jnp.array(places)]
        return stacked.transpose(3, 1, 0, 2).reshape(half, k)

    own, other = columns(owns), columns(others)
    first = lax.rem(lax.axis_index("col"), 2) == 0
    return jnp.where(first, jnp.concatenate([own, other]), jnp.concatenate([other, own])), after[0]


def solution(mesh):
    body = functools.partial(shards, mesh.shape["row"], mesh.shape["col"])
    in_specs = (P("row", "col"), P("col", None))
    out_specs = (P("row", None), P("col", "row"))
    return jax.shard_map(body, mesh=mesh, in_specs=in_specs, out_specs=out_specs, check_vma=False)
```

```python
import functools

import jax
import jax.numpy as jnp
from jax import lax
from jax.experimental import pallas as pl
from jax.experimental.pallas import tpu as pltpu
from jax.sharding import PartitionSpec as P

EIGHTHS = (2, 2, 2, 2)
BLOCK = 512
F32 = jnp.float32
BF16 = jnp.bfloat16
NT = (((1,), (1,)), ((), ()))
SPECS = {"v": pl.BlockSpec(memory_space=pltpu.VMEM), "a": pl.BlockSpec(memory_space=pl.ANY)}
E0 = 19.5
DE = 10
GT = 12.4
WEIGHT = 0
WQ = 0
WE = 5*10**8
WC = 0
WP = 0
SPLIT = 2
DIRECT = 1


def call(body, args, outs, kinds=None, after=(), scratch=(), results=0, weight=None):
    n = len(args)
    kinds = (kinds or "v" * n) + "a" * len(after)

    def run(*refs):
        body(*refs[:n], *refs[len(kinds) :])

    return pl.pallas_call(
        run,
        out_shape=[pltpu.VMEM(*o) if i >= results else jax.ShapeDtypeStruct(*o) for i, o in enumerate(outs)],
        in_specs=[SPECS[kind] for kind in kinds],
        out_specs=[SPECS["v"]] * len(outs),
        scratch_shapes=list(scratch),
        cost_estimate=pl.CostEstimate(flops=WEIGHT if weight is None else weight, bytes_accessed=0, transcendentals=0),
        compiler_params=pltpu.CompilerParams(vmem_limit_bytes=16 << 20),
    )(*args, *after)


def owner_at(index, n_row):
    owner, bit = index * 0, 1
    while bit < n_row:
        owner = 2 * owner + index % 2
        index = index // 2
        bit *= 2
    return owner


def column_of(position, k, n_row, pieces):
    column, first, done = position * 0, 0, 0
    for piece in pieces:
        rest = position - first
        found = owner_at(rest // piece, n_row) * (k // n_row) + done + rest % piece
        column = jnp.where((rest >= 0) & (rest < piece * n_row), found, column)
        first += piece * n_row
        done += piece
    return column


def stream_half(delta, held, sem, mine):
    rows = held.shape[0]
    parity = lax.rem(lax.axis_index("col"), 2)
    first = (parity if mine else 1 - parity) * rows
    copies = []
    for b in range(rows // BLOCK):
        source = delta.at[pl.ds(pl.multiple_of(first + b * BLOCK, BLOCK), BLOCK), :]
        copies.append(pltpu.make_async_copy(source, held.at[pl.ds(b * BLOCK, BLOCK), :], sem.at[b]))
        copies[-1].start()
    return copies


def sketch_half(omega_t, held, copies, out):
    for b, copy in enumerate(copies):
        copy.wait()
        block = pl.ds(b * BLOCK, BLOCK)
        out[:, block] = lax.dot_general(omega_t[...], held[block, :], NT, preferred_element_type=F32)


def first_half_body(n_row, pieces, delta, omega, held, omega_t, out, omega_v, sem, omega_sem):
    k = out.shape[0]
    fetch = pltpu.make_async_copy(omega, omega_v, omega_sem)
    fetch.start()
    copies = stream_half(delta, held, sem, False)
    position = lax.broadcasted_iota(jnp.int32, (k, k), 0)
    column = lax.broadcasted_iota(jnp.int32, (k, k), 1)
    pick = jnp.where(column_of(position, k, n_row, pieces) == column, 1.0, 0.0).astype(BF16)
    fetch.wait()
    omega_t[...] = lax.dot_general(pick, omega_v[...], NT, preferred_element_type=F32).astype(BF16)
    sketch_half(omega_t, held, copies, out)


def second_half_body(delta, omega_t, held, out, sem):
    sketch_half(omega_t, held, stream_half(delta, held, sem, True), out)


def add_chunks_body(kept, received, *outs):
    first = 0
    for out in outs:
        part = pl.ds(first, out.shape[0])
        out[...] = kept[part, :] + received[part, :]
        first += out.shape[0]


def add_body(a, b, *outs):
    first = 0
    for out in outs:
        part = pl.ds(first, out.shape[0])
        out[...] = a[part, :] + b[part, :]
        first += out.shape[0]


def joined(refs):
    return jnp.concatenate([ref[...] for ref in refs], axis=0)


def product_body(*refs):
    *sketch, held, out = refs
    out[...] = jnp.dot(joined(sketch).astype(BF16), held[...], preferred_element_type=F32)


def halves(bit, ref):
    half = ref.shape[0] // 2
    own = lax.rem(lax.axis_index("row") // bit, 2)
    if half % 8:
        low, high = ref[:half, :], ref[half:, :]
        return jnp.where(own == 0, high, low), jnp.where(own == 0, low, high)
    theirs = pl.ds(pl.multiple_of((1 - own) * half, half), half)
    mine = pl.ds(pl.multiple_of(own * half, half), half)
    return ref[theirs, :], ref[mine, :]


def product_send_body(*refs):
    *sketch, held, before, send, keep, total = refs
    total[...] = before[...] + jnp.dot(joined(sketch).astype(BF16), held[...], preferred_element_type=F32)
    send[...], keep[...] = halves(1, total)


def add_send_body(bit, kept, received, send, keep):
    for out, a, b in zip((send, keep), halves(bit, kept), halves(bit, received)):
        out[...] = a + b


def add_spread_body(n_high, kept, received, *outs):
    piece = outs[0].shape[0]
    place = owner_at(lax.axis_index("row") // 2, n_high)
    for flip, out in enumerate(outs):
        part = pl.ds(pl.multiple_of(lax.bitwise_xor(place, flip) * piece, piece), piece)
        out[...] = kept[part, :] + received[part, :]


def final_corange_body(counts, *refs):
    out = refs[-1]
    first, used = 0, 0
    for count in counts:
        terms = refs[used : used + count]
        piece = terms[0].shape[0]
        out[pl.ds(first, piece), :] = functools.reduce(jnp.add, [term[...] for term in terms])
        first += piece
        used += count


def final_sketch_body(n_row, pieces, *refs):
    out, done = refs[-2:]
    n, rows = len(refs) // 2 - 1, refs[0].shape[1]
    parity = lax.rem(lax.axis_index("col"), 2)
    per_part = n_row // SPLIT
    for side in range(2):
        parts = refs[side * n : (side + 1) * n]
        first = (parity if side == 0 else 1 - parity) * rows
        for b in range(rows // 128):
            lanes = pl.ds(b * 128, 128)
            found = []
            for r in range(n_row):
                place = owner_at(r, n_row)
                for c, piece in enumerate(pieces):
                    part = parts[c * SPLIT + place // per_part]
                    found.append(part[pl.ds(place % per_part * piece, piece), lanes])
            block = jnp.concatenate(found, axis=0)
            out[pl.ds(pl.multiple_of(first + b * 128, 128), 128), :] = block.T
    done[...] = jnp.zeros_like(done)


def swap(x, axis, size, bit):
    return lax.ppermute(x, axis, [(i, i ^ bit) for i in range(size)])


def shards(n_row, n_col, delta, omega):
    rows, d = delta.shape
    k = omega.shape[1]
    half = rows // 2
    per_owner = k // n_row
    pieces = [per_owner * part // sum(EIGHTHS) for part in EIGHTHS] if per_owner % 8 == 0 else [1] * per_owner
    widths = [piece * n_row for piece in pieces]
    n = len(pieces)
    bits = [1 << i for i in range(n_row.bit_length() - 1)]

    in_hbm = pltpu.with_memory_space_constraint(delta, pltpu.HBM)
    sems = pltpu.SemaphoreType.DMA((half // BLOCK,))
    held_other, omega_t, to_send = call(
        functools.partial(first_half_body, n_row, pieces),
        (in_hbm, pltpu.with_memory_space_constraint(omega, pltpu.HBM)),
        [((half, d), BF16), ((k, d), BF16), ((k, half), F32)],
        "aa",
        scratch=[pltpu.VMEM((d, k), BF16), sems, pltpu.SemaphoreType.DMA],
    )
    received = swap(to_send, "col", n_col, 1)
    held_own, kept = call(second_half_body, (in_hbm, omega_t), [((half, d), BF16), ((k, half), F32)], "av", scratch=[sems])
    partial = call(add_chunks_body, (kept, received), [((width, half), F32) for width in widths])
    bit = 2
    while bit < n_col // 2:
        moved = [swap(x, "col", n_col, bit) for x in partial]
        partial = [call(add_body, pair, [(pair[0].shape, F32)])[0] for pair in zip(partial, moved)]
        bit *= 2
    moved = [swap(x, "col", n_col, bit) for x in partial]

    owns, others, befores, pending = {}, {}, {}, {}
    sketch = None
    last = ()
    steps = []
    direct = [len(bits) == 3 and pieces[c] % 8 == 0 and c >= n - DIRECT for c in range(n)]
    for c in range(n):
        steps += [(10 * c, "own", c, 0), (10 * c + 1, "before", c, 0), (10 * c + 2, "send", c, 0)]
        steps += [(10 * c + E0 + DE * s, "add", c, s + 1) for s in range(1 if direct[c] else len(bits) - 1)]
    steps.append((10 * (n - 1) + GT, "sketch", 0, 0))
    for _, step, c, s in sorted(steps):
        width = widths[c]
        if step == "own":
            outs = [((width // SPLIT, half), F32)] * SPLIT
            owns[c] = call(add_body, (partial[c], moved[c]), outs, after=last, weight=WC)
            others[c] = [swap(x, "col", n_col, 1) for x in owns[c]]
            last = (owns[c][0],)
        elif step == "before":
            befores[c] = call(product_body, (*owns[c], held_own), [((width, d), F32)], after=last, weight=WP)[0]
            last = (befores[c],)
        elif step == "send":
            outs = [((width // 2, d), F32)] * 2
            total = pltpu.VMEM((width, d), F32)
            args = (*others[c], held_other, befores[c])
            send, keep = call(product_send_body, args, outs, after=last, scratch=[total], weight=WQ)
            pending[c] = keep, swap(send, "row", n_row, bits[0])
            last = (keep,)
        elif step == "add" and direct[c]:
            outs = [((pieces[c], d), F32)] * (n_row // 2)
            own, *sends = call(functools.partial(add_spread_body, n_row // 2), pending[c], outs, after=last, weight=WE)
            flips = [2 * owner_at(flip, n_row // 2) for flip in range(1, n_row // 2)]
            pending[c] = own, *[swap(x, "row", n_row, flip) for x, flip in zip(sends, flips)]
            last = (own,)
        elif step == "add":
            outs = [((width >> (s + 1), d), F32)] * 2
            send, keep = call(functools.partial(add_send_body, bits[s]), pending[c], outs, after=last, weight=WE)
            pending[c] = keep, swap(send, "row", n_row, bits[s])
            last = (keep,)
        else:
            parts = [[x for group in groups.values() for x in group] for groups in (owns, others)]
            sketch, done = finish_sketch(n_row, k, pieces, *parts, last)
            last = (done,)
    flat = [x for c in range(n) for x in pending[c]]
    if per_owner % 8 == 0:
        body = functools.partial(final_corange_body, [len(pending[c]) for c in range(n)])
        corange = call(body, flat, [((per_owner, d), F32)], results=1)[0]
    else:
        corange = jnp.concatenate([functools.reduce(jnp.add, pending[c]) for c in range(n)], axis=0)
    return sketch, corange.T


def finish_sketch(n_row, k, pieces, owns, others, after):
    half = owns[0].shape[1]
    if k // n_row % 8 == 0:
        body = functools.partial(final_sketch_body, n_row, pieces)
        return call(body, (*owns, *others), [((2 * half, k), F32), ((8, 128), F32)], after=after, results=1)
    places = jnp.array([owner_at(r, n_row) for r in range(n_row)])

    def columns(parts):
        parts = [jnp.concatenate(parts[c : c + SPLIT], axis=0) for c in range(0, len(parts), SPLIT)]
        found = [part.reshape(n_row, piece, half)[places] for part, piece in zip(parts, pieces)]
        return jnp.concatenate(found, axis=1).reshape(k, half).T

    own, other = columns(owns), columns(others)
    first = lax.rem(lax.axis_index("col"), 2) == 0
    return jnp.where(first, jnp.concatenate([own, other]), jnp.concatenate([other, own])), after[0]


def solution(mesh):
    body = functools.partial(shards, mesh.shape["row"], mesh.shape["col"])
    in_specs = (P("row", "col"), P("col", None))
    out_specs = (P("row", None), P("col", "row"))
    return jax.shard_map(body, mesh=mesh, in_specs=in_specs, out_specs=out_specs, check_vma=False)
```

```python
import functools

import jax
import jax.numpy as jnp
from jax import lax
from jax.experimental import pallas as pl
from jax.experimental.pallas import tpu as pltpu
from jax.sharding import PartitionSpec as P

EIGHTHS = (2, 2, 2, 2)
BLOCK = 512
F32 = jnp.float32
BF16 = jnp.bfloat16
NT = (((1,), (1,)), ((), ()))
SPECS = {"v": pl.BlockSpec(memory_space=pltpu.VMEM), "a": pl.BlockSpec(memory_space=pl.ANY)}
ORDER = "own0 before0 send0 own1 before1 send1 add0.1 own2 before2 send2 add0.2 add1.1 own3 before3 send3 add2.1 add1.2 add2.2 add3.1 sketch"
WEIGHTS = {'add2.2': 1000000000, 'send1': 200000000, 'own1': 1000000000, 'own2': 0, 'before2': 2000000000, 'before1': 500000000, 'add0.2': 0, 'sketch': 500000000, 'add3.1': 200000000}
SPLIT = 2
DIRECT = 1
GROUPS = ((0,), (1,), (2,), (3,))


def call(body, args, outs, kinds=None, after=(), scratch=(), results=0, weight=0):
    n = len(args)
    kinds = (kinds or "v" * n) + "a" * len(after)

    def run(*refs):
        body(*refs[:n], *refs[len(kinds) :])

    return pl.pallas_call(
        run,
        out_shape=[pltpu.VMEM(*o) if i >= results else jax.ShapeDtypeStruct(*o) for i, o in enumerate(outs)],
        in_specs=[SPECS[kind] for kind in kinds],
        out_specs=[SPECS["v"]] * len(outs),
        scratch_shapes=list(scratch),
        cost_estimate=pl.CostEstimate(flops=weight, bytes_accessed=0, transcendentals=0),
        compiler_params=pltpu.CompilerParams(vmem_limit_bytes=16 << 20),
    )(*args, *after)


def owner_at(index, n_row):
    owner, bit = index * 0, 1
    while bit < n_row:
        owner = 2 * owner + index % 2
        index = index // 2
        bit *= 2
    return owner


def column_of(position, k, n_row, pieces):
    column, first, done = position * 0, 0, 0
    for piece in pieces:
        rest = position - first
        found = owner_at(rest // piece, n_row) * (k // n_row) + done + rest % piece
        column = jnp.where((rest >= 0) & (rest < piece * n_row), found, column)
        first += piece * n_row
        done += piece
    return column


def stream_half(delta, held, sem, mine):
    rows = held.shape[0]
    parity = lax.rem(lax.axis_index("col"), 2)
    first = (parity if mine else 1 - parity) * rows
    copies = []
    for b in range(rows // BLOCK):
        source = delta.at[pl.ds(pl.multiple_of(first + b * BLOCK, BLOCK), BLOCK), :]
        copies.append(pltpu.make_async_copy(source, held.at[pl.ds(b * BLOCK, BLOCK), :], sem.at[b]))
        copies[-1].start()
    return copies


def sketch_half(omega_t, held, copies, out):
    for b, copy in enumerate(copies):
        copy.wait()
        block = pl.ds(b * BLOCK, BLOCK)
        out[:, block] = lax.dot_general(omega_t[...], held[block, :], NT, preferred_element_type=F32)


def first_half_body(n_row, pieces, delta, omega, held, omega_t, out, omega_v, sem, omega_sem):
    k = out.shape[0]
    fetch = pltpu.make_async_copy(omega, omega_v, omega_sem)
    fetch.start()
    copies = stream_half(delta, held, sem, False)
    position = lax.broadcasted_iota(jnp.int32, (k, k), 0)
    column = lax.broadcasted_iota(jnp.int32, (k, k), 1)
    pick = jnp.where(column_of(position, k, n_row, pieces) == column, 1.0, 0.0).astype(BF16)
    fetch.wait()
    omega_t[...] = lax.dot_general(pick, omega_v[...], NT, preferred_element_type=F32).astype(BF16)
    sketch_half(omega_t, held, copies, out)


def second_half_body(delta, omega_t, held, out, sem):
    sketch_half(omega_t, held, stream_half(delta, held, sem, True), out)


def add_chunks_body(kept, received, *outs):
    first = 0
    for out in outs:
        part = pl.ds(first, out.shape[0])
        out[...] = kept[part, :] + received[part, :]
        first += out.shape[0]


def add_body(a, b, *outs):
    first = 0
    for out in outs:
        part = pl.ds(first, out.shape[0])
        out[...] = a[part, :] + b[part, :]
        first += out.shape[0]


def joined(refs):
    return jnp.concatenate([ref[...] for ref in refs], axis=0)


def product_body(*refs):
    *sketch, held, out = refs
    out[...] = jnp.dot(joined(sketch).astype(BF16), held[...], preferred_element_type=F32)


def split(bit, segments, refs, send, keep):
    own = lax.rem(lax.axis_index("row") // bit, 2)
    start, first = 0, 0
    for rows in segments:
        half = rows // 2
        for out, which in ((send, 1 - own), (keep, own)):
            if half % 8:
                low, high = (
                    functools.reduce(jnp.add, [ref[pl.ds(start + i * half, half), :] for ref in refs]) for i in range(2)
                )
                value = jnp.where(which == 0, low, high)
            else:
                part = pl.ds(pl.multiple_of(start + which * half, 8), half)
                value = functools.reduce(jnp.add, [ref[part, :] for ref in refs])
            out[pl.ds(first, half), :] = value
        start += rows
        first += half


def product_send_body(*refs):
    *sketch, held, before, send, keep, total = refs
    total[...] = before[...] + jnp.dot(joined(sketch).astype(BF16), held[...], preferred_element_type=F32)
    split(1, [total.shape[0]], [total], send, keep)


def add_send_body(bit, segments, *refs):
    *pairs, send, keep = refs
    first = 0
    for kept, got in zip(pairs[::2], pairs[1::2]):
        mine = segments if len(pairs) == 2 else [kept.shape[0]]
        half = kept.shape[0] // 2
        part = pl.ds(first, half)
        split(bit, mine, [kept, got], send.at[part, :], keep.at[part, :])
        first += half


def add_spread_body(n_high, kept, received, *outs):
    piece = outs[0].shape[0]
    place = owner_at(lax.axis_index("row") // 2, n_high)
    for flip, out in enumerate(outs):
        part = pl.ds(pl.multiple_of(lax.bitwise_xor(place, flip) * piece, piece), piece)
        out[...] = kept[part, :] + received[part, :]


def final_corange_body(counts, *refs):
    out = refs[-1]
    first, used = 0, 0
    for count in counts:
        terms = refs[used : used + count]
        piece = terms[0].shape[0]
        out[pl.ds(first, piece), :] = functools.reduce(jnp.add, [term[...] for term in terms])
        first += piece
        used += count


def final_sketch_body(n_row, pieces, *refs):
    out, done = refs[-2:]
    n, rows = len(refs) // 2 - 1, refs[0].shape[1]
    parity = lax.rem(lax.axis_index("col"), 2)
    per_part = n_row // SPLIT
    for side in range(2):
        parts = refs[side * n : (side + 1) * n]
        first = (parity if side == 0 else 1 - parity) * rows
        for b in range(rows // 128):
            lanes = pl.ds(b * 128, 128)
            found = []
            for r in range(n_row):
                place = owner_at(r, n_row)
                for c, piece in enumerate(pieces):
                    part = parts[c * SPLIT + place // per_part]
                    found.append(part[pl.ds(place % per_part * piece, piece), lanes])
            block = jnp.concatenate(found, axis=0)
            out[pl.ds(pl.multiple_of(first + b * 128, 128), 128), :] = block.T
    done[...] = jnp.zeros_like(done)


def swap(x, axis, size, bit):
    return lax.ppermute(x, axis, [(i, i ^ bit) for i in range(size)])


def shards(n_row, n_col, delta, omega):
    rows, d = delta.shape
    k = omega.shape[1]
    half = rows // 2
    per_owner = k // n_row
    pieces = [per_owner * part // sum(EIGHTHS) for part in EIGHTHS] if per_owner % 8 == 0 else [1] * per_owner
    widths = [piece * n_row for piece in pieces]
    n = len(pieces)
    bits = [1 << i for i in range(n_row.bit_length() - 1)]

    in_hbm = pltpu.with_memory_space_constraint(delta, pltpu.HBM)
    sems = pltpu.SemaphoreType.DMA((half // BLOCK,))
    held_other, omega_t, to_send = call(
        functools.partial(first_half_body, n_row, pieces),
        (in_hbm, pltpu.with_memory_space_constraint(omega, pltpu.HBM)),
        [((half, d), BF16), ((k, d), BF16), ((k, half), F32)],
        "aa",
        scratch=[pltpu.VMEM((d, k), BF16), sems, pltpu.SemaphoreType.DMA],
    )
    received = swap(to_send, "col", n_col, 1)
    held_own, kept = call(second_half_body, (in_hbm, omega_t), [((half, d), BF16), ((k, half), F32)], "av", scratch=[sems])
    partial = call(add_chunks_body, (kept, received), [((width, half), F32) for width in widths])
    bit = 2
    while bit < n_col // 2:
        moved = [swap(x, "col", n_col, bit) for x in partial]
        partial = [call(add_body, pair, [(pair[0].shape, F32)])[0] for pair in zip(partial, moved)]
        bit *= 2
    moved = [swap(x, "col", n_col, bit) for x in partial]

    owns, others, befores, pending = {}, {}, {}, {}
    sketch = None
    last = ()
    groups = GROUPS if n == 4 else tuple((c,) for c in range(n))
    direct = [len(bits) == 3 and len(group) == 1 and pieces[group[0]] % 8 == 0 and g >= len(groups) - DIRECT for g, group in enumerate(groups)]
    steps = ORDER.split() if len(bits) == 3 and n == 4 else []
    if not steps:
        found = []
        for c in range(n):
            found += [(10 * c, f"own{c}"), (10 * c + 1, f"before{c}"), (10 * c + 2, f"send{c}")]
        for g, group in enumerate(groups):
            found += [(10 * group[-1] + 9.5 + 10 * s, f"add{g}.{s}") for s in range(1, 2 if direct[g] else len(bits))]
        steps = [step for _, step in sorted(found)] + ["sketch"]

    for step in steps:
        weight = WEIGHTS.get(step, 0)
        if step.startswith("own"):
            c = int(step[3:])
            outs = [((widths[c] // SPLIT, half), F32)] * SPLIT
            owns[c] = call(add_body, (partial[c], moved[c]), outs, after=last, weight=weight)
            others[c] = [swap(x, "col", n_col, 1) for x in owns[c]]
            last = (owns[c][0],)
        elif step.startswith("before"):
            c = int(step[6:])
            befores[c] = call(product_body, (*owns[c], held_own), [((widths[c], d), F32)], after=last, weight=weight)[0]
            last = (befores[c],)
        elif step.startswith("send"):
            c = int(step[4:])
            outs = [((widths[c] // 2, d), F32)] * 2
            total = pltpu.VMEM((widths[c], d), F32)
            args = (*others[c], held_other, befores[c])
            send, keep = call(product_send_body, args, outs, after=last, scratch=[total], weight=weight)
            pending[(c,)] = keep, swap(send, "row", n_row, bits[0])
            last = (keep,)
        elif step.startswith("add"):
            g, s = (int(x) for x in step[3:].split("."))
            group = groups[g]
            if direct[g]:
                outs = [((pieces[group[0]], d), F32)] * (n_row // 2)
                body = functools.partial(add_spread_body, n_row // 2)
                own, *sends = call(body, pending[group], outs, after=last, weight=weight)
                flips = [2 * owner_at(flip, n_row // 2) for flip in range(1, n_row // 2)]
                pending[group] = own, *[swap(x, "row", n_row, flip) for x, flip in zip(sends, flips)]
                last = (own,)
                continue
            if s == 1:
                pending[group] = [x for c in group for x in pending[(c,)]]
            segments = [widths[c] >> s for c in group]
            body = functools.partial(add_send_body, bits[s], segments)
            outs = [((sum(segments) // 2, d), F32)] * 2
            send, keep = call(body, pending[group], outs, after=last, weight=weight)
            pending[group] = keep, swap(send, "row", n_row, bits[s])
            last = (keep,)
        else:
            parts = [[x for found in halves.values() for x in found] for halves in (owns, others)]
            sketch, done = finish_sketch(n_row, k, pieces, *parts, last)
            last = (done,)
    flat = [x for group in groups for x in pending[group]]
    if per_owner % 8 == 0:
        body = functools.partial(final_corange_body, [len(pending[group]) for group in groups])
        corange = call(body, flat, [((per_owner, d), F32)], after=last, results=1, weight=WEIGHTS.get("F", 0))[0]
    else:
        corange = jnp.concatenate([functools.reduce(jnp.add, pending[group]) for group in groups], axis=0)
    return sketch, corange.T


def finish_sketch(n_row, k, pieces, owns, others, after):
    half = owns[0].shape[1]
    if k // n_row % 8 == 0:
        body = functools.partial(final_sketch_body, n_row, pieces)
        return call(body, (*owns, *others), [((2 * half, k), F32), ((8, 128), F32)], after=after, results=1)
    places = jnp.array([owner_at(r, n_row) for r in range(n_row)])

    def columns(parts):
        parts = [jnp.concatenate(parts[c : c + SPLIT], axis=0) for c in range(0, len(parts), SPLIT)]
        found = [part.reshape(n_row, piece, half)[places] for part, piece in zip(parts, pieces)]
        return jnp.concatenate(found, axis=1).reshape(k, half).T

    own, other = columns(owns), columns(others)
    first = lax.rem(lax.axis_index("col"), 2) == 0
    return jnp.where(first, jnp.concatenate([own, other]), jnp.concatenate([other, own])), after[0]


def solution(mesh):
    body = functools.partial(shards, mesh.shape["row"], mesh.shape["col"])
    in_specs = (P("row", "col"), P("col", None))
    out_specs = (P("row", None), P("col", "row"))
    return jax.shard_map(body, mesh=mesh, in_specs=in_specs, out_specs=out_specs, check_vma=False)
```

```python
import functools

import jax
import jax.numpy as jnp
from jax import lax
from jax.experimental import pallas as pl
from jax.experimental.pallas import tpu as pltpu
from jax.sharding import PartitionSpec as P

EIGHTHS = (2, 2, 2, 2)
BLOCK = 512
F32 = jnp.float32
BF16 = jnp.bfloat16
NT = (((1,), (1,)), ((), ()))
SPECS = {"v": pl.BlockSpec(memory_space=pltpu.VMEM), "a": pl.BlockSpec(memory_space=pl.ANY)}
ORDER = ()
WEIGHTS = {}
SPLIT = 2
GROUPS = ((0,), (1,), (2,), (3,))
MODES = ("all", "all", "all", "all")


def call(body, args, outs, kinds=None, after=(), scratch=(), results=0, weight=0):
    n = len(args)
    kinds = (kinds or "v" * n) + "a" * len(after)

    def run(*refs):
        body(*refs[:n], *refs[len(kinds) :])

    return pl.pallas_call(
        run,
        out_shape=[pltpu.VMEM(*o) if i >= results else jax.ShapeDtypeStruct(*o) for i, o in enumerate(outs)],
        in_specs=[SPECS[kind] for kind in kinds],
        out_specs=[SPECS["v"]] * len(outs),
        scratch_shapes=list(scratch),
        cost_estimate=pl.CostEstimate(flops=weight, bytes_accessed=0, transcendentals=0),
        compiler_params=pltpu.CompilerParams(vmem_limit_bytes=16 << 20),
    )(*args, *after)


def owner_at(index, n_row):
    owner, bit = index * 0, 1
    while bit < n_row:
        owner = 2 * owner + index % 2
        index = index // 2
        bit *= 2
    return owner


def column_of(position, k, n_row, pieces):
    column, first, done = position * 0, 0, 0
    for piece in pieces:
        rest = position - first
        found = owner_at(rest // piece, n_row) * (k // n_row) + done + rest % piece
        column = jnp.where((rest >= 0) & (rest < piece * n_row), found, column)
        first += piece * n_row
        done += piece
    return column


def stream_half(delta, held, sem, mine):
    rows = held.shape[0]
    parity = lax.rem(lax.axis_index("col"), 2)
    first = (parity if mine else 1 - parity) * rows
    copies = []
    for b in range(rows // BLOCK):
        source = delta.at[pl.ds(pl.multiple_of(first + b * BLOCK, BLOCK), BLOCK), :]
        copies.append(pltpu.make_async_copy(source, held.at[pl.ds(b * BLOCK, BLOCK), :], sem.at[b]))
        copies[-1].start()
    return copies


def sketch_half(omega_t, held, copies, out):
    for b, copy in enumerate(copies):
        copy.wait()
        block = pl.ds(b * BLOCK, BLOCK)
        out[:, block] = lax.dot_general(omega_t[...], held[block, :], NT, preferred_element_type=F32)


def first_half_body(n_row, pieces, delta, omega, held, omega_t, out, omega_v, sem, omega_sem):
    k = out.shape[0]
    fetch = pltpu.make_async_copy(omega, omega_v, omega_sem)
    fetch.start()
    copies = stream_half(delta, held, sem, False)
    position = lax.broadcasted_iota(jnp.int32, (k, k), 0)
    column = lax.broadcasted_iota(jnp.int32, (k, k), 1)
    pick = jnp.where(column_of(position, k, n_row, pieces) == column, 1.0, 0.0).astype(BF16)
    fetch.wait()
    omega_t[...] = lax.dot_general(pick, omega_v[...], NT, preferred_element_type=F32).astype(BF16)
    sketch_half(omega_t, held, copies, out)


def second_half_body(delta, omega_t, held, out, sem):
    sketch_half(omega_t, held, stream_half(delta, held, sem, True), out)


def add_chunks_body(kept, received, *outs):
    first = 0
    for out in outs:
        part = pl.ds(first, out.shape[0])
        out[...] = kept[part, :] + received[part, :]
        first += out.shape[0]


def add_body(a, b, *outs):
    first = 0
    for out in outs:
        part = pl.ds(first, out.shape[0])
        out[...] = a[part, :] + b[part, :]
        first += out.shape[0]


def joined(refs):
    return jnp.concatenate([ref[...] for ref in refs], axis=0)


def product_body(*refs):
    *sketch, held, out = refs
    out[...] = jnp.dot(joined(sketch).astype(BF16), held[...], preferred_element_type=F32)


def split(bit, segments, refs, send, keep):
    own = lax.rem(lax.axis_index("row") // bit, 2)
    start, first = 0, 0
    for rows in segments:
        half = rows // 2
        for out, which in ((send, 1 - own), (keep, own)):
            if half % 8:
                low, high = (
                    functools.reduce(jnp.add, [ref[pl.ds(start + i * half, half), :] for ref in refs]) for i in range(2)
                )
                value = jnp.where(which == 0, low, high)
            else:
                part = pl.ds(pl.multiple_of(start + which * half, 8), half)
                value = functools.reduce(jnp.add, [ref[part, :] for ref in refs])
            out[pl.ds(first, half), :] = value
        start += rows
        first += half


def product_send_body(*refs):
    *sketch, held, before, send, keep, total = refs
    total[...] = before[...] + jnp.dot(joined(sketch).astype(BF16), held[...], preferred_element_type=F32)
    split(1, [total.shape[0]], [total], send, keep)


def product_spread_body(n_row, *refs):
    outs, total = refs[-1 - n_row : -1], refs[-1]
    *sketch, held, before = refs[: -1 - n_row]
    total[...] = before[...] + jnp.dot(joined(sketch).astype(BF16), held[...], preferred_element_type=F32)
    piece = outs[0].shape[0]
    place = owner_at(lax.axis_index("row"), n_row)
    for flip, out in enumerate(outs):
        out[...] = total[pl.ds(pl.multiple_of(lax.bitwise_xor(place, flip) * piece, piece), piece), :]


def add_send_body(bit, segments, *refs):
    *pairs, send, keep = refs
    first = 0
    for kept, got in zip(pairs[::2], pairs[1::2]):
        mine = segments if len(pairs) == 2 else [kept.shape[0]]
        half = kept.shape[0] // 2
        part = pl.ds(first, half)
        split(bit, mine, [kept, got], send.at[part, :], keep.at[part, :])
        first += half


def add_spread_body(n_high, kept, received, *outs):
    piece = outs[0].shape[0]
    place = owner_at(lax.axis_index("row") // 2, n_high)
    for flip, out in enumerate(outs):
        part = pl.ds(pl.multiple_of(lax.bitwise_xor(place, flip) * piece, piece), piece)
        out[...] = kept[part, :] + received[part, :]


def add_all_body(n_high, kept, received, out):
    piece = out.shape[0] // n_high
    for high in range(n_high):
        part = pl.ds(owner_at(high, n_high) * piece, piece)
        out[pl.ds(high * piece, piece), :] = kept[part, :] + received[part, :]


def final_corange_body(counts, rows, *refs):
    out = refs[-1]
    first, used = 0, 0
    for count, piece in zip(counts, rows):
        terms = refs[used : used + count]
        parts = [term[pl.ds(i, piece), :] for term in terms for i in range(0, term.shape[0], piece)]
        out[pl.ds(first, piece), :] = functools.reduce(jnp.add, parts)
        first += piece
        used += count


def final_sketch_body(n_row, pieces, *refs):
    out, done = refs[-2:]
    n, rows = len(refs) // 2 - 1, refs[0].shape[1]
    parity = lax.rem(lax.axis_index("col"), 2)
    per_part = n_row // SPLIT
    for side in range(2):
        parts = refs[side * n : (side + 1) * n]
        first = (parity if side == 0 else 1 - parity) * rows
        for b in range(rows // 128):
            lanes = pl.ds(b * 128, 128)
            found = []
            for r in range(n_row):
                place = owner_at(r, n_row)
                for c, piece in enumerate(pieces):
                    part = parts[c * SPLIT + place // per_part]
                    found.append(part[pl.ds(place % per_part * piece, piece), lanes])
            block = jnp.concatenate(found, axis=0)
            out[pl.ds(pl.multiple_of(first + b * 128, 128), 128), :] = block.T
    done[...] = jnp.zeros_like(done)


def swap(x, axis, size, bit):
    return lax.ppermute(x, axis, [(i, i ^ bit) for i in range(size)])


def shards(n_row, n_col, delta, omega):
    rows, d = delta.shape
    k = omega.shape[1]
    half = rows // 2
    per_owner = k // n_row
    pieces = [per_owner * part // sum(EIGHTHS) for part in EIGHTHS] if per_owner % 8 == 0 else [1] * per_owner
    widths = [piece * n_row for piece in pieces]
    n = len(pieces)
    bits = [1 << i for i in range(n_row.bit_length() - 1)]

    in_hbm = pltpu.with_memory_space_constraint(delta, pltpu.HBM)
    sems = pltpu.SemaphoreType.DMA((half // BLOCK,))
    held_other, omega_t, to_send = call(
        functools.partial(first_half_body, n_row, pieces),
        (in_hbm, pltpu.with_memory_space_constraint(omega, pltpu.HBM)),
        [((half, d), BF16), ((k, d), BF16), ((k, half), F32)],
        "aa",
        scratch=[pltpu.VMEM((d, k), BF16), sems, pltpu.SemaphoreType.DMA],
    )
    received = swap(to_send, "col", n_col, 1)
    held_own, kept = call(second_half_body, (in_hbm, omega_t), [((half, d), BF16), ((k, half), F32)], "av", scratch=[sems])
    partial = call(add_chunks_body, (kept, received), [((width, half), F32) for width in widths])
    bit = 2
    while bit < n_col // 2:
        moved = [swap(x, "col", n_col, bit) for x in partial]
        partial = [call(add_body, pair, [(pair[0].shape, F32)])[0] for pair in zip(partial, moved)]
        bit *= 2
    moved = [swap(x, "col", n_col, bit) for x in partial]

    owns, others, befores, pending = {}, {}, {}, {}
    sketch = None
    last = ()
    groups = GROUPS if n == sum(len(group) for group in GROUPS) else tuple((c,) for c in range(n))
    modes = MODES if len(groups) == len(MODES) else ("all",) * len(groups)
    whole = [any(mode == "spread" and c in group for mode, group in zip(modes, groups)) for c in range(n)]
    steps = ORDER
    if not steps:
        found = []
        for c in range(n):
            found += [(10 * c, f"own{c}"), (10 * c + 1, f"before{c}"), (10 * c + 2, f"send{c}")]
        for g, group in enumerate(groups):
            last_step = {"all": 2, "direct": 2, "spread": 1, "pairs": len(bits)}[modes[g]]
            found += [(10 * group[-1] + 9.5 + 10 * s, f"add{g}.{s}") for s in range(1, last_step)]
        steps = [step for _, step in sorted(found)] + ["sketch"]
    for step in steps:
        weight = WEIGHTS.get(step, 0)
        if step.startswith("own"):
            c = int(step[3:])
            outs = [((widths[c] // SPLIT, half), F32)] * SPLIT
            owns[c] = call(add_body, (partial[c], moved[c]), outs, after=last, weight=weight)
            others[c] = [swap(x, "col", n_col, 1) for x in owns[c]]
            last = (owns[c][0],)
        elif step.startswith("before"):
            c = int(step[6:])
            befores[c] = call(product_body, (*owns[c], held_own), [((widths[c], d), F32)], after=last, weight=weight)[0]
            last = (befores[c],)
        elif step.startswith("send"):
            c = int(step[4:])
            if whole[c]:
                args = (*others[c], held_other, befores[c])
                body = functools.partial(product_spread_body, n_row)
                outs = [((pieces[c], d), F32)] * n_row
                own, *sends = call(body, args, outs, after=last, scratch=[pltpu.VMEM((widths[c], d), F32)], weight=weight)
                flips = [owner_at(flip, n_row) for flip in range(1, n_row)]
                pending[(c,)] = own, *[swap(x, "row", n_row, flip) for x, flip in zip(sends, flips)]
                last = (own,)
                continue
            outs = [((widths[c] // 2, d), F32)] * 2
            total = pltpu.VMEM((widths[c], d), F32)
            args = (*others[c], held_other, befores[c])
            send, keep = call(product_send_body, args, outs, after=last, scratch=[total], weight=weight)
            pending[(c,)] = keep, swap(send, "row", n_row, bits[0])
            last = (keep,)
        elif step.startswith("add"):
            g, s = (int(x) for x in step[3:].split("."))
            group = groups[g]
            if modes[g] == "all":
                outs = [((n_row // 2 * pieces[group[0]], d), F32)]
                total = call(functools.partial(add_all_body, n_row // 2), pending[group], outs, after=last, weight=weight)[0]
                across = [[2 * high + low for high in range(n_row // 2)] for low in range(2)]
                pending[group] = (lax.all_to_all(total, "row", 0, 0, axis_index_groups=across, tiled=True),)
                last = (total,)
                continue
            if modes[g] == "direct":
                outs = [((pieces[group[0]], d), F32)] * (n_row // 2)
                body = functools.partial(add_spread_body, n_row // 2)
                own, *sends = call(body, pending[group], outs, after=last, weight=weight)
                flips = [2 * owner_at(flip, n_row // 2) for flip in range(1, n_row // 2)]
                pending[group] = own, *[swap(x, "row", n_row, flip) for x, flip in zip(sends, flips)]
                last = (own,)
                continue
            if s == 1:
                pending[group] = [x for c in group for x in pending[(c,)]]
            segments = [widths[c] >> s for c in group]
            body = functools.partial(add_send_body, bits[s], segments)
            outs = [((sum(segments) // 2, d), F32)] * 2
            send, keep = call(body, pending[group], outs, after=last, weight=weight)
            pending[group] = keep, swap(send, "row", n_row, bits[s])
            last = (keep,)
        else:
            parts = [[x for found in halves.values() for x in found] for halves in (owns, others)]
            sketch, done = finish_sketch(n_row, k, pieces, *parts, last)
            last = (done,)
    flat = [x for group in groups for x in pending[group]]
    if per_owner % 8 == 0:
        body = functools.partial(final_corange_body, [len(pending[group]) for group in groups], [sum(pieces[c] for c in group) for group in groups])
        corange = call(body, flat, [((per_owner, d), F32)], after=last, results=1, weight=WEIGHTS.get("F", 0))[0]
    else:
        parts = [x for group in groups for x in pending[group]]
        corange = jnp.concatenate([part.reshape(n_row // 2, -1, d).sum(0) for part in parts], axis=0)
    return sketch, corange.T


def finish_sketch(n_row, k, pieces, owns, others, after):
    half = owns[0].shape[1]
    if k // n_row % 8 == 0:
        body = functools.partial(final_sketch_body, n_row, pieces)
        return call(body, (*owns, *others), [((2 * half, k), F32), ((8, 128), F32)], after=after, results=1)
    places = jnp.array([owner_at(r, n_row) for r in range(n_row)])

    def columns(parts):
        parts = [jnp.concatenate(parts[c : c + SPLIT], axis=0) for c in range(0, len(parts), SPLIT)]
        found = [part.reshape(n_row, piece, half)[places] for part, piece in zip(parts, pieces)]
        return jnp.concatenate(found, axis=1).reshape(k, half).T

    own, other = columns(owns), columns(others)
    first = lax.rem(lax.axis_index("col"), 2) == 0
    return jnp.where(first, jnp.concatenate([own, other]), jnp.concatenate([other, own])), after[0]


def solution(mesh):
    body = functools.partial(shards, mesh.shape["row"], mesh.shape["col"])
    in_specs = (P("row", "col"), P("col", None))
    out_specs = (P("row", None), P("col", "row"))
    return jax.shard_map(body, mesh=mesh, in_specs=in_specs, out_specs=out_specs, check_vma=False)
```

```python
import functools

import jax
import jax.numpy as jnp
from jax import lax
from jax.experimental import pallas as pl
from jax.experimental.pallas import tpu as pltpu
from jax.sharding import PartitionSpec as P

EIGHTHS = (2, 2, 2, 2)
BLOCK = 512
F32 = jnp.float32
BF16 = jnp.bfloat16
NT = (((1,), (1,)), ((), ()))
SPECS = {"v": pl.BlockSpec(memory_space=pltpu.VMEM), "a": pl.BlockSpec(memory_space=pl.ANY)}
ORDER = ('own0', 'before0', 'send0', 'own1', 'before1', 'send1', 'add0.1', 'own2', 'before2', 'send2', 'add1.1', 'own3', 'before3', 'send3', 'add2.1', 'add1.2', 'add0.2', 'add2.2', 'sketch', 'add3.1')
REST_PARTS = 4
WEIGHTS = {'add2.1': 500000000, 'F': 500000000, 'send1': 0, 'send0': 0, 'send3': 0, 'add2.2': 200000000, 'add0.2': 1000000000, 'own2': 500000000, 'before1': 500000000, 'add0.1': 500000000, 'before3': 2000000000, 'sketch': 500000000, 'send2': 0, 'add1.2': 200000000}
SPLITS = (2, 2, 2, 2)
GROUPS = ((0,), (1,), (2,), (3,))
MODES = ('pairs', 'pairs', 'pairs', 'direct')


def call(body, args, outs, kinds=None, after=(), scratch=(), results=0, weight=0):
    n = len(args)
    kinds = (kinds or "v" * n) + "a" * len(after)

    def run(*refs):
        body(*refs[:n], *refs[len(kinds) :])

    return pl.pallas_call(
        run,
        out_shape=[pltpu.VMEM(*o) if i >= results else jax.ShapeDtypeStruct(*o) for i, o in enumerate(outs)],
        in_specs=[SPECS[kind] for kind in kinds],
        out_specs=[SPECS["v"]] * len(outs),
        scratch_shapes=list(scratch),
        cost_estimate=pl.CostEstimate(flops=weight, bytes_accessed=0, transcendentals=0),
        compiler_params=pltpu.CompilerParams(vmem_limit_bytes=16 << 20),
    )(*args, *after)


def owner_at(index, n_row):
    owner, bit = index * 0, 1
    while bit < n_row:
        owner = 2 * owner + index % 2
        index = index // 2
        bit *= 2
    return owner


def column_of(position, k, n_row, pieces):
    column, first, done = position * 0, 0, 0
    for piece in pieces:
        rest = position - first
        found = owner_at(rest // piece, n_row) * (k // n_row) + done + rest % piece
        column = jnp.where((rest >= 0) & (rest < piece * n_row), found, column)
        first += piece * n_row
        done += piece
    return column


def stream_half(delta, held, sem, mine):
    rows = held.shape[0]
    parity = lax.rem(lax.axis_index("col"), 2)
    first = (parity if mine else 1 - parity) * rows
    copies = []
    for b in range(rows // BLOCK):
        source = delta.at[pl.ds(pl.multiple_of(first + b * BLOCK, BLOCK), BLOCK), :]
        copies.append(pltpu.make_async_copy(source, held.at[pl.ds(b * BLOCK, BLOCK), :], sem.at[b]))
        copies[-1].start()
    return copies


def sketch_half(omega_t, held, copies, out):
    for b, copy in enumerate(copies):
        copy.wait()
        block = pl.ds(b * BLOCK, BLOCK)
        out[:, block] = lax.dot_general(omega_t[: out.shape[0], :], held[block, :], NT, preferred_element_type=F32)


def first_half_body(n_row, pieces, delta, omega, held, omega_t, out, omega_v, sem, omega_sem):
    k = omega_t.shape[0]
    fetch = pltpu.make_async_copy(omega, omega_v, omega_sem)
    fetch.start()
    copies = stream_half(delta, held, sem, False)
    position = lax.broadcasted_iota(jnp.int32, (k, k), 0)
    column = lax.broadcasted_iota(jnp.int32, (k, k), 1)
    pick = jnp.where(column_of(position, k, n_row, pieces) == column, 1.0, 0.0).astype(BF16)
    fetch.wait()
    omega_t[...] = lax.dot_general(pick, omega_v[...], NT, preferred_element_type=F32).astype(BF16)
    sketch_half(omega_t, held, copies, out)


def second_half_body(delta, omega_t, held, out, sem):
    sketch_half(omega_t, held, stream_half(delta, held, sem, True), out)


def rest_half_body(omega_t, held, *outs):
    rows = sum(out.shape[0] for out in outs)
    later = omega_t[omega_t.shape[0] - rows :, :]
    for b in range(held.shape[0] // BLOCK):
        block = pl.ds(b * BLOCK, BLOCK)
        found = lax.dot_general(later, held[block, :], NT, preferred_element_type=F32)
        first = 0
        for out in outs:
            out[:, block] = found[first : first + out.shape[0]]
            first += out.shape[0]


def add_chunks_body(parts, kept, *refs):
    received, first = joined(refs[:parts]), 0
    for out in refs[parts:]:
        part = pl.ds(first, out.shape[0])
        out[...] = kept[part, :] + received[first : first + out.shape[0]]
        first += out.shape[0]


def add_body(a, b, *outs):
    first = 0
    for out in outs:
        part = pl.ds(first, out.shape[0])
        out[...] = a[part, :] + b[part, :]
        first += out.shape[0]


def joined(refs):
    return jnp.concatenate([ref[...] for ref in refs], axis=0)


def product_body(*refs):
    *sketch, held, out = refs
    out[...] = jnp.dot(joined(sketch).astype(BF16), held[...], preferred_element_type=F32)


def split(bit, segments, refs, send, keep):
    own = lax.rem(lax.axis_index("row") // bit, 2)
    start, first = 0, 0
    for rows in segments:
        half = rows // 2
        for out, which in ((send, 1 - own), (keep, own)):
            if half % 8:
                low, high = (
                    functools.reduce(jnp.add, [ref[pl.ds(start + i * half, half), :] for ref in refs]) for i in range(2)
                )
                value = jnp.where(which == 0, low, high)
            else:
                part = pl.ds(pl.multiple_of(start + which * half, 8), half)
                value = functools.reduce(jnp.add, [ref[part, :] for ref in refs])
            out[pl.ds(first, half), :] = value
        start += rows
        first += half


def product_send_body(*refs):
    *sketch, held, before, send, keep, total = refs
    total[...] = before[...] + jnp.dot(joined(sketch).astype(BF16), held[...], preferred_element_type=F32)
    split(1, [total.shape[0]], [total], send, keep)


def add_send_body(bit, segments, *refs):
    *pairs, send, keep = refs
    first = 0
    for kept, got in zip(pairs[::2], pairs[1::2]):
        mine = segments if len(pairs) == 2 else [kept.shape[0]]
        half = kept.shape[0] // 2
        part = pl.ds(first, half)
        split(bit, mine, [kept, got], send.at[part, :], keep.at[part, :])
        first += half


def add_spread_body(n_high, kept, received, *outs):
    piece = outs[0].shape[0]
    place = owner_at(lax.axis_index("row") // 2, n_high)
    for flip, out in enumerate(outs):
        which = lax.bitwise_xor(place, flip)
        if piece % 8 == 0:
            part = pl.ds(pl.multiple_of(which * piece, piece), piece)
            out[...] = kept[part, :] + received[part, :]
            continue
        found = jnp.zeros(out.shape, F32)
        for i in range(n_high):
            part = pl.ds(i * piece, piece)
            found = jnp.where(which == i, kept[part, :] + received[part, :], found)
        out[...] = found


def final_corange_body(counts, rows, *refs):
    out = refs[-1]
    first, used = 0, 0
    for count, piece in zip(counts, rows):
        terms = refs[used : used + count]
        parts = [term[pl.ds(i, piece), :] for term in terms for i in range(0, term.shape[0], piece)]
        out[pl.ds(first, piece), :] = functools.reduce(jnp.add, parts)
        first += piece
        used += count


def final_sketch_body(n_row, pieces, splits, *refs):
    out, done = refs[-2:]
    n, rows = sum(splits), refs[0].shape[1]
    parity = lax.rem(lax.axis_index("col"), 2)
    for side in range(2):
        parts = refs[side * n : (side + 1) * n]
        first = (parity if side == 0 else 1 - parity) * rows
        for b in range(rows // 128):
            lanes = pl.ds(b * 128, 128)
            found = []
            for r in range(n_row):
                place, used = owner_at(r, n_row), 0
                for piece, split in zip(pieces, splits):
                    per_part = n_row // split
                    part = parts[used + place // per_part]
                    found.append(part[pl.ds(place % per_part * piece, piece), lanes])
                    used += split
            block = jnp.concatenate(found, axis=0)
            out[pl.ds(pl.multiple_of(first + b * 128, 128), 128), :] = block.T
    done[...] = jnp.zeros_like(done)


def swap(x, axis, size, bit):
    return lax.ppermute(x, axis, [(i, i ^ bit) for i in range(size)])


def shards(n_row, n_col, delta, omega):
    rows, d = delta.shape
    k = omega.shape[1]
    half = rows // 2
    per_owner = k // n_row
    pieces = [per_owner * part // sum(EIGHTHS) for part in EIGHTHS] if per_owner % 8 == 0 else [1] * per_owner
    widths = [piece * n_row for piece in pieces]
    n = len(pieces)
    splits = SPLITS if len(SPLITS) == n else (2,) * n
    bits = [1 << i for i in range(n_row.bit_length() - 1)]

    in_hbm = pltpu.with_memory_space_constraint(delta, pltpu.HBM)
    sems = pltpu.SemaphoreType.DMA((half // BLOCK,))
    held_other, omega_t, to_send = call(
        functools.partial(first_half_body, n_row, pieces),
        (in_hbm, pltpu.with_memory_space_constraint(omega, pltpu.HBM)),
        [((half, d), BF16), ((k, d), BF16), ((widths[0], half), F32)],
        "aa",
        scratch=[pltpu.VMEM((d, k), BF16), sems, pltpu.SemaphoreType.DMA],
    )
    received = swap(to_send, "col", n_col, 1)
    outs = [((half, d), BF16), ((widths[0], half), F32)]
    held_own, kept = call(second_half_body, (in_hbm, omega_t), outs, "av", (to_send,), [sems])
    partial = call(add_body, (kept, received), [((widths[0], half), F32)])
    rest = k - widths[0]
    outs = [((rest // REST_PARTS, half), F32)] * REST_PARTS
    to_send = call(rest_half_body, (omega_t, held_other), outs, after=partial)
    received = [swap(x, "col", n_col, 1) for x in to_send]
    kept = call(rest_half_body, (omega_t, held_own), [((rest, half), F32)], after=to_send[:1])
    outs = [((width, half), F32) for width in widths[1:]]
    partial += call(functools.partial(add_chunks_body, REST_PARTS), (*kept, *received), outs)
    bit = 2
    while bit < n_col // 2:
        moved = [swap(x, "col", n_col, bit) for x in partial]
        partial = [call(add_body, pair, [(pair[0].shape, F32)])[0] for pair in zip(partial, moved)]
        bit *= 2
    moved = [swap(x, "col", n_col, bit) for x in partial]

    owns, others, befores, pending = {}, {}, {}, {}
    sketch = None
    last = ()
    planned = n == 4 and len(bits) == 3
    groups = GROUPS if planned else tuple((c,) for c in range(n))
    modes = MODES if planned else ("pairs",) * n
    steps = ORDER if planned else ()
    if not steps:
        found = []
        for c in range(n):
            found += [(10 * c, f"own{c}"), (10 * c + 1, f"before{c}"), (10 * c + 2, f"send{c}")]
        for g, group in enumerate(groups):
            stages = 2 if modes[g] == "direct" else len(bits)
            found += [(10 * group[-1] + 9.5 + 10 * s, f"add{g}.{s}") for s in range(1, stages)]
        steps = [step for _, step in sorted(found)] + ["sketch"]
    for step in steps:
        weight = WEIGHTS.get(step, 0)
        if step.startswith("own"):
            c = int(step[3:])
            outs = [((widths[c] // splits[c], half), F32)] * splits[c]
            owns[c] = call(add_body, (partial[c], moved[c]), outs, after=last, weight=weight)
            others[c] = [swap(x, "col", n_col, 1) for x in owns[c]]
            last = (owns[c][0],)
        elif step.startswith("before"):
            c = int(step[6:])
            befores[c] = call(product_body, (*owns[c], held_own), [((widths[c], d), F32)], after=last, weight=weight)[0]
            last = (befores[c],)
        elif step.startswith("send"):
            c = int(step[4:])
            outs = [((widths[c] // 2, d), F32)] * 2
            total = pltpu.VMEM((widths[c], d), F32)
            args = (*others[c], held_other, befores[c])
            send, keep = call(product_send_body, args, outs, after=last, scratch=[total], weight=weight)
            pending[(c,)] = keep, swap(send, "row", n_row, bits[0])
            last = (keep,)
        elif step.startswith("add"):
            g, s = (int(x) for x in step[3:].split("."))
            group = groups[g]
            if modes[g] == "direct":
                outs = [((pieces[group[0]], d), F32)] * (n_row // 2)
                body = functools.partial(add_spread_body, n_row // 2)
                own, *sends = call(body, pending[group], outs, after=last, weight=weight)
                flips = [2 * owner_at(flip, n_row // 2) for flip in range(1, n_row // 2)]
                pending[group] = own, *[swap(x, "row", n_row, flip) for x, flip in zip(sends, flips)]
                last = (own,)
                continue
            if s == 1:
                pending[group] = [x for c in group for x in pending[(c,)]]
            segments = [widths[c] >> s for c in group]
            body = functools.partial(add_send_body, bits[s], segments)
            outs = [((sum(segments) // 2, d), F32)] * 2
            send, keep = call(body, pending[group], outs, after=last, weight=weight)
            pending[group] = keep, swap(send, "row", n_row, bits[s])
            last = (keep,)
        else:
            parts = [[x for found in halves.values() for x in found] for halves in (owns, others)]
            sketch, done = finish_sketch(n_row, k, pieces, splits, *parts, last)
            last = (done,)
    flat = [x for group in groups for x in pending[group]]
    if per_owner % 8 == 0:
        body = functools.partial(final_corange_body, [len(pending[group]) for group in groups], [sum(pieces[c] for c in group) for group in groups])
        corange = call(body, flat, [((per_owner, d), F32)], after=last, results=1, weight=WEIGHTS.get("F", 0))[0]
    else:
        corange = jnp.concatenate([functools.reduce(jnp.add, pending[group]) for group in groups], axis=0)
    return sketch, corange.T


def finish_sketch(n_row, k, pieces, splits, owns, others, after):
    half = owns[0].shape[1]
    if k // n_row % 8 == 0:
        body = functools.partial(final_sketch_body, n_row, pieces, splits)
        return call(body, (*owns, *others), [((2 * half, k), F32), ((8, 128), F32)], after=after, results=1)
    places = jnp.array([owner_at(r, n_row) for r in range(n_row)])

    def columns(parts):
        starts = [sum(splits[:c]) for c in range(len(splits))]
        parts = [jnp.concatenate(parts[start : start + split], axis=0) for start, split in zip(starts, splits)]
        found = [part.reshape(n_row, piece, half)[places] for part, piece in zip(parts, pieces)]
        return jnp.concatenate(found, axis=1).reshape(k, half).T

    own, other = columns(owns), columns(others)
    first = lax.rem(lax.axis_index("col"), 2) == 0
    return jnp.where(first, jnp.concatenate([own, other]), jnp.concatenate([other, own])), after[0]


def solution(mesh):
    body = functools.partial(shards, mesh.shape["row"], mesh.shape["col"])
    in_specs = (P("row", "col"), P("col", None))
    out_specs = (P("row", None), P("col", "row"))
    return jax.shard_map(body, mesh=mesh, in_specs=in_specs, out_specs=out_specs, check_vma=False)
```

```python
import functools

import jax
import jax.numpy as jnp
from jax import lax
from jax.experimental import pallas as pl
from jax.experimental.pallas import tpu as pltpu
from jax.sharding import PartitionSpec as P

EIGHTHS = (2, 2, 2, 2)
BLOCK = 512
STREAM = 128
OMEGA_PARTS = 4
F32 = jnp.float32
BF16 = jnp.bfloat16
NT = (((1,), (1,)), ((), ()))
SPECS = {"v": pl.BlockSpec(memory_space=pltpu.VMEM), "a": pl.BlockSpec(memory_space=pl.ANY)}
ORDER = ('own0', 'before0', 'send0', 'own1', 'before1', 'send1', 'add0.1', 'own2', 'before2', 'send2', 'add1.1', 'own3', 'before3', 'send3', 'add2.1', 'add1.2', 'add0.2', 'add2.2', 'sketch', 'add3.1')
REST_PARTS = 4
WEIGHTS = {'add2.1': 500000000, 'F': 500000000, 'send1': 0, 'send0': 0, 'send3': 0, 'add2.2': 200000000, 'add0.2': 1000000000, 'own2': 500000000, 'before1': 500000000, 'add0.1': 500000000, 'before3': 2000000000, 'sketch': 500000000, 'send2': 0, 'add1.2': 200000000}
SPLITS = (2, 2, 2, 2)
GROUPS = ((0,), (1,), (2,), (3,))
MODES = ('pairs', 'pairs', 'pairs', 'direct')


def call(body, args, outs, kinds=None, after=(), scratch=(), results=0, weight=0):
    n = len(args)
    kinds = (kinds or "v" * n) + "a" * len(after)

    def run(*refs):
        body(*refs[:n], *refs[len(kinds) :])

    return pl.pallas_call(
        run,
        out_shape=[pltpu.VMEM(*o) if i >= results else jax.ShapeDtypeStruct(*o) for i, o in enumerate(outs)],
        in_specs=[SPECS[kind] for kind in kinds],
        out_specs=[SPECS["v"]] * len(outs),
        scratch_shapes=list(scratch),
        cost_estimate=pl.CostEstimate(flops=weight, bytes_accessed=0, transcendentals=0),
        compiler_params=pltpu.CompilerParams(vmem_limit_bytes=16 << 20),
    )(*args, *after)


def owner_at(index, n_row):
    owner, bit = index * 0, 1
    while bit < n_row:
        owner = 2 * owner + index % 2
        index = index // 2
        bit *= 2
    return owner


def column_of(position, k, n_row, pieces):
    column, first, done = position * 0, 0, 0
    for piece in pieces:
        rest = position - first
        found = owner_at(rest // piece, n_row) * (k // n_row) + done + rest % piece
        column = jnp.where((rest >= 0) & (rest < piece * n_row), found, column)
        first += piece * n_row
        done += piece
    return column


def stream_half(delta, held, sem, mine):
    rows = held.shape[0]
    parity = lax.rem(lax.axis_index("col"), 2)
    first = (parity if mine else 1 - parity) * rows
    copies = []
    for b in range(rows // STREAM):
        source = delta.at[pl.ds(pl.multiple_of(first + b * STREAM, STREAM), STREAM), :]
        copies.append(pltpu.make_async_copy(source, held.at[pl.ds(b * STREAM, STREAM), :], sem.at[b]))
        copies[-1].start()
    return copies


def sketch_half(omega_t, held, copies, out):
    each = BLOCK // STREAM
    for b in range(held.shape[0] // BLOCK):
        for copy in copies[b * each : (b + 1) * each]:
            copy.wait()
        block = pl.ds(b * BLOCK, BLOCK)
        out[:, block] = lax.dot_general(omega_t[: out.shape[0], :], held[block, :], NT, preferred_element_type=F32)


def first_half_body(n_row, pieces, delta, omega, held, omega_t, out, omega_v, sem, omega_sem):
    k = omega_t.shape[0]
    fetches = []
    for i in range(OMEGA_PARTS):
        part = pl.ds(i * (omega.shape[0] // OMEGA_PARTS), omega.shape[0] // OMEGA_PARTS)
        fetches.append(pltpu.make_async_copy(omega.at[part, :], omega_v.at[part, :], omega_sem.at[i]))
        fetches[-1].start()
    copies = stream_half(delta, held, sem, False)
    position = lax.broadcasted_iota(jnp.int32, (k, k), 0)
    column = lax.broadcasted_iota(jnp.int32, (k, k), 1)
    pick = jnp.where(column_of(position, k, n_row, pieces) == column, 1.0, 0.0).astype(BF16)
    for fetch in fetches:
        fetch.wait()
    omega_t[...] = lax.dot_general(pick, omega_v[...], NT, preferred_element_type=F32).astype(BF16)
    sketch_half(omega_t, held, copies, out)


def second_half_body(delta, omega_t, held, out, sem):
    sketch_half(omega_t, held, stream_half(delta, held, sem, True), out)


def rest_half_body(omega_t, held, *outs):
    rows = sum(out.shape[0] for out in outs)
    later = omega_t[omega_t.shape[0] - rows :, :]
    for b in range(held.shape[0] // BLOCK):
        block = pl.ds(b * BLOCK, BLOCK)
        found = lax.dot_general(later, held[block, :], NT, preferred_element_type=F32)
        first = 0
        for out in outs:
            out[:, block] = found[first : first + out.shape[0]]
            first += out.shape[0]


def add_chunks_body(parts, kept, *refs):
    received, first = joined(refs[:parts]), 0
    for out in refs[parts:]:
        part = pl.ds(first, out.shape[0])
        out[...] = kept[part, :] + received[first : first + out.shape[0]]
        first += out.shape[0]


def add_body(a, b, *outs):
    first = 0
    for out in outs:
        part = pl.ds(first, out.shape[0])
        out[...] = a[part, :] + b[part, :]
        first += out.shape[0]


def joined(refs):
    return jnp.concatenate([ref[...] for ref in refs], axis=0)


def product_body(*refs):
    *sketch, held, out = refs
    out[...] = jnp.dot(joined(sketch).astype(BF16), held[...], preferred_element_type=F32)


def split(bit, segments, refs, send, keep):
    own = lax.rem(lax.axis_index("row") // bit, 2)
    start, first = 0, 0
    for rows in segments:
        half = rows // 2
        for out, which in ((send, 1 - own), (keep, own)):
            if half % 8:
                low, high = (
                    functools.reduce(jnp.add, [ref[pl.ds(start + i * half, half), :] for ref in refs]) for i in range(2)
                )
                value = jnp.where(which == 0, low, high)
            else:
                part = pl.ds(pl.multiple_of(start + which * half, 8), half)
                value = functools.reduce(jnp.add, [ref[part, :] for ref in refs])
            out[pl.ds(first, half), :] = value
        start += rows
        first += half


def product_send_body(*refs):
    *sketch, held, before, send, keep, total = refs
    total[...] = before[...] + jnp.dot(joined(sketch).astype(BF16), held[...], preferred_element_type=F32)
    split(1, [total.shape[0]], [total], send, keep)


def add_send_body(bit, segments, *refs):
    *pairs, send, keep = refs
    first = 0
    for kept, got in zip(pairs[::2], pairs[1::2]):
        mine = segments if len(pairs) == 2 else [kept.shape[0]]
        half = kept.shape[0] // 2
        part = pl.ds(first, half)
        split(bit, mine, [kept, got], send.at[part, :], keep.at[part, :])
        first += half


def add_spread_body(n_high, kept, received, *outs):
    piece = outs[0].shape[0]
    place = owner_at(lax.axis_index("row") // 2, n_high)
    for flip, out in enumerate(outs):
        which = lax.bitwise_xor(place, flip)
        if piece % 8 == 0:
            part = pl.ds(pl.multiple_of(which * piece, piece), piece)
            out[...] = kept[part, :] + received[part, :]
            continue
        found = jnp.zeros(out.shape, F32)
        for i in range(n_high):
            part = pl.ds(i * piece, piece)
            found = jnp.where(which == i, kept[part, :] + received[part, :], found)
        out[...] = found


def final_corange_body(counts, rows, *refs):
    out = refs[-1]
    first, used = 0, 0
    for count, piece in zip(counts, rows):
        terms = refs[used : used + count]
        parts = [term[pl.ds(i, piece), :] for term in terms for i in range(0, term.shape[0], piece)]
        out[pl.ds(first, piece), :] = functools.reduce(jnp.add, parts)
        first += piece
        used += count


def final_sketch_body(n_row, pieces, splits, *refs):
    out, done = refs[-2:]
    n, rows = sum(splits), refs[0].shape[1]
    parity = lax.rem(lax.axis_index("col"), 2)
    for side in range(2):
        parts = refs[side * n : (side + 1) * n]
        first = (parity if side == 0 else 1 - parity) * rows
        for b in range(rows // 128):
            lanes = pl.ds(b * 128, 128)
            found = []
            for r in range(n_row):
                place, used = owner_at(r, n_row), 0
                for piece, split in zip(pieces, splits):
                    per_part = n_row // split
                    part = parts[used + place // per_part]
                    found.append(part[pl.ds(place % per_part * piece, piece), lanes])
                    used += split
            block = jnp.concatenate(found, axis=0)
            out[pl.ds(pl.multiple_of(first + b * 128, 128), 128), :] = block.T
    done[...] = jnp.zeros_like(done)


def swap(x, axis, size, bit):
    return lax.ppermute(x, axis, [(i, i ^ bit) for i in range(size)])


def shards(n_row, n_col, delta, omega):
    rows, d = delta.shape
    k = omega.shape[1]
    half = rows // 2
    per_owner = k // n_row
    pieces = [per_owner * part // sum(EIGHTHS) for part in EIGHTHS] if per_owner % 8 == 0 else [1] * per_owner
    widths = [piece * n_row for piece in pieces]
    n = len(pieces)
    splits = SPLITS if len(SPLITS) == n else (2,) * n
    bits = [1 << i for i in range(n_row.bit_length() - 1)]

    in_hbm = pltpu.with_memory_space_constraint(delta, pltpu.HBM)
    sems = pltpu.SemaphoreType.DMA((half // STREAM,))
    held_other, omega_t, to_send = call(
        functools.partial(first_half_body, n_row, pieces),
        (in_hbm, pltpu.with_memory_space_constraint(omega, pltpu.HBM)),
        [((half, d), BF16), ((k, d), BF16), ((widths[0], half), F32)],
        "aa",
        scratch=[pltpu.VMEM((d, k), BF16), sems, pltpu.SemaphoreType.DMA((OMEGA_PARTS,))],
    )
    received = swap(to_send, "col", n_col, 1)
    outs = [((half, d), BF16), ((widths[0], half), F32)]
    held_own, kept = call(second_half_body, (in_hbm, omega_t), outs, "av", (to_send,), [sems])
    partial = call(add_body, (kept, received), [((widths[0], half), F32)])
    rest = k - widths[0]
    outs = [((rest // REST_PARTS, half), F32)] * REST_PARTS
    to_send = call(rest_half_body, (omega_t, held_other), outs, after=partial)
    received = [swap(x, "col", n_col, 1) for x in to_send]
    kept = call(rest_half_body, (omega_t, held_own), [((rest, half), F32)], after=to_send[:1])
    outs = [((width, half), F32) for width in widths[1:]]
    partial += call(functools.partial(add_chunks_body, REST_PARTS), (*kept, *received), outs)
    bit = 2
    while bit < n_col // 2:
        moved = [swap(x, "col", n_col, bit) for x in partial]
        partial = [call(add_body, pair, [(pair[0].shape, F32)])[0] for pair in zip(partial, moved)]
        bit *= 2
    moved = [swap(x, "col", n_col, bit) for x in partial]

    owns, others, befores, pending = {}, {}, {}, {}
    sketch = None
    last = ()
    planned = n == 4 and len(bits) == 3
    groups = GROUPS if planned else tuple((c,) for c in range(n))
    modes = MODES if planned else ("pairs",) * n
    steps = ORDER if planned else ()
    if not steps:
        found = []
        for c in range(n):
            found += [(10 * c, f"own{c}"), (10 * c + 1, f"before{c}"), (10 * c + 2, f"send{c}")]
        for g, group in enumerate(groups):
            stages = 2 if modes[g] == "direct" else len(bits)
            found += [(10 * group[-1] + 9.5 + 10 * s, f"add{g}.{s}") for s in range(1, stages)]
        steps = [step for _, step in sorted(found)] + ["sketch"]
    for step in steps:
        weight = WEIGHTS.get(step, 0)
        if step.startswith("own"):
            c = int(step[3:])
            outs = [((widths[c] // splits[c], half), F32)] * splits[c]
            owns[c] = call(add_body, (partial[c], moved[c]), outs, after=last, weight=weight)
            others[c] = [swap(x, "col", n_col, 1) for x in owns[c]]
            last = (owns[c][0],)
        elif step.startswith("before"):
            c = int(step[6:])
            befores[c] = call(product_body, (*owns[c], held_own), [((widths[c], d), F32)], after=last, weight=weight)[0]
            last = (befores[c],)
        elif step.startswith("send"):
            c = int(step[4:])
            outs = [((widths[c] // 2, d), F32)] * 2
            total = pltpu.VMEM((widths[c], d), F32)
            args = (*others[c], held_other, befores[c])
            send, keep = call(product_send_body, args, outs, after=last, scratch=[total], weight=weight)
            pending[(c,)] = keep, swap(send, "row", n_row, bits[0])
            last = (keep,)
        elif step.startswith("add"):
            g, s = (int(x) for x in step[3:].split("."))
            group = groups[g]
            if modes[g] == "direct":
                outs = [((pieces[group[0]], d), F32)] * (n_row // 2)
                body = functools.partial(add_spread_body, n_row // 2)
                own, *sends = call(body, pending[group], outs, after=last, weight=weight)
                flips = [2 * owner_at(flip, n_row // 2) for flip in range(1, n_row // 2)]
                pending[group] = own, *[swap(x, "row", n_row, flip) for x, flip in zip(sends, flips)]
                last = (own,)
                continue
            if s == 1:
                pending[group] = [x for c in group for x in pending[(c,)]]
            segments = [widths[c] >> s for c in group]
            body = functools.partial(add_send_body, bits[s], segments)
            outs = [((sum(segments) // 2, d), F32)] * 2
            send, keep = call(body, pending[group], outs, after=last, weight=weight)
            pending[group] = keep, swap(send, "row", n_row, bits[s])
            last = (keep,)
        else:
            parts = [[x for found in halves.values() for x in found] for halves in (owns, others)]
            sketch, done = finish_sketch(n_row, k, pieces, splits, *parts, last)
            last = (done,)
    flat = [x for group in groups for x in pending[group]]
    if per_owner % 8 == 0:
        body = functools.partial(final_corange_body, [len(pending[group]) for group in groups], [sum(pieces[c] for c in group) for group in groups])
        corange = call(body, flat, [((per_owner, d), F32)], after=last, results=1, weight=WEIGHTS.get("F", 0))[0]
    else:
        corange = jnp.concatenate([functools.reduce(jnp.add, pending[group]) for group in groups], axis=0)
    return sketch, corange.T


def finish_sketch(n_row, k, pieces, splits, owns, others, after):
    half = owns[0].shape[1]
    if k // n_row % 8 == 0:
        body = functools.partial(final_sketch_body, n_row, pieces, splits)
        return call(body, (*owns, *others), [((2 * half, k), F32), ((8, 128), F32)], after=after, results=1)
    places = jnp.array([owner_at(r, n_row) for r in range(n_row)])

    def columns(parts):
        starts = [sum(splits[:c]) for c in range(len(splits))]
        parts = [jnp.concatenate(parts[start : start + split], axis=0) for start, split in zip(starts, splits)]
        found = [part.reshape(n_row, piece, half)[places] for part, piece in zip(parts, pieces)]
        return jnp.concatenate(found, axis=1).reshape(k, half).T

    own, other = columns(owns), columns(others)
    first = lax.rem(lax.axis_index("col"), 2) == 0
    return jnp.where(first, jnp.concatenate([own, other]), jnp.concatenate([other, own])), after[0]


def solution(mesh):
    body = functools.partial(shards, mesh.shape["row"], mesh.shape["col"])
    in_specs = (P("row", "col"), P("col", None))
    out_specs = (P("row", None), P("col", "row"))
    return jax.shard_map(body, mesh=mesh, in_specs=in_specs, out_specs=out_specs, check_vma=False)
```

```python
import functools

import jax
import jax.numpy as jnp
from jax import lax
from jax.experimental import pallas as pl
from jax.experimental.pallas import tpu as pltpu
from jax.sharding import PartitionSpec as P

EIGHTHS = (2, 2, 2, 2)
BLOCK = 512
STREAM = 256
F32 = jnp.float32
BF16 = jnp.bfloat16
NT = (((1,), (1,)), ((), ()))
SPECS = {"v": pl.BlockSpec(memory_space=pltpu.VMEM), "a": pl.BlockSpec(memory_space=pl.ANY)}
ORDER = ('own0', 'before0', 'send0', 'own1', 'before1', 'send1', 'add0.1', 'own2', 'before2', 'send2', 'own3', 'add1.1', 'add0.2', 'before3', 'send3', 'add2.1', 'add1.2', 'add2.2', 'add3.1', 'sketch')
REST_PARTS = 4
WEIGHTS = {'add2.1': 500000000, 'F': 500000000, 'send1': 0, 'send0': 0, 'send3': 0, 'add2.2': 200000000, 'add0.2': 1000000000, 'own2': 500000000, 'before1': 0, 'add0.1': 200000000}
SPLITS = (2, 2, 2, 2)
GROUPS = ((0,), (1,), (2,), (3,))
MODES = ('pairs', 'pairs', 'pairs', 'direct')


def call(body, args, outs, kinds=None, after=(), scratch=(), results=0, weight=0):
    n = len(args)
    kinds = (kinds or "v" * n) + "a" * len(after)

    def run(*refs):
        body(*refs[:n], *refs[len(kinds) :])

    return pl.pallas_call(
        run,
        out_shape=[pltpu.VMEM(*o) if i >= results else jax.ShapeDtypeStruct(*o) for i, o in enumerate(outs)],
        in_specs=[SPECS[kind] for kind in kinds],
        out_specs=[SPECS["v"]] * len(outs),
        scratch_shapes=list(scratch),
        cost_estimate=pl.CostEstimate(flops=weight, bytes_accessed=0, transcendentals=0),
        compiler_params=pltpu.CompilerParams(vmem_limit_bytes=16 << 20),
    )(*args, *after)


def owner_at(index, n_row):
    owner, bit = index * 0, 1
    while bit < n_row:
        owner = 2 * owner + index % 2
        index = index // 2
        bit *= 2
    return owner


def column_of(position, k, n_row, pieces):
    column, first, done = position * 0, 0, 0
    for piece in pieces:
        rest = position - first
        found = owner_at(rest // piece, n_row) * (k // n_row) + done + rest % piece
        column = jnp.where((rest >= 0) & (rest < piece * n_row), found, column)
        first += piece * n_row
        done += piece
    return column


def half_copies(delta, held, sem, mine):
    rows = held.shape[0]
    parity = lax.rem(lax.axis_index("col"), 2)
    first = (parity if mine else 1 - parity) * rows
    copies = []
    for b in range(rows // STREAM):
        source = delta.at[pl.ds(pl.multiple_of(first + b * STREAM, STREAM), STREAM), :]
        copies.append(pltpu.make_async_copy(source, held.at[pl.ds(b * STREAM, STREAM), :], sem.at[b]))
    return copies


def sketch_half(omega_t, held, copies, out):
    for b, copy in enumerate(copies):
        copy.wait()
        block = pl.ds(b * STREAM, STREAM)
        out[:, block] = lax.dot_general(omega_t[: out.shape[0], :], held[block, :], NT, preferred_element_type=F32)


def first_half_body(n_row, pieces, delta, omega, held, omega_t, out, omega_v, sem, omega_sem):
    k = omega_t.shape[0]
    fetch = pltpu.make_async_copy(omega, omega_v, omega_sem)
    fetch.start()
    copies = half_copies(delta, held, sem, False)
    copies[0].start()
    position = lax.broadcasted_iota(jnp.int32, (k, k), 0)
    column = lax.broadcasted_iota(jnp.int32, (k, k), 1)
    pick = jnp.where(column_of(position, k, n_row, pieces) == column, 1.0, 0.0).astype(BF16)
    fetch.wait()
    for copy in copies[1:]:
        copy.start()
    omega_t[...] = lax.dot_general(pick, omega_v[...], NT, preferred_element_type=F32).astype(BF16)
    sketch_half(omega_t, held, copies, out)


def second_half_body(delta, omega_t, held, out, sem):
    copies = half_copies(delta, held, sem, True)
    for copy in copies:
        copy.start()
    sketch_half(omega_t, held, copies, out)


def rest_half_body(omega_t, held, *outs):
    rows = sum(out.shape[0] for out in outs)
    later = omega_t[omega_t.shape[0] - rows :, :]
    for b in range(held.shape[0] // BLOCK):
        block = pl.ds(b * BLOCK, BLOCK)
        found = lax.dot_general(later, held[block, :], NT, preferred_element_type=F32)
        first = 0
        for out in outs:
            out[:, block] = found[first : first + out.shape[0]]
            first += out.shape[0]


def add_chunks_body(parts, kept, *refs):
    received, first = joined(refs[:parts]), 0
    for out in refs[parts:]:
        part = pl.ds(first, out.shape[0])
        out[...] = kept[part, :] + received[first : first + out.shape[0]]
        first += out.shape[0]


def add_body(a, b, *outs):
    first = 0
    for out in outs:
        part = pl.ds(first, out.shape[0])
        out[...] = a[part, :] + b[part, :]
        first += out.shape[0]


def joined(refs):
    return jnp.concatenate([ref[...] for ref in refs], axis=0)


def product_body(*refs):
    *sketch, held, out = refs
    out[...] = jnp.dot(joined(sketch).astype(BF16), held[...], preferred_element_type=F32)


def split(bit, segments, refs, send, keep):
    own = lax.rem(lax.axis_index("row") // bit, 2)
    start, first = 0, 0
    for rows in segments:
        half = rows // 2
        for out, which in ((send, 1 - own), (keep, own)):
            if half % 8:
                low, high = (
                    functools.reduce(jnp.add, [ref[pl.ds(start + i * half, half), :] for ref in refs]) for i in range(2)
                )
                value = jnp.where(which == 0, low, high)
            else:
                part = pl.ds(pl.multiple_of(start + which * half, 8), half)
                value = functools.reduce(jnp.add, [ref[part, :] for ref in refs])
            out[pl.ds(first, half), :] = value
        start += rows
        first += half


def product_send_body(*refs):
    *sketch, held, before, send, keep, total = refs
    total[...] = before[...] + jnp.dot(joined(sketch).astype(BF16), held[...], preferred_element_type=F32)
    split(1, [total.shape[0]], [total], send, keep)


def add_send_body(bit, segments, *refs):
    *pairs, send, keep = refs
    first = 0
    for kept, got in zip(pairs[::2], pairs[1::2]):
        mine = segments if len(pairs) == 2 else [kept.shape[0]]
        half = kept.shape[0] // 2
        part = pl.ds(first, half)
        split(bit, mine, [kept, got], send.at[part, :], keep.at[part, :])
        first += half


def add_spread_body(n_high, kept, received, *outs):
    piece = outs[0].shape[0]
    place = owner_at(lax.axis_index("row") // 2, n_high)
    for flip, out in enumerate(outs):
        which = lax.bitwise_xor(place, flip)
        if piece % 8 == 0:
            part = pl.ds(pl.multiple_of(which * piece, piece), piece)
            out[...] = kept[part, :] + received[part, :]
            continue
        found = jnp.zeros(out.shape, F32)
        for i in range(n_high):
            part = pl.ds(i * piece, piece)
            found = jnp.where(which == i, kept[part, :] + received[part, :], found)
        out[...] = found


def final_corange_body(counts, rows, *refs):
    out = refs[-1]
    first, used = 0, 0
    for count, piece in zip(counts, rows):
        terms = refs[used : used + count]
        parts = [term[pl.ds(i, piece), :] for term in terms for i in range(0, term.shape[0], piece)]
        out[pl.ds(first, piece), :] = functools.reduce(jnp.add, parts)
        first += piece
        used += count


def final_sketch_body(n_row, pieces, splits, *refs):
    out, done = refs[-2:]
    n, rows = sum(splits), refs[0].shape[1]
    parity = lax.rem(lax.axis_index("col"), 2)
    for side in range(2):
        parts = refs[side * n : (side + 1) * n]
        first = (parity if side == 0 else 1 - parity) * rows
        for b in range(rows // 128):
            lanes = pl.ds(b * 128, 128)
            found = []
            for r in range(n_row):
                place, used = owner_at(r, n_row), 0
                for piece, split in zip(pieces, splits):
                    per_part = n_row // split
                    part = parts[used + place // per_part]
                    found.append(part[pl.ds(place % per_part * piece, piece), lanes])
                    used += split
            block = jnp.concatenate(found, axis=0)
            out[pl.ds(pl.multiple_of(first + b * 128, 128), 128), :] = block.T
    done[...] = jnp.zeros_like(done)


def swap(x, axis, size, bit):
    return lax.ppermute(x, axis, [(i, i ^ bit) for i in range(size)])


def shards(n_row, n_col, delta, omega):
    rows, d = delta.shape
    k = omega.shape[1]
    half = rows // 2
    per_owner = k // n_row
    pieces = [per_owner * part // sum(EIGHTHS) for part in EIGHTHS] if per_owner % 8 == 0 else [1] * per_owner
    widths = [piece * n_row for piece in pieces]
    n = len(pieces)
    splits = SPLITS if len(SPLITS) == n else (2,) * n
    bits = [1 << i for i in range(n_row.bit_length() - 1)]

    in_hbm = pltpu.with_memory_space_constraint(delta, pltpu.HBM)
    sems = pltpu.SemaphoreType.DMA((half // STREAM,))
    held_other, omega_t, to_send = call(
        functools.partial(first_half_body, n_row, pieces),
        (in_hbm, pltpu.with_memory_space_constraint(omega, pltpu.HBM)),
        [((half, d), BF16), ((k, d), BF16), ((widths[0], half), F32)],
        "aa",
        scratch=[pltpu.VMEM((d, k), BF16), sems, pltpu.SemaphoreType.DMA],
    )
    received = swap(to_send, "col", n_col, 1)
    outs = [((half, d), BF16), ((widths[0], half), F32)]
    held_own, kept = call(second_half_body, (in_hbm, omega_t), outs, "av", (to_send,), [sems])
    partial = call(add_body, (kept, received), [((widths[0], half), F32)])
    rest = k - widths[0]
    outs = [((rest // REST_PARTS, half), F32)] * REST_PARTS
    to_send = call(rest_half_body, (omega_t, held_other), outs, after=partial)
    received = [swap(x, "col", n_col, 1) for x in to_send]
    kept = call(rest_half_body, (omega_t, held_own), [((rest, half), F32)], after=to_send[:1])
    outs = [((width, half), F32) for width in widths[1:]]
    partial += call(functools.partial(add_chunks_body, REST_PARTS), (*kept, *received), outs)
    bit = 2
    while bit < n_col // 2:
        moved = [swap(x, "col", n_col, bit) for x in partial]
        partial = [call(add_body, pair, [(pair[0].shape, F32)])[0] for pair in zip(partial, moved)]
        bit *= 2
    moved = [swap(x, "col", n_col, bit) for x in partial]

    owns, others, befores, pending = {}, {}, {}, {}
    sketch = None
    last = ()
    planned = n == 4 and len(bits) == 3
    groups = GROUPS if planned else tuple((c,) for c in range(n))
    modes = MODES if planned else ("pairs",) * n
    steps = ORDER if planned else ()
    if not steps:
        found = []
        for c in range(n):
            found += [(10 * c, f"own{c}"), (10 * c + 1, f"before{c}"), (10 * c + 2, f"send{c}")]
        for g, group in enumerate(groups):
            stages = 2 if modes[g] == "direct" else len(bits)
            found += [(10 * group[-1] + 9.5 + 10 * s, f"add{g}.{s}") for s in range(1, stages)]
        steps = [step for _, step in sorted(found)] + ["sketch"]
    for step in steps:
        weight = WEIGHTS.get(step, 0)
        if step.startswith("own"):
            c = int(step[3:])
            outs = [((widths[c] // splits[c], half), F32)] * splits[c]
            owns[c] = call(add_body, (partial[c], moved[c]), outs, after=last, weight=weight)
            others[c] = [swap(x, "col", n_col, 1) for x in owns[c]]
            last = (owns[c][0],)
        elif step.startswith("before"):
            c = int(step[6:])
            befores[c] = call(product_body, (*owns[c], held_own), [((widths[c], d), F32)], after=last, weight=weight)[0]
            last = (befores[c],)
        elif step.startswith("send"):
            c = int(step[4:])
            outs = [((widths[c] // 2, d), F32)] * 2
            total = pltpu.VMEM((widths[c], d), F32)
            args = (*others[c], held_other, befores[c])
            send, keep = call(product_send_body, args, outs, after=last, scratch=[total], weight=weight)
            pending[(c,)] = keep, swap(send, "row", n_row, bits[0])
            last = (keep,)
        elif step.startswith("add"):
            g, s = (int(x) for x in step[3:].split("."))
            group = groups[g]
            if modes[g] == "direct":
                outs = [((pieces[group[0]], d), F32)] * (n_row // 2)
                body = functools.partial(add_spread_body, n_row // 2)
                own, *sends = call(body, pending[group], outs, after=last, weight=weight)
                flips = [2 * owner_at(flip, n_row // 2) for flip in range(1, n_row // 2)]
                pending[group] = own, *[swap(x, "row", n_row, flip) for x, flip in zip(sends, flips)]
                last = (own,)
                continue
            if s == 1:
                pending[group] = [x for c in group for x in pending[(c,)]]
            segments = [widths[c] >> s for c in group]
            body = functools.partial(add_send_body, bits[s], segments)
            outs = [((sum(segments) // 2, d), F32)] * 2
            send, keep = call(body, pending[group], outs, after=last, weight=weight)
            pending[group] = keep, swap(send, "row", n_row, bits[s])
            last = (keep,)
        else:
            parts = [[x for found in halves.values() for x in found] for halves in (owns, others)]
            sketch, done = finish_sketch(n_row, k, pieces, splits, *parts, last)
            last = (done,)
    flat = [x for group in groups for x in pending[group]]
    if per_owner % 8 == 0:
        body = functools.partial(final_corange_body, [len(pending[group]) for group in groups], [sum(pieces[c] for c in group) for group in groups])
        corange = call(body, flat, [((per_owner, d), F32)], after=last, results=1, weight=WEIGHTS.get("F", 0))[0]
    else:
        corange = jnp.concatenate([functools.reduce(jnp.add, pending[group]) for group in groups], axis=0)
    return sketch, corange.T


def finish_sketch(n_row, k, pieces, splits, owns, others, after):
    half = owns[0].shape[1]
    if k // n_row % 8 == 0:
        body = functools.partial(final_sketch_body, n_row, pieces, splits)
        return call(body, (*owns, *others), [((2 * half, k), F32), ((8, 128), F32)], after=after, results=1)
    places = jnp.array([owner_at(r, n_row) for r in range(n_row)])

    def columns(parts):
        starts = [sum(splits[:c]) for c in range(len(splits))]
        parts = [jnp.concatenate(parts[start : start + split], axis=0) for start, split in zip(starts, splits)]
        found = [part.reshape(n_row, piece, half)[places] for part, piece in zip(parts, pieces)]
        return jnp.concatenate(found, axis=1).reshape(k, half).T

    own, other = columns(owns), columns(others)
    first = lax.rem(lax.axis_index("col"), 2) == 0
    return jnp.where(first, jnp.concatenate([own, other]), jnp.concatenate([other, own])), after[0]


def solution(mesh):
    body = functools.partial(shards, mesh.shape["row"], mesh.shape["col"])
    in_specs = (P("row", "col"), P("col", None))
    out_specs = (P("row", None), P("col", "row"))
    return jax.shard_map(body, mesh=mesh, in_specs=in_specs, out_specs=out_specs, check_vma=False)
```

```python
import functools

import jax
import jax.numpy as jnp
from jax import lax
from jax.experimental import pallas as pl
from jax.experimental.pallas import tpu as pltpu
from jax.sharding import PartitionSpec as P

EIGHTHS = (2, 2, 2, 2)
BLOCK = 512
F32 = jnp.float32
BF16 = jnp.bfloat16
NT = (((1,), (1,)), ((), ()))
SPECS = {"v": pl.BlockSpec(memory_space=pltpu.VMEM), "a": pl.BlockSpec(memory_space=pl.ANY)}
ORDER = ('own0', 'before0', 'send0', 'own1', 'before1', 'send1', 'add0.1', 'own2', 'before2', 'send2', 'own3', 'add1.1', 'add0.2', 'before3', 'send3', 'add2.1', 'add1.2', 'add2.2', 'add3.1', 'sketch')
WEIGHTS = {'add2.1': 500000000, 'F': 500000000, 'send1': 0, 'send0': 0, 'send3': 0, 'add2.2': 200000000, 'add0.2': 1000000000, 'own2': 500000000, 'before1': 0, 'add0.1': 200000000}
SPLITS = (2, 2, 2, 2)
GROUPS = ((0,), (1,), (2,), (3,))
MODES = ('pairs', 'pairs', 'pairs', 'direct')


def call(body, args, outs, kinds=None, after=(), scratch=(), results=0, weight=0):
    n = len(args)
    kinds = (kinds or "v" * n) + "a" * len(after)

    def run(*refs):
        body(*refs[:n], *refs[len(kinds) :])

    return pl.pallas_call(
        run,
        out_shape=[pltpu.VMEM(*o) if i >= results else jax.ShapeDtypeStruct(*o) for i, o in enumerate(outs)],
        in_specs=[SPECS[kind] for kind in kinds],
        out_specs=[SPECS["v"]] * len(outs),
        scratch_shapes=list(scratch),
        cost_estimate=pl.CostEstimate(flops=weight, bytes_accessed=0, transcendentals=0),
        compiler_params=pltpu.CompilerParams(vmem_limit_bytes=16 << 20),
    )(*args, *after)


def owner_at(index, n_row):
    owner, bit = index * 0, 1
    while bit < n_row:
        owner = 2 * owner + index % 2
        index = index // 2
        bit *= 2
    return owner


def column_of(position, k, n_row, pieces):
    column, first, done = position * 0, 0, 0
    for piece in pieces:
        rest = position - first
        found = owner_at(rest // piece, n_row) * (k // n_row) + done + rest % piece
        column = jnp.where((rest >= 0) & (rest < piece * n_row), found, column)
        first += piece * n_row
        done += piece
    return column


def stream_half(delta, held, sem, mine):
    rows = held.shape[0]
    parity = lax.rem(lax.axis_index("col"), 2)
    first = (parity if mine else 1 - parity) * rows
    copies = []
    for b in range(rows // BLOCK):
        source = delta.at[pl.ds(pl.multiple_of(first + b * BLOCK, BLOCK), BLOCK), :]
        copies.append(pltpu.make_async_copy(source, held.at[pl.ds(b * BLOCK, BLOCK), :], sem.at[b]))
        copies[-1].start()
    return copies


def sketch_half(omega_t, held, copies, out):
    for b, copy in enumerate(copies):
        copy.wait()
        block = pl.ds(b * BLOCK, BLOCK)
        out[:, block] = lax.dot_general(omega_t[...], held[block, :], NT, preferred_element_type=F32)


def first_half_body(n_row, pieces, delta, omega, held, omega_t, out, omega_v, sem, omega_sem):
    k = out.shape[0]
    fetch = pltpu.make_async_copy(omega, omega_v, omega_sem)
    fetch.start()
    copies = stream_half(delta, held, sem, False)
    position = lax.broadcasted_iota(jnp.int32, (k, k), 0)
    column = lax.broadcasted_iota(jnp.int32, (k, k), 1)
    pick = jnp.where(column_of(position, k, n_row, pieces) == column, 1.0, 0.0).astype(BF16)
    fetch.wait()
    omega_t[...] = lax.dot_general(pick, omega_v[...], NT, preferred_element_type=F32).astype(BF16)
    sketch_half(omega_t, held, copies, out)


def second_half_body(delta, omega_t, held, out, sem):
    sketch_half(omega_t, held, stream_half(delta, held, sem, True), out)


def add_chunks_body(kept, received, *outs):
    first = 0
    for out in outs:
        part = pl.ds(first, out.shape[0])
        out[...] = kept[part, :] + received[part, :]
        first += out.shape[0]


def add_body(a, b, *outs):
    first = 0
    for out in outs:
        part = pl.ds(first, out.shape[0])
        out[...] = a[part, :] + b[part, :]
        first += out.shape[0]


def joined(refs):
    return jnp.concatenate([ref[...] for ref in refs], axis=0)


def product_body(*refs):
    *sketch, held, out = refs
    out[...] = jnp.dot(joined(sketch).astype(BF16), held[...], preferred_element_type=F32)


def split(bit, segments, refs, send, keep):
    own = lax.rem(lax.axis_index("row") // bit, 2)
    start, first = 0, 0
    for rows in segments:
        half = rows // 2
        for out, which in ((send, 1 - own), (keep, own)):
            if half % 8:
                low, high = (
                    functools.reduce(jnp.add, [ref[pl.ds(start + i * half, half), :] for ref in refs]) for i in range(2)
                )
                value = jnp.where(which == 0, low, high)
            else:
                part = pl.ds(pl.multiple_of(start + which * half, 8), half)
                value = functools.reduce(jnp.add, [ref[part, :] for ref in refs])
            out[pl.ds(first, half), :] = value
        start += rows
        first += half


def product_send_body(*refs):
    *sketch, held, before, send, keep, total = refs
    total[...] = before[...] + jnp.dot(joined(sketch).astype(BF16), held[...], preferred_element_type=F32)
    split(1, [total.shape[0]], [total], send, keep)


def add_send_body(bit, segments, *refs):
    *pairs, send, keep = refs
    first = 0
    for kept, got in zip(pairs[::2], pairs[1::2]):
        mine = segments if len(pairs) == 2 else [kept.shape[0]]
        half = kept.shape[0] // 2
        part = pl.ds(first, half)
        split(bit, mine, [kept, got], send.at[part, :], keep.at[part, :])
        first += half


def add_spread_body(n_high, kept, received, *outs):
    piece = outs[0].shape[0]
    place = owner_at(lax.axis_index("row") // 2, n_high)
    for flip, out in enumerate(outs):
        which = lax.bitwise_xor(place, flip)
        if piece % 8 == 0:
            part = pl.ds(pl.multiple_of(which * piece, piece), piece)
            out[...] = kept[part, :] + received[part, :]
            continue
        found = jnp.zeros(out.shape, F32)
        for i in range(n_high):
            part = pl.ds(i * piece, piece)
            found = jnp.where(which == i, kept[part, :] + received[part, :], found)
        out[...] = found


def final_corange_body(counts, rows, *refs):
    out = refs[-1]
    first, used = 0, 0
    for count, piece in zip(counts, rows):
        terms = refs[used : used + count]
        parts = [term[pl.ds(i, piece), :] for term in terms for i in range(0, term.shape[0], piece)]
        out[pl.ds(first, piece), :] = functools.reduce(jnp.add, parts)
        first += piece
        used += count


def final_sketch_body(n_row, pieces, splits, *refs):
    out, done = refs[-2:]
    n, rows = sum(splits), refs[0].shape[1]
    parity = lax.rem(lax.axis_index("col"), 2)
    for side in range(2):
        parts = refs[side * n : (side + 1) * n]
        first = (parity if side == 0 else 1 - parity) * rows
        for b in range(rows // 128):
            lanes = pl.ds(b * 128, 128)
            found = []
            for r in range(n_row):
                place, used = owner_at(r, n_row), 0
                for piece, split in zip(pieces, splits):
                    per_part = n_row // split
                    part = parts[used + place // per_part]
                    found.append(part[pl.ds(place % per_part * piece, piece), lanes])
                    used += split
            block = jnp.concatenate(found, axis=0)
            out[pl.ds(pl.multiple_of(first + b * 128, 128), 128), :] = block.T
    done[...] = jnp.zeros_like(done)


def swap(x, axis, size, bit):
    return lax.ppermute(x, axis, [(i, i ^ bit) for i in range(size)])


def shards(n_row, n_col, delta, omega):
    rows, d = delta.shape
    k = omega.shape[1]
    half = rows // 2
    per_owner = k // n_row
    pieces = [per_owner * part // sum(EIGHTHS) for part in EIGHTHS] if per_owner % 8 == 0 else [1] * per_owner
    widths = [piece * n_row for piece in pieces]
    n = len(pieces)
    splits = SPLITS if len(SPLITS) == n else (2,) * n
    bits = [1 << i for i in range(n_row.bit_length() - 1)]

    in_hbm = pltpu.with_memory_space_constraint(delta, pltpu.HBM)
    sems = pltpu.SemaphoreType.DMA((half // BLOCK,))
    held_other, omega_t, to_send = call(
        functools.partial(first_half_body, n_row, pieces),
        (in_hbm, pltpu.with_memory_space_constraint(omega, pltpu.HBM)),
        [((half, d), BF16), ((k, d), BF16), ((k, half), F32)],
        "aa",
        scratch=[pltpu.VMEM((d, k), BF16), sems, pltpu.SemaphoreType.DMA],
    )
    received = swap(to_send, "col", n_col, 1)
    held_own, kept = call(second_half_body, (in_hbm, omega_t), [((half, d), BF16), ((k, half), F32)], "av", scratch=[sems])
    partial = call(add_chunks_body, (kept, received), [((width, half), F32) for width in widths])
    bit = 2
    while bit < n_col // 2:
        moved = [swap(x, "col", n_col, bit) for x in partial]
        partial = [call(add_body, pair, [(pair[0].shape, F32)])[0] for pair in zip(partial, moved)]
        bit *= 2
    moved = [swap(x, "col", n_col, bit) for x in partial]

    owns, others, befores, pending = {}, {}, {}, {}
    sketch = None
    last = ()
    planned = len(bits) == 3 and n == sum(len(group) for group in GROUPS)
    groups = GROUPS if planned else tuple((c,) for c in range(n))
    modes = MODES if planned else ("pairs",) * n
    steps = ORDER if planned else ()
    if not steps:
        found = []
        for c in range(n):
            found += [(10 * c, f"own{c}"), (10 * c + 1, f"before{c}"), (10 * c + 2, f"send{c}")]
        for g, group in enumerate(groups):
            stages = 2 if modes[g] == "direct" else len(bits)
            found += [(10 * group[-1] + 9.5 + 10 * s, f"add{g}.{s}") for s in range(1, stages)]
        steps = [step for _, step in sorted(found)] + ["sketch"]
    for step in steps:
        weight = WEIGHTS.get(step, 0)
        if step.startswith("own"):
            c = int(step[3:])
            outs = [((widths[c] // splits[c], half), F32)] * splits[c]
            owns[c] = call(add_body, (partial[c], moved[c]), outs, after=last, weight=weight)
            others[c] = [swap(x, "col", n_col, 1) for x in owns[c]]
            last = (owns[c][0],)
        elif step.startswith("before"):
            c = int(step[6:])
            befores[c] = call(product_body, (*owns[c], held_own), [((widths[c], d), F32)], after=last, weight=weight)[0]
            last = (befores[c],)
        elif step.startswith("send"):
            c = int(step[4:])
            outs = [((widths[c] // 2, d), F32)] * 2
            total = pltpu.VMEM((widths[c], d), F32)
            args = (*others[c], held_other, befores[c])
            send, keep = call(product_send_body, args, outs, after=last, scratch=[total], weight=weight)
            pending[(c,)] = keep, swap(send, "row", n_row, bits[0])
            last = (keep,)
        elif step.startswith("add"):
            g, s = (int(x) for x in step[3:].split("."))
            group = groups[g]
            if modes[g] == "direct":
                outs = [((pieces[group[0]], d), F32)] * (n_row // 2)
                body = functools.partial(add_spread_body, n_row // 2)
                own, *sends = call(body, pending[group], outs, after=last, weight=weight)
                flips = [2 * owner_at(flip, n_row // 2) for flip in range(1, n_row // 2)]
                pending[group] = own, *[swap(x, "row", n_row, flip) for x, flip in zip(sends, flips)]
                last = (own,)
                continue
            if s == 1:
                pending[group] = [x for c in group for x in pending[(c,)]]
            segments = [widths[c] >> s for c in group]
            body = functools.partial(add_send_body, bits[s], segments)
            outs = [((sum(segments) // 2, d), F32)] * 2
            send, keep = call(body, pending[group], outs, after=last, weight=weight)
            pending[group] = keep, swap(send, "row", n_row, bits[s])
            last = (keep,)
        else:
            parts = [[x for found in halves.values() for x in found] for halves in (owns, others)]
            sketch, done = finish_sketch(n_row, k, pieces, splits, *parts, last)
            last = (done,)
    flat = [x for group in groups for x in pending[group]]
    if per_owner % 8 == 0:
        body = functools.partial(final_corange_body, [len(pending[group]) for group in groups], [sum(pieces[c] for c in group) for group in groups])
        corange = call(body, flat, [((per_owner, d), F32)], after=last, results=1, weight=WEIGHTS.get("F", 0))[0]
    else:
        corange = jnp.concatenate([functools.reduce(jnp.add, pending[group]) for group in groups], axis=0)
    return sketch, corange.T


def finish_sketch(n_row, k, pieces, splits, owns, others, after):
    half = owns[0].shape[1]
    if k // n_row % 8 == 0:
        body = functools.partial(final_sketch_body, n_row, pieces, splits)
        return call(body, (*owns, *others), [((2 * half, k), F32), ((8, 128), F32)], after=after, results=1)
    places = jnp.array([owner_at(r, n_row) for r in range(n_row)])

    def columns(parts):
        starts = [sum(splits[:c]) for c in range(len(splits))]
        parts = [jnp.concatenate(parts[start : start + split], axis=0) for start, split in zip(starts, splits)]
        found = [part.reshape(n_row, piece, half)[places] for part, piece in zip(parts, pieces)]
        return jnp.concatenate(found, axis=1).reshape(k, half).T

    own, other = columns(owns), columns(others)
    first = lax.rem(lax.axis_index("col"), 2) == 0
    return jnp.where(first, jnp.concatenate([own, other]), jnp.concatenate([other, own])), after[0]


def solution(mesh):
    body = functools.partial(shards, mesh.shape["row"], mesh.shape["col"])
    in_specs = (P("row", "col"), P("col", None))
    out_specs = (P("row", None), P("col", "row"))
    return jax.shard_map(body, mesh=mesh, in_specs=in_specs, out_specs=out_specs, check_vma=False)
```

```python
import functools

import jax
import jax.numpy as jnp
from jax import lax
from jax.experimental import pallas as pl
from jax.experimental.pallas import tpu as pltpu
from jax.sharding import PartitionSpec as P

EIGHTHS = (2,2,2,2)
BLOCK = 512
F32 = jnp.float32
BF16 = jnp.bfloat16
NT = (((1,), (1,)), ((), ()))
SPECS = {"v": pl.BlockSpec(memory_space=pltpu.VMEM), "a": pl.BlockSpec(memory_space=pl.ANY)}
ORDER = ('own0', 'before0', 'send0', 'own1', 'before1', 'send1', 'add0.1', 'own2', 'before2', 'send2', 'add1.1', 'own3', 'before3', 'send3', 'add2.1', 'add1.2', 'add0.2', 'add2.2', 'add3.1', 'sketch')
WEIGHTS = {'add2.1': 500000000, 'F': 500000000, 'send1': 0, 'send0': 0, 'send3': 0, 'add2.2': 200000000, 'add0.2': 1000000000, 'own2': 500000000, 'before1': 500000000, 'add0.1': 500000000, 'before3': 2000000000, 'sketch': 500000000, 'send2': 0, 'add1.2': 200000000}
SPLITS = (2,2,2,2)
GROUPS = ((0,),(1,),(2,),(3,))
MODES = ('pairs','pairs','pairs','direct')


def call(body, args, outs, kinds=None, after=(), scratch=(), results=0, weight=0):
    n = len(args)
    kinds = (kinds or "v" * n) + "a" * len(after)

    def run(*refs):
        body(*refs[:n], *refs[len(kinds) :])

    return pl.pallas_call(
        run,
        out_shape=[pltpu.VMEM(*o) if i >= results else jax.ShapeDtypeStruct(*o) for i, o in enumerate(outs)],
        in_specs=[SPECS[kind] for kind in kinds],
        out_specs=[SPECS["v"]] * len(outs),
        scratch_shapes=list(scratch),
        cost_estimate=pl.CostEstimate(flops=weight, bytes_accessed=0, transcendentals=0),
        compiler_params=pltpu.CompilerParams(vmem_limit_bytes=16 << 20),
    )(*args, *after)


def owner_at(index, n_row):
    owner, bit = index * 0, 1
    while bit < n_row:
        owner = 2 * owner + index % 2
        index = index // 2
        bit *= 2
    return owner


def column_of(position, k, n_row, pieces):
    column, first, done = position * 0, 0, 0
    for piece in pieces:
        rest = position - first
        found = owner_at(rest // piece, n_row) * (k // n_row) + done + rest % piece
        column = jnp.where((rest >= 0) & (rest < piece * n_row), found, column)
        first += piece * n_row
        done += piece
    return column


def stream_half(delta, held, sem, mine):
    rows = held.shape[0]
    parity = lax.rem(lax.axis_index("col"), 2)
    first = (parity if mine else 1 - parity) * rows
    copies = []
    for b in range(rows // BLOCK):
        source = delta.at[pl.ds(pl.multiple_of(first + b * BLOCK, BLOCK), BLOCK), :]
        copies.append(pltpu.make_async_copy(source, held.at[pl.ds(b * BLOCK, BLOCK), :], sem.at[b]))
        copies[-1].start()
    return copies


def sketch_half(omega_t, held, copies, out):
    for b, copy in enumerate(copies):
        copy.wait()
        block = pl.ds(b * BLOCK, BLOCK)
        out[:, block] = lax.dot_general(omega_t[...], held[block, :], NT, preferred_element_type=F32)


def first_half_body(n_row, pieces, delta, omega, held, omega_t, out, omega_v, sem, omega_sem):
    k = out.shape[0]
    fetch = pltpu.make_async_copy(omega, omega_v, omega_sem)
    fetch.start()
    copies = stream_half(delta, held, sem, False)
    position = lax.broadcasted_iota(jnp.int32, (k, k), 0)
    column = lax.broadcasted_iota(jnp.int32, (k, k), 1)
    pick = jnp.where(column_of(position, k, n_row, pieces) == column, 1.0, 0.0).astype(BF16)
    fetch.wait()
    omega_t[...] = lax.dot_general(pick, omega_v[...], NT, preferred_element_type=F32).astype(BF16)
    sketch_half(omega_t, held, copies, out)


def second_half_body(delta, omega_t, held, out, sem):
    sketch_half(omega_t, held, stream_half(delta, held, sem, True), out)


def add_chunks_body(kept, received, *outs):
    first = 0
    for out in outs:
        part = pl.ds(first, out.shape[0])
        out[...] = kept[part, :] + received[part, :]
        first += out.shape[0]


def add_body(a, b, *outs):
    first = 0
    for out in outs:
        part = pl.ds(first, out.shape[0])
        out[...] = a[part, :] + b[part, :]
        first += out.shape[0]


def joined(refs):
    return jnp.concatenate([ref[...] for ref in refs], axis=0)


def product_body(*refs):
    *sketch, held, out = refs
    out[...] = jnp.dot(joined(sketch).astype(BF16), held[...], preferred_element_type=F32)


def split(bit, segments, refs, send, keep):
    own = lax.rem(lax.axis_index("row") // bit, 2)
    start, first = 0, 0
    for rows in segments:
        half = rows // 2
        for out, which in ((send, 1 - own), (keep, own)):
            if half % 8:
                low, high = (
                    functools.reduce(jnp.add, [ref[pl.ds(start + i * half, half), :] for ref in refs]) for i in range(2)
                )
                value = jnp.where(which == 0, low, high)
            else:
                part = pl.ds(pl.multiple_of(start + which * half, 8), half)
                value = functools.reduce(jnp.add, [ref[part, :] for ref in refs])
            out[pl.ds(first, half), :] = value
        start += rows
        first += half


def product_send_body(*refs):
    *sketch, held, before, send, keep, total = refs
    total[...] = before[...] + jnp.dot(joined(sketch).astype(BF16), held[...], preferred_element_type=F32)
    split(1, [total.shape[0]], [total], send, keep)


def add_send_body(bit, segments, *refs):
    *pairs, send, keep = refs
    first = 0
    for kept, got in zip(pairs[::2], pairs[1::2]):
        mine = segments if len(pairs) == 2 else [kept.shape[0]]
        half = kept.shape[0] // 2
        part = pl.ds(first, half)
        split(bit, mine, [kept, got], send.at[part, :], keep.at[part, :])
        first += half


def add_spread_body(n_high, kept, received, *outs):
    piece = outs[0].shape[0]
    place = owner_at(lax.axis_index("row") // 2, n_high)
    for flip, out in enumerate(outs):
        which = lax.bitwise_xor(place, flip)
        if piece % 8 == 0:
            part = pl.ds(pl.multiple_of(which * piece, piece), piece)
            out[...] = kept[part, :] + received[part, :]
            continue
        found = jnp.zeros(out.shape, F32)
        for i in range(n_high):
            part = pl.ds(i * piece, piece)
            found = jnp.where(which == i, kept[part, :] + received[part, :], found)
        out[...] = found


def final_corange_body(counts, rows, *refs):
    out = refs[-1]
    first, used = 0, 0
    for count, piece in zip(counts, rows):
        terms = refs[used : used + count]
        parts = [term[pl.ds(i, piece), :] for term in terms for i in range(0, term.shape[0], piece)]
        out[pl.ds(first, piece), :] = functools.reduce(jnp.add, parts)
        first += piece
        used += count


def final_sketch_body(n_row, pieces, splits, *refs):
    out, done = refs[-2:]
    n, rows = sum(splits), refs[0].shape[1]
    parity = lax.rem(lax.axis_index("col"), 2)
    for side in range(2):
        parts = refs[side * n : (side + 1) * n]
        first = (parity if side == 0 else 1 - parity) * rows
        for b in range(rows // 128):
            lanes = pl.ds(b * 128, 128)
            found = []
            for r in range(n_row):
                place, used = owner_at(r, n_row), 0
                for piece, split in zip(pieces, splits):
                    per_part = n_row // split
                    part = parts[used + place // per_part]
                    found.append(part[pl.ds(place % per_part * piece, piece), lanes])
                    used += split
            block = jnp.concatenate(found, axis=0)
            out[pl.ds(pl.multiple_of(first + b * 128, 128), 128), :] = block.T
    done[...] = jnp.zeros_like(done)


def swap(x, axis, size, bit):
    return lax.ppermute(x, axis, [(i, i ^ bit) for i in range(size)])


def shards(n_row, n_col, delta, omega):
    rows, d = delta.shape
    k = omega.shape[1]
    half = rows // 2
    per_owner = k // n_row
    pieces = [per_owner * part // sum(EIGHTHS) for part in EIGHTHS] if per_owner % 8 == 0 else [1] * per_owner
    widths = [piece * n_row for piece in pieces]
    n = len(pieces)
    splits = SPLITS if len(SPLITS) == n else (2,) * n
    bits = [1 << i for i in range(n_row.bit_length() - 1)]

    in_hbm = pltpu.with_memory_space_constraint(delta, pltpu.HBM)
    sems = pltpu.SemaphoreType.DMA((half // BLOCK,))
    held_other, omega_t, to_send = call(
        functools.partial(first_half_body, n_row, pieces),
        (in_hbm, pltpu.with_memory_space_constraint(omega, pltpu.HBM)),
        [((half, d), BF16), ((k, d), BF16), ((k, half), F32)],
        "aa",
        scratch=[pltpu.VMEM((d, k), BF16), sems, pltpu.SemaphoreType.DMA],
    )
    received = swap(to_send, "col", n_col, 1)
    held_own, kept = call(second_half_body, (in_hbm, omega_t), [((half, d), BF16), ((k, half), F32)], "av", scratch=[sems])
    partial = call(add_chunks_body, (kept, received), [((width, half), F32) for width in widths])
    bit = 2
    while bit < n_col // 2:
        moved = [swap(x, "col", n_col, bit) for x in partial]
        partial = [call(add_body, pair, [(pair[0].shape, F32)])[0] for pair in zip(partial, moved)]
        bit *= 2
    moved = [swap(x, "col", n_col, bit) for x in partial]

    owns, others, befores, pending = {}, {}, {}, {}
    sketch = None
    last = ()
    planned = len(bits) == 3 and n == sum(len(group) for group in GROUPS)
    groups = GROUPS if planned else tuple((c,) for c in range(n))
    modes = MODES if planned else ("pairs",) * n
    steps = ORDER if planned else ()
    if not steps:
        found = []
        for c in range(n):
            found += [(10 * c, f"own{c}"), (10 * c + 1, f"before{c}"), (10 * c + 2, f"send{c}")]
        for g, group in enumerate(groups):
            stages = 2 if modes[g] == "direct" else len(bits)
            found += [(10 * group[-1] + 9.5 + 10 * s, f"add{g}.{s}") for s in range(1, stages)]
        steps = [step for _, step in sorted(found)] + ["sketch"]
    for step in steps:
        weight = WEIGHTS.get(step, 0)
        if step.startswith("own"):
            c = int(step[3:])
            outs = [((widths[c] // splits[c], half), F32)] * splits[c]
            owns[c] = call(add_body, (partial[c], moved[c]), outs, after=last, weight=weight)
            others[c] = [swap(x, "col", n_col, 1) for x in owns[c]]
            last = (owns[c][0],)
        elif step.startswith("before"):
            c = int(step[6:])
            befores[c] = call(product_body, (*owns[c], held_own), [((widths[c], d), F32)], after=last, weight=weight)[0]
            last = (befores[c],)
        elif step.startswith("send"):
            c = int(step[4:])
            outs = [((widths[c] // 2, d), F32)] * 2
            total = pltpu.VMEM((widths[c], d), F32)
            args = (*others[c], held_other, befores[c])
            send, keep = call(product_send_body, args, outs, after=last, scratch=[total], weight=weight)
            pending[(c,)] = keep, swap(send, "row", n_row, bits[0])
            last = (keep,)
        elif step.startswith("add"):
            g, s = (int(x) for x in step[3:].split("."))
            group = groups[g]
            if modes[g] == "direct":
                outs = [((pieces[group[0]], d), F32)] * (n_row // 2)
                body = functools.partial(add_spread_body, n_row // 2)
                own, *sends = call(body, pending[group], outs, after=last, weight=weight)
                flips = [2 * owner_at(flip, n_row // 2) for flip in range(1, n_row // 2)]
                pending[group] = own, *[swap(x, "row", n_row, flip) for x, flip in zip(sends, flips)]
                last = (own,)
                continue
            if s == 1:
                pending[group] = [x for c in group for x in pending[(c,)]]
            segments = [widths[c] >> s for c in group]
            body = functools.partial(add_send_body, bits[s], segments)
            outs = [((sum(segments) // 2, d), F32)] * 2
            send, keep = call(body, pending[group], outs, after=last, weight=weight)
            pending[group] = keep, swap(send, "row", n_row, bits[s])
            last = (keep,)
        else:
            parts = [[x for found in halves.values() for x in found] for halves in (owns, others)]
            sketch, done = finish_sketch(n_row, k, pieces, splits, *parts, last)
            last = (done,)
    flat = [x for group in groups for x in pending[group]]
    if per_owner % 8 == 0:
        body = functools.partial(final_corange_body, [len(pending[group]) for group in groups], [sum(pieces[c] for c in group) for group in groups])
        corange = call(body, flat, [((per_owner, d), F32)], after=last, results=1, weight=WEIGHTS.get("F", 0))[0]
    else:
        corange = jnp.concatenate([functools.reduce(jnp.add, pending[group]) for group in groups], axis=0)
    return sketch, corange.T


def finish_sketch(n_row, k, pieces, splits, owns, others, after):
    half = owns[0].shape[1]
    if k // n_row % 8 == 0:
        body = functools.partial(final_sketch_body, n_row, pieces, splits)
        return call(body, (*owns, *others), [((2 * half, k), F32), ((8, 128), F32)], after=after, results=1)
    places = jnp.array([owner_at(r, n_row) for r in range(n_row)])

    def columns(parts):
        starts = [sum(splits[:c]) for c in range(len(splits))]
        parts = [jnp.concatenate(parts[start : start + split], axis=0) for start, split in zip(starts, splits)]
        found = [part.reshape(n_row, piece, half)[places] for part, piece in zip(parts, pieces)]
        return jnp.concatenate(found, axis=1).reshape(k, half).T

    own, other = columns(owns), columns(others)
    first = lax.rem(lax.axis_index("col"), 2) == 0
    return jnp.where(first, jnp.concatenate([own, other]), jnp.concatenate([other, own])), after[0]


def solution(mesh):
    body = functools.partial(shards, mesh.shape["row"], mesh.shape["col"])
    in_specs = (P("row", "col"), P("col", None))
    out_specs = (P("row", None), P("col", "row"))
    return jax.shard_map(body, mesh=mesh, in_specs=in_specs, out_specs=out_specs, check_vma=False)
```

```python
import functools

import jax
import jax.numpy as jnp
from jax import lax
from jax.experimental import pallas as pl
from jax.experimental.pallas import tpu as pltpu
from jax.sharding import PartitionSpec as P

EIGHTHS = (2,2,2,2)
BLOCK = 512
FAR_FIRST = (0, 1)
F32 = jnp.float32
BF16 = jnp.bfloat16
NT = (((1,), (1,)), ((), ()))
SPECS = {"v": pl.BlockSpec(memory_space=pltpu.VMEM), "a": pl.BlockSpec(memory_space=pl.ANY)}
ORDER = ('own0', 'before0', 'send0', 'own1', 'before1', 'send1', 'add0.1', 'own2', 'before2', 'send2', 'add1.1', 'own3', 'before3', 'send3', 'add2.1', 'add1.2', 'add0.2', 'add2.2', 'add3.1', 'sketch')
WEIGHTS = {'add2.1': 500000000, 'F': 500000000, 'send1': 0, 'send0': 0, 'send3': 0, 'add2.2': 200000000, 'add0.2': 1000000000, 'own2': 500000000, 'before1': 500000000, 'add0.1': 500000000, 'before3': 2000000000, 'sketch': 500000000, 'send2': 0, 'add1.2': 200000000}
SPLITS = (2,2,2,2)
GROUPS = ((0,),(1,),(2,),(3,))
MODES = ('pairs','pairs','pairs','direct')


def call(body, args, outs, kinds=None, after=(), scratch=(), results=0, weight=0):
    n = len(args)
    kinds = (kinds or "v" * n) + "a" * len(after)

    def run(*refs):
        body(*refs[:n], *refs[len(kinds) :])

    return pl.pallas_call(
        run,
        out_shape=[pltpu.VMEM(*o) if i >= results else jax.ShapeDtypeStruct(*o) for i, o in enumerate(outs)],
        in_specs=[SPECS[kind] for kind in kinds],
        out_specs=[SPECS["v"]] * len(outs),
        scratch_shapes=list(scratch),
        cost_estimate=pl.CostEstimate(flops=weight, bytes_accessed=0, transcendentals=0),
        compiler_params=pltpu.CompilerParams(vmem_limit_bytes=16 << 20),
    )(*args, *after)


def owner_at(index, n_row):
    owner, bit = index * 0, 1
    while bit < n_row:
        owner = 2 * owner + index % 2
        index = index // 2
        bit *= 2
    return owner


def owner_of(place, order):
    return sum(place // (1 << (len(order) - 1 - i)) % 2 * bit for i, bit in enumerate(order))


def place_of(owner, order):
    return sum(owner // bit % 2 * (1 << (len(order) - 1 - i)) for i, bit in enumerate(order))


def column_of(position, k, n_row, pieces, orders):
    column, first, done = position * 0, 0, 0
    for piece, order in zip(pieces, orders):
        rest = position - first
        found = owner_of(rest // piece, order) * (k // n_row) + done + rest % piece
        column = jnp.where((rest >= 0) & (rest < piece * n_row), found, column)
        first += piece * n_row
        done += piece
    return column


def stream_half(delta, held, sem, mine):
    rows = held.shape[0]
    parity = lax.rem(lax.axis_index("col"), 2)
    first = (parity if mine else 1 - parity) * rows
    copies = []
    for b in range(rows // BLOCK):
        source = delta.at[pl.ds(pl.multiple_of(first + b * BLOCK, BLOCK), BLOCK), :]
        copies.append(pltpu.make_async_copy(source, held.at[pl.ds(b * BLOCK, BLOCK), :], sem.at[b]))
        copies[-1].start()
    return copies


def sketch_half(omega_t, held, copies, out):
    for b, copy in enumerate(copies):
        copy.wait()
        block = pl.ds(b * BLOCK, BLOCK)
        out[:, block] = lax.dot_general(omega_t[...], held[block, :], NT, preferred_element_type=F32)


def first_half_body(n_row, pieces, orders, delta, omega, held, omega_t, out, omega_v, sem, omega_sem):
    k = out.shape[0]
    fetch = pltpu.make_async_copy(omega, omega_v, omega_sem)
    fetch.start()
    copies = stream_half(delta, held, sem, False)
    position = lax.broadcasted_iota(jnp.int32, (k, k), 0)
    column = lax.broadcasted_iota(jnp.int32, (k, k), 1)
    pick = jnp.where(column_of(position, k, n_row, pieces, orders) == column, 1.0, 0.0).astype(BF16)
    fetch.wait()
    omega_t[...] = lax.dot_general(pick, omega_v[...], NT, preferred_element_type=F32).astype(BF16)
    sketch_half(omega_t, held, copies, out)


def second_half_body(delta, omega_t, held, out, sem):
    sketch_half(omega_t, held, stream_half(delta, held, sem, True), out)


def add_chunks_body(kept, received, *outs):
    first = 0
    for out in outs:
        part = pl.ds(first, out.shape[0])
        out[...] = kept[part, :] + received[part, :]
        first += out.shape[0]


def add_body(a, b, *outs):
    first = 0
    for out in outs:
        part = pl.ds(first, out.shape[0])
        out[...] = a[part, :] + b[part, :]
        first += out.shape[0]


def joined(refs):
    return jnp.concatenate([ref[...] for ref in refs], axis=0)


def product_body(*refs):
    *sketch, held, out = refs
    out[...] = jnp.dot(joined(sketch).astype(BF16), held[...], preferred_element_type=F32)


def split(bit, segments, refs, send, keep):
    own = lax.rem(lax.axis_index("row") // bit, 2)
    start, first = 0, 0
    for rows in segments:
        half = rows // 2
        for out, which in ((send, 1 - own), (keep, own)):
            if half % 8:
                low, high = (
                    functools.reduce(jnp.add, [ref[pl.ds(start + i * half, half), :] for ref in refs]) for i in range(2)
                )
                value = jnp.where(which == 0, low, high)
            else:
                part = pl.ds(pl.multiple_of(start + which * half, 8), half)
                value = functools.reduce(jnp.add, [ref[part, :] for ref in refs])
            out[pl.ds(first, half), :] = value
        start += rows
        first += half


def product_send_body(*refs):
    *sketch, held, before, send, keep, total = refs
    total[...] = before[...] + jnp.dot(joined(sketch).astype(BF16), held[...], preferred_element_type=F32)
    split(1, [total.shape[0]], [total], send, keep)


def add_send_body(bit, segments, *refs):
    *pairs, send, keep = refs
    first = 0
    for kept, got in zip(pairs[::2], pairs[1::2]):
        mine = segments if len(pairs) == 2 else [kept.shape[0]]
        half = kept.shape[0] // 2
        part = pl.ds(first, half)
        split(bit, mine, [kept, got], send.at[part, :], keep.at[part, :])
        first += half


def add_spread_body(n_high, kept, received, *outs):
    piece = outs[0].shape[0]
    place = owner_at(lax.axis_index("row") // 2, n_high)
    for flip, out in enumerate(outs):
        which = lax.bitwise_xor(place, flip)
        if piece % 8 == 0:
            part = pl.ds(pl.multiple_of(which * piece, piece), piece)
            out[...] = kept[part, :] + received[part, :]
            continue
        found = jnp.zeros(out.shape, F32)
        for i in range(n_high):
            part = pl.ds(i * piece, piece)
            found = jnp.where(which == i, kept[part, :] + received[part, :], found)
        out[...] = found


def final_corange_body(counts, rows, *refs):
    out = refs[-1]
    first, used = 0, 0
    for count, piece in zip(counts, rows):
        terms = refs[used : used + count]
        parts = [term[pl.ds(i, piece), :] for term in terms for i in range(0, term.shape[0], piece)]
        out[pl.ds(first, piece), :] = functools.reduce(jnp.add, parts)
        first += piece
        used += count


def final_sketch_body(n_row, pieces, splits, orders, *refs):
    out, done = refs[-2:]
    n, rows = sum(splits), refs[0].shape[1]
    parity = lax.rem(lax.axis_index("col"), 2)
    for side in range(2):
        parts = refs[side * n : (side + 1) * n]
        first = (parity if side == 0 else 1 - parity) * rows
        for b in range(rows // 128):
            lanes = pl.ds(b * 128, 128)
            found = []
            for r in range(n_row):
                used = 0
                for piece, split, order in zip(pieces, splits, orders):
                    place = place_of(r, order)
                    per_part = n_row // split
                    part = parts[used + place // per_part]
                    found.append(part[pl.ds(place % per_part * piece, piece), lanes])
                    used += split
            block = jnp.concatenate(found, axis=0)
            out[pl.ds(pl.multiple_of(first + b * 128, 128), 128), :] = block.T
    done[...] = jnp.zeros_like(done)


def swap(x, axis, size, bit):
    return lax.ppermute(x, axis, [(i, i ^ bit) for i in range(size)])


def shards(n_row, n_col, delta, omega):
    rows, d = delta.shape
    k = omega.shape[1]
    half = rows // 2
    per_owner = k // n_row
    pieces = [per_owner * part // sum(EIGHTHS) for part in EIGHTHS] if per_owner % 8 == 0 else [1] * per_owner
    widths = [piece * n_row for piece in pieces]
    n = len(pieces)
    splits = SPLITS if len(SPLITS) == n else (2,) * n
    bits = [1 << i for i in range(n_row.bit_length() - 1)]
    orders = [[1, 4, 2] if n == 4 and len(bits) == 3 and c in FAR_FIRST else bits for c in range(n)]

    in_hbm = pltpu.with_memory_space_constraint(delta, pltpu.HBM)
    sems = pltpu.SemaphoreType.DMA((half // BLOCK,))
    held_other, omega_t, to_send = call(
        functools.partial(first_half_body, n_row, pieces, orders),
        (in_hbm, pltpu.with_memory_space_constraint(omega, pltpu.HBM)),
        [((half, d), BF16), ((k, d), BF16), ((k, half), F32)],
        "aa",
        scratch=[pltpu.VMEM((d, k), BF16), sems, pltpu.SemaphoreType.DMA],
    )
    received = swap(to_send, "col", n_col, 1)
    held_own, kept = call(second_half_body, (in_hbm, omega_t), [((half, d), BF16), ((k, half), F32)], "av", scratch=[sems])
    partial = call(add_chunks_body, (kept, received), [((width, half), F32) for width in widths])
    bit = 2
    while bit < n_col // 2:
        moved = [swap(x, "col", n_col, bit) for x in partial]
        partial = [call(add_body, pair, [(pair[0].shape, F32)])[0] for pair in zip(partial, moved)]
        bit *= 2
    moved = [swap(x, "col", n_col, bit) for x in partial]

    owns, others, befores, pending = {}, {}, {}, {}
    sketch = None
    last = ()
    planned = len(bits) == 3 and n == sum(len(group) for group in GROUPS)
    groups = GROUPS if planned else tuple((c,) for c in range(n))
    modes = MODES if planned else ("pairs",) * n
    steps = ORDER if planned else ()
    if not steps:
        found = []
        for c in range(n):
            found += [(10 * c, f"own{c}"), (10 * c + 1, f"before{c}"), (10 * c + 2, f"send{c}")]
        for g, group in enumerate(groups):
            stages = 2 if modes[g] == "direct" else len(bits)
            found += [(10 * group[-1] + 9.5 + 10 * s, f"add{g}.{s}") for s in range(1, stages)]
        steps = [step for _, step in sorted(found)] + ["sketch"]
    for step in steps:
        weight = WEIGHTS.get(step, 0)
        if step.startswith("own"):
            c = int(step[3:])
            outs = [((widths[c] // splits[c], half), F32)] * splits[c]
            owns[c] = call(add_body, (partial[c], moved[c]), outs, after=last, weight=weight)
            others[c] = [swap(x, "col", n_col, 1) for x in owns[c]]
            last = (owns[c][0],)
        elif step.startswith("before"):
            c = int(step[6:])
            befores[c] = call(product_body, (*owns[c], held_own), [((widths[c], d), F32)], after=last, weight=weight)[0]
            last = (befores[c],)
        elif step.startswith("send"):
            c = int(step[4:])
            outs = [((widths[c] // 2, d), F32)] * 2
            total = pltpu.VMEM((widths[c], d), F32)
            args = (*others[c], held_other, befores[c])
            send, keep = call(product_send_body, args, outs, after=last, scratch=[total], weight=weight)
            pending[(c,)] = keep, swap(send, "row", n_row, bits[0])
            last = (keep,)
        elif step.startswith("add"):
            g, s = (int(x) for x in step[3:].split("."))
            group = groups[g]
            if modes[g] == "direct":
                outs = [((pieces[group[0]], d), F32)] * (n_row // 2)
                body = functools.partial(add_spread_body, n_row // 2)
                own, *sends = call(body, pending[group], outs, after=last, weight=weight)
                flips = [2 * owner_at(flip, n_row // 2) for flip in range(1, n_row // 2)]
                pending[group] = own, *[swap(x, "row", n_row, flip) for x, flip in zip(sends, flips)]
                last = (own,)
                continue
            if s == 1:
                pending[group] = [x for c in group for x in pending[(c,)]]
            segments = [widths[c] >> s for c in group]
            bit = orders[group[0]][s]
            body = functools.partial(add_send_body, bit, segments)
            outs = [((sum(segments) // 2, d), F32)] * 2
            send, keep = call(body, pending[group], outs, after=last, weight=weight)
            pending[group] = keep, swap(send, "row", n_row, bit)
            last = (keep,)
        else:
            parts = [[x for found in halves.values() for x in found] for halves in (owns, others)]
            sketch, done = finish_sketch(n_row, k, pieces, splits, orders, *parts, last)
            last = (done,)
    flat = [x for group in groups for x in pending[group]]
    if per_owner % 8 == 0:
        body = functools.partial(final_corange_body, [len(pending[group]) for group in groups], [sum(pieces[c] for c in group) for group in groups])
        corange = call(body, flat, [((per_owner, d), F32)], after=last, results=1, weight=WEIGHTS.get("F", 0))[0]
    else:
        corange = jnp.concatenate([functools.reduce(jnp.add, pending[group]) for group in groups], axis=0)
    return sketch, corange.T


def finish_sketch(n_row, k, pieces, splits, orders, owns, others, after):
    half = owns[0].shape[1]
    if k // n_row % 8 == 0:
        body = functools.partial(final_sketch_body, n_row, pieces, splits, orders)
        return call(body, (*owns, *others), [((2 * half, k), F32), ((8, 128), F32)], after=after, results=1)
    places = jnp.array([place_of(r, orders[0]) for r in range(n_row)])

    def columns(parts):
        starts = [sum(splits[:c]) for c in range(len(splits))]
        parts = [jnp.concatenate(parts[start : start + split], axis=0) for start, split in zip(starts, splits)]
        found = [part.reshape(n_row, piece, half)[places] for part, piece in zip(parts, pieces)]
        return jnp.concatenate(found, axis=1).reshape(k, half).T

    own, other = columns(owns), columns(others)
    first = lax.rem(lax.axis_index("col"), 2) == 0
    return jnp.where(first, jnp.concatenate([own, other]), jnp.concatenate([other, own])), after[0]


def solution(mesh):
    body = functools.partial(shards, mesh.shape["row"], mesh.shape["col"])
    in_specs = (P("row", "col"), P("col", None))
    out_specs = (P("row", None), P("col", "row"))
    return jax.shard_map(body, mesh=mesh, in_specs=in_specs, out_specs=out_specs, check_vma=False)
```

```python
import functools

import jax
import jax.numpy as jnp
from jax import lax
from jax.experimental import pallas as pl
from jax.experimental.pallas import tpu as pltpu
from jax.sharding import PartitionSpec as P

EIGHTHS = (2,2,2,2)
BLOCK = 512
FAR_FIRST = (1,)
F32 = jnp.float32
BF16 = jnp.bfloat16
NT = (((1,), (1,)), ((), ()))
SPECS = {"v": pl.BlockSpec(memory_space=pltpu.VMEM), "a": pl.BlockSpec(memory_space=pl.ANY)}
ORDER = ('own0', 'before0', 'send0', 'own1', 'before1', 'send1', 'add0.1', 'own2', 'before2', 'send2', 'add1.1', 'own3', 'before3', 'send3', 'add2.1', 'add1.2', 'add0.2', 'add2.2', 'add3.1', 'sketch')
WEIGHTS = {'add2.1': 500000000, 'F': 500000000, 'send1': 0, 'send0': 0, 'send3': 0, 'add2.2': 200000000, 'add0.2': 1000000000, 'own2': 500000000, 'before1': 500000000, 'add0.1': 500000000, 'before3': 2000000000, 'sketch': 500000000, 'send2': 0, 'add1.2': 200000000}
SPLITS = (2,2,2,2)
GROUPS = ((0,),(1,),(2,),(3,))
MODES = ('pairs','pairs','pairs','direct')


def call(body, args, outs, kinds=None, after=(), scratch=(), results=0, weight=0):
    n = len(args)
    kinds = (kinds or "v" * n) + "a" * len(after)

    def run(*refs):
        body(*refs[:n], *refs[len(kinds) :])

    return pl.pallas_call(
        run,
        out_shape=[pltpu.VMEM(*o) if i >= results else jax.ShapeDtypeStruct(*o) for i, o in enumerate(outs)],
        in_specs=[SPECS[kind] for kind in kinds],
        out_specs=[SPECS["v"]] * len(outs),
        scratch_shapes=list(scratch),
        cost_estimate=pl.CostEstimate(flops=weight, bytes_accessed=0, transcendentals=0),
        compiler_params=pltpu.CompilerParams(vmem_limit_bytes=16 << 20),
    )(*args, *after)


def owner_at(index, n_row):
    owner, bit = index * 0, 1
    while bit < n_row:
        owner = 2 * owner + index % 2
        index = index // 2
        bit *= 2
    return owner


def owner_of(place, order):
    return sum(place // (1 << (len(order) - 1 - i)) % 2 * bit for i, bit in enumerate(order))


def place_of(owner, order):
    return sum(owner // bit % 2 * (1 << (len(order) - 1 - i)) for i, bit in enumerate(order))


def column_of(position, k, n_row, pieces, orders):
    column, first, done = position * 0, 0, 0
    for piece, order in zip(pieces, orders):
        rest = position - first
        found = owner_of(rest // piece, order) * (k // n_row) + done + rest % piece
        column = jnp.where((rest >= 0) & (rest < piece * n_row), found, column)
        first += piece * n_row
        done += piece
    return column


def stream_half(delta, held, sem, mine):
    rows = held.shape[0]
    parity = lax.rem(lax.axis_index("col"), 2)
    first = (parity if mine else 1 - parity) * rows
    copies = []
    for b in range(rows // BLOCK):
        source = delta.at[pl.ds(pl.multiple_of(first + b * BLOCK, BLOCK), BLOCK), :]
        copies.append(pltpu.make_async_copy(source, held.at[pl.ds(b * BLOCK, BLOCK), :], sem.at[b]))
        copies[-1].start()
    return copies


def sketch_half(omega_t, held, copies, out):
    for b, copy in enumerate(copies):
        copy.wait()
        block = pl.ds(b * BLOCK, BLOCK)
        out[:, block] = lax.dot_general(omega_t[...], held[block, :], NT, preferred_element_type=F32)


def first_half_body(n_row, pieces, orders, delta, omega, held, omega_t, out, omega_v, sem, omega_sem):
    k = out.shape[0]
    fetch = pltpu.make_async_copy(omega, omega_v, omega_sem)
    fetch.start()
    copies = stream_half(delta, held, sem, False)
    position = lax.broadcasted_iota(jnp.int32, (k, k), 0)
    column = lax.broadcasted_iota(jnp.int32, (k, k), 1)
    pick = jnp.where(column_of(position, k, n_row, pieces, orders) == column, 1.0, 0.0).astype(BF16)
    fetch.wait()
    omega_t[...] = lax.dot_general(pick, omega_v[...], NT, preferred_element_type=F32).astype(BF16)
    sketch_half(omega_t, held, copies, out)


def second_half_body(delta, omega_t, held, out, sem):
    sketch_half(omega_t, held, stream_half(delta, held, sem, True), out)


def add_chunks_body(kept, received, *outs):
    first = 0
    for out in outs:
        part = pl.ds(first, out.shape[0])
        out[...] = kept[part, :] + received[part, :]
        first += out.shape[0]


def add_body(a, b, *outs):
    first = 0
    for out in outs:
        part = pl.ds(first, out.shape[0])
        out[...] = a[part, :] + b[part, :]
        first += out.shape[0]


def joined(refs):
    return jnp.concatenate([ref[...] for ref in refs], axis=0)


def product_body(*refs):
    *sketch, held, out = refs
    out[...] = jnp.dot(joined(sketch).astype(BF16), held[...], preferred_element_type=F32)


def split(bit, segments, refs, send, keep):
    own = lax.rem(lax.axis_index("row") // bit, 2)
    start, first = 0, 0
    for rows in segments:
        half = rows // 2
        for out, which in ((send, 1 - own), (keep, own)):
            if half % 8:
                low, high = (
                    functools.reduce(jnp.add, [ref[pl.ds(start + i * half, half), :] for ref in refs]) for i in range(2)
                )
                value = jnp.where(which == 0, low, high)
            else:
                part = pl.ds(pl.multiple_of(start + which * half, 8), half)
                value = functools.reduce(jnp.add, [ref[part, :] for ref in refs])
            out[pl.ds(first, half), :] = value
        start += rows
        first += half


def product_send_body(*refs):
    *sketch, held, before, send, keep, total = refs
    total[...] = before[...] + jnp.dot(joined(sketch).astype(BF16), held[...], preferred_element_type=F32)
    split(1, [total.shape[0]], [total], send, keep)


def add_send_body(bit, segments, *refs):
    *pairs, send, keep = refs
    first = 0
    for kept, got in zip(pairs[::2], pairs[1::2]):
        mine = segments if len(pairs) == 2 else [kept.shape[0]]
        half = kept.shape[0] // 2
        part = pl.ds(first, half)
        split(bit, mine, [kept, got], send.at[part, :], keep.at[part, :])
        first += half


def add_spread_body(n_high, kept, received, *outs):
    piece = outs[0].shape[0]
    place = owner_at(lax.axis_index("row") // 2, n_high)
    for flip, out in enumerate(outs):
        which = lax.bitwise_xor(place, flip)
        if piece % 8 == 0:
            part = pl.ds(pl.multiple_of(which * piece, piece), piece)
            out[...] = kept[part, :] + received[part, :]
            continue
        found = jnp.zeros(out.shape, F32)
        for i in range(n_high):
            part = pl.ds(i * piece, piece)
            found = jnp.where(which == i, kept[part, :] + received[part, :], found)
        out[...] = found


def final_corange_body(counts, rows, *refs):
    out = refs[-1]
    first, used = 0, 0
    for count, piece in zip(counts, rows):
        terms = refs[used : used + count]
        parts = [term[pl.ds(i, piece), :] for term in terms for i in range(0, term.shape[0], piece)]
        out[pl.ds(first, piece), :] = functools.reduce(jnp.add, parts)
        first += piece
        used += count


def final_sketch_body(n_row, pieces, splits, orders, *refs):
    out, done = refs[-2:]
    n, rows = sum(splits), refs[0].shape[1]
    parity = lax.rem(lax.axis_index("col"), 2)
    for side in range(2):
        parts = refs[side * n : (side + 1) * n]
        first = (parity if side == 0 else 1 - parity) * rows
        for b in range(rows // 128):
            lanes = pl.ds(b * 128, 128)
            found = []
            for r in range(n_row):
                used = 0
                for piece, split, order in zip(pieces, splits, orders):
                    place = place_of(r, order)
                    per_part = n_row // split
                    part = parts[used + place // per_part]
                    found.append(part[pl.ds(place % per_part * piece, piece), lanes])
                    used += split
            block = jnp.concatenate(found, axis=0)
            out[pl.ds(pl.multiple_of(first + b * 128, 128), 128), :] = block.T
    done[...] = jnp.zeros_like(done)


def swap(x, axis, size, bit):
    return lax.ppermute(x, axis, [(i, i ^ bit) for i in range(size)])


def shards(n_row, n_col, delta, omega):
    rows, d = delta.shape
    k = omega.shape[1]
    half = rows // 2
    per_owner = k // n_row
    pieces = [per_owner * part // sum(EIGHTHS) for part in EIGHTHS] if per_owner % 8 == 0 else [1] * per_owner
    widths = [piece * n_row for piece in pieces]
    n = len(pieces)
    splits = SPLITS if len(SPLITS) == n else (2,) * n
    bits = [1 << i for i in range(n_row.bit_length() - 1)]
    orders = [[1, 4, 2] if n == 4 and len(bits) == 3 and c in FAR_FIRST else bits for c in range(n)]

    in_hbm = pltpu.with_memory_space_constraint(delta, pltpu.HBM)
    sems = pltpu.SemaphoreType.DMA((half // BLOCK,))
    held_other, omega_t, to_send = call(
        functools.partial(first_half_body, n_row, pieces, orders),
        (in_hbm, pltpu.with_memory_space_constraint(omega, pltpu.HBM)),
        [((half, d), BF16), ((k, d), BF16), ((k, half), F32)],
        "aa",
        scratch=[pltpu.VMEM((d, k), BF16), sems, pltpu.SemaphoreType.DMA],
    )
    received = swap(to_send, "col", n_col, 1)
    held_own, kept = call(second_half_body, (in_hbm, omega_t), [((half, d), BF16), ((k, half), F32)], "av", scratch=[sems])
    partial = call(add_chunks_body, (kept, received), [((width, half), F32) for width in widths])
    bit = 2
    while bit < n_col // 2:
        moved = [swap(x, "col", n_col, bit) for x in partial]
        partial = [call(add_body, pair, [(pair[0].shape, F32)])[0] for pair in zip(partial, moved)]
        bit *= 2
    moved = [swap(x, "col", n_col, bit) for x in partial]

    owns, others, befores, pending = {}, {}, {}, {}
    sketch = None
    last = ()
    planned = len(bits) == 3 and n == sum(len(group) for group in GROUPS)
    groups = GROUPS if planned else tuple((c,) for c in range(n))
    modes = MODES if planned else ("pairs",) * n
    steps = ORDER if planned else ()
    if not steps:
        found = []
        for c in range(n):
            found += [(10 * c, f"own{c}"), (10 * c + 1, f"before{c}"), (10 * c + 2, f"send{c}")]
        for g, group in enumerate(groups):
            stages = 2 if modes[g] == "direct" else len(bits)
            found += [(10 * group[-1] + 9.5 + 10 * s, f"add{g}.{s}") for s in range(1, stages)]
        steps = [step for _, step in sorted(found)] + ["sketch"]
    for step in steps:
        weight = WEIGHTS.get(step, 0)
        if step.startswith("own"):
            c = int(step[3:])
            outs = [((widths[c] // splits[c], half), F32)] * splits[c]
            owns[c] = call(add_body, (partial[c], moved[c]), outs, after=last, weight=weight)
            others[c] = [swap(x, "col", n_col, 1) for x in owns[c]]
            last = (owns[c][0],)
        elif step.startswith("before"):
            c = int(step[6:])
            befores[c] = call(product_body, (*owns[c], held_own), [((widths[c], d), F32)], after=last, weight=weight)[0]
            last = (befores[c],)
        elif step.startswith("send"):
            c = int(step[4:])
            outs = [((widths[c] // 2, d), F32)] * 2
            total = pltpu.VMEM((widths[c], d), F32)
            args = (*others[c], held_other, befores[c])
            send, keep = call(product_send_body, args, outs, after=last, scratch=[total], weight=weight)
            pending[(c,)] = keep, swap(send, "row", n_row, bits[0])
            last = (keep,)
        elif step.startswith("add"):
            g, s = (int(x) for x in step[3:].split("."))
            group = groups[g]
            if modes[g] == "direct":
                outs = [((pieces[group[0]], d), F32)] * (n_row // 2)
                body = functools.partial(add_spread_body, n_row // 2)
                own, *sends = call(body, pending[group], outs, after=last, weight=weight)
                flips = [2 * owner_at(flip, n_row // 2) for flip in range(1, n_row // 2)]
                pending[group] = own, *[swap(x, "row", n_row, flip) for x, flip in zip(sends, flips)]
                last = (own,)
                continue
            if s == 1:
                pending[group] = [x for c in group for x in pending[(c,)]]
            segments = [widths[c] >> s for c in group]
            bit = orders[group[0]][s]
            body = functools.partial(add_send_body, bit, segments)
            outs = [((sum(segments) // 2, d), F32)] * 2
            send, keep = call(body, pending[group], outs, after=last, weight=weight)
            pending[group] = keep, swap(send, "row", n_row, bit)
            last = (keep,)
        else:
            parts = [[x for found in halves.values() for x in found] for halves in (owns, others)]
            sketch, done = finish_sketch(n_row, k, pieces, splits, orders, *parts, last)
            last = (done,)
    flat = [x for group in groups for x in pending[group]]
    if per_owner % 8 == 0:
        body = functools.partial(final_corange_body, [len(pending[group]) for group in groups], [sum(pieces[c] for c in group) for group in groups])
        corange = call(body, flat, [((per_owner, d), F32)], after=last, results=1, weight=WEIGHTS.get("F", 0))[0]
    else:
        corange = jnp.concatenate([functools.reduce(jnp.add, pending[group]) for group in groups], axis=0)
    return sketch, corange.T


def finish_sketch(n_row, k, pieces, splits, orders, owns, others, after):
    half = owns[0].shape[1]
    if k // n_row % 8 == 0:
        body = functools.partial(final_sketch_body, n_row, pieces, splits, orders)
        return call(body, (*owns, *others), [((2 * half, k), F32), ((8, 128), F32)], after=after, results=1)
    places = jnp.array([place_of(r, orders[0]) for r in range(n_row)])

    def columns(parts):
        starts = [sum(splits[:c]) for c in range(len(splits))]
        parts = [jnp.concatenate(parts[start : start + split], axis=0) for start, split in zip(starts, splits)]
        found = [part.reshape(n_row, piece, half)[places] for part, piece in zip(parts, pieces)]
        return jnp.concatenate(found, axis=1).reshape(k, half).T

    own, other = columns(owns), columns(others)
    first = lax.rem(lax.axis_index("col"), 2) == 0
    return jnp.where(first, jnp.concatenate([own, other]), jnp.concatenate([other, own])), after[0]


def solution(mesh):
    body = functools.partial(shards, mesh.shape["row"], mesh.shape["col"])
    in_specs = (P("row", "col"), P("col", None))
    out_specs = (P("row", None), P("col", "row"))
    return jax.shard_map(body, mesh=mesh, in_specs=in_specs, out_specs=out_specs, check_vma=False)
```

```python
import functools

import jax
import jax.numpy as jnp
from jax import lax
from jax.experimental import pallas as pl
from jax.experimental.pallas import tpu as pltpu
from jax.sharding import PartitionSpec as P

EIGHTHS = (2,2,2,2)
BLOCK = 512
F32 = jnp.float32
BF16 = jnp.bfloat16
NT = (((1,), (1,)), ((), ()))
SPECS = {"v": pl.BlockSpec(memory_space=pltpu.VMEM), "a": pl.BlockSpec(memory_space=pl.ANY)}
ORDER = ('own0', 'before0', 'send0', 'own1', 'before1', 'send1', 'add0.1', 'own2', 'before2', 'send2', 'add1.1', 'own3', 'before3', 'send3', 'add2.1', 'add1.2', 'add0.2', 'add2.2', 'add3.1', 'sketch')
WEIGHTS = {'add2.1': 500000000, 'F': 500000000, 'send1': 0, 'send0': 0, 'send3': 0, 'add2.2': 200000000, 'add0.2': 1000000000, 'own2': 500000000, 'before1': 500000000, 'add0.1': 500000000, 'before3': 2000000000, 'sketch': 500000000, 'send2': 0, 'add1.2': 200000000}
SPLITS = (2,2,2,2)
GROUPS = ((0,),(1,),(2,),(3,))
MODES = ('pairs','pairs','pairs','direct')


def call(body, args, outs, kinds=None, after=(), scratch=(), results=0, weight=0):
    n = len(args)
    kinds = (kinds or "v" * n) + "a" * len(after)

    def run(*refs):
        body(*refs[:n], *refs[len(kinds) :])

    return pl.pallas_call(
        run,
        out_shape=[pltpu.VMEM(*o) if i >= results else jax.ShapeDtypeStruct(*o) for i, o in enumerate(outs)],
        in_specs=[SPECS[kind] for kind in kinds],
        out_specs=[SPECS["v"]] * len(outs),
        scratch_shapes=list(scratch),
        cost_estimate=pl.CostEstimate(flops=weight, bytes_accessed=0, transcendentals=0),
        compiler_params=pltpu.CompilerParams(vmem_limit_bytes=16 << 20),
    )(*args, *after)


def owner_at(index, n_row):
    owner, bit = index * 0, 1
    while bit < n_row:
        owner = 2 * owner + index % 2
        index = index // 2
        bit *= 2
    return owner


def column_of(position, k, n_row, pieces):
    column, first, done = position * 0, 0, 0
    for piece in pieces:
        rest = position - first
        found = owner_at(rest // piece, n_row) * (k // n_row) + done + rest % piece
        column = jnp.where((rest >= 0) & (rest < piece * n_row), found, column)
        first += piece * n_row
        done += piece
    return column


def stream_half(delta, held, sem, mine, skipped=0):
    rows = delta.shape[0] // 2
    parity = lax.rem(lax.axis_index("col"), 2)
    first = (parity if mine else 1 - parity) * rows + skipped
    copies = []
    for b in range(held.shape[0] // BLOCK):
        source = delta.at[pl.ds(pl.multiple_of(first + b * BLOCK, BLOCK), BLOCK), :]
        copies.append(pltpu.make_async_copy(source, held.at[pl.ds(b * BLOCK, BLOCK), :], sem.at[b]))
        copies[-1].start()
    return copies


def sketch_half(omega_t, held, copies, out, skipped=0):
    for b, copy in enumerate(copies):
        copy.wait()
        rows, lanes = pl.ds(b * BLOCK, BLOCK), pl.ds(skipped + b * BLOCK, BLOCK)
        out[:, lanes] = lax.dot_general(omega_t[...], held[rows, :], NT, preferred_element_type=F32)


def first_half_body(n_row, pieces, delta, omega, held, omega_t, out, ahead, omega_v, sem, omega_sem, ahead_sem):
    k = out.shape[0]
    fetch = pltpu.make_async_copy(omega, omega_v, omega_sem)
    fetch.start()
    copies = stream_half(delta, held, sem, False)
    early = stream_half(delta, ahead, ahead_sem, True)
    position = lax.broadcasted_iota(jnp.int32, (k, k), 0)
    column = lax.broadcasted_iota(jnp.int32, (k, k), 1)
    pick = jnp.where(column_of(position, k, n_row, pieces) == column, 1.0, 0.0).astype(BF16)
    fetch.wait()
    omega_t[...] = lax.dot_general(pick, omega_v[...], NT, preferred_element_type=F32).astype(BF16)
    sketch_half(omega_t, held, copies, out)
    for copy in early:
        copy.wait()


def second_half_body(delta, omega_t, ahead, held, out, sem):
    copies = stream_half(delta, held, sem, True, BLOCK)
    out[:, pl.ds(0, BLOCK)] = lax.dot_general(omega_t[...], ahead[...], NT, preferred_element_type=F32)
    sketch_half(omega_t, held, copies, out, BLOCK)


def add_chunks_body(kept, received, *outs):
    first = 0
    for out in outs:
        part = pl.ds(first, out.shape[0])
        out[...] = kept[part, :] + received[part, :]
        first += out.shape[0]


def add_body(a, b, *outs):
    first = 0
    for out in outs:
        part = pl.ds(first, out.shape[0])
        out[...] = a[part, :] + b[part, :]
        first += out.shape[0]


def joined(refs):
    return jnp.concatenate([ref[...] for ref in refs], axis=0)


def product_body(*refs):
    *sketch, ahead, held, out = refs
    rounded = joined(sketch).astype(BF16)
    total = jnp.dot(rounded[:, :BLOCK], ahead[...], preferred_element_type=F32)
    out[...] = total + jnp.dot(rounded[:, BLOCK:], held[...], preferred_element_type=F32)


def split(bit, segments, refs, send, keep):
    own = lax.rem(lax.axis_index("row") // bit, 2)
    start, first = 0, 0
    for rows in segments:
        half = rows // 2
        for out, which in ((send, 1 - own), (keep, own)):
            if half % 8:
                low, high = (
                    functools.reduce(jnp.add, [ref[pl.ds(start + i * half, half), :] for ref in refs]) for i in range(2)
                )
                value = jnp.where(which == 0, low, high)
            else:
                part = pl.ds(pl.multiple_of(start + which * half, 8), half)
                value = functools.reduce(jnp.add, [ref[part, :] for ref in refs])
            out[pl.ds(first, half), :] = value
        start += rows
        first += half


def product_send_body(*refs):
    *sketch, held, before, send, keep, total = refs
    total[...] = before[...] + jnp.dot(joined(sketch).astype(BF16), held[...], preferred_element_type=F32)
    split(1, [total.shape[0]], [total], send, keep)


def add_send_body(bit, segments, *refs):
    *pairs, send, keep = refs
    first = 0
    for kept, got in zip(pairs[::2], pairs[1::2]):
        mine = segments if len(pairs) == 2 else [kept.shape[0]]
        half = kept.shape[0] // 2
        part = pl.ds(first, half)
        split(bit, mine, [kept, got], send.at[part, :], keep.at[part, :])
        first += half


def add_spread_body(n_high, kept, received, *outs):
    piece = outs[0].shape[0]
    place = owner_at(lax.axis_index("row") // 2, n_high)
    for flip, out in enumerate(outs):
        which = lax.bitwise_xor(place, flip)
        if piece % 8 == 0:
            part = pl.ds(pl.multiple_of(which * piece, piece), piece)
            out[...] = kept[part, :] + received[part, :]
            continue
        found = jnp.zeros(out.shape, F32)
        for i in range(n_high):
            part = pl.ds(i * piece, piece)
            found = jnp.where(which == i, kept[part, :] + received[part, :], found)
        out[...] = found


def final_corange_body(counts, rows, *refs):
    out = refs[-1]
    first, used = 0, 0
    for count, piece in zip(counts, rows):
        terms = refs[used : used + count]
        parts = [term[pl.ds(i, piece), :] for term in terms for i in range(0, term.shape[0], piece)]
        out[pl.ds(first, piece), :] = functools.reduce(jnp.add, parts)
        first += piece
        used += count


def final_sketch_body(n_row, pieces, splits, *refs):
    out, done = refs[-2:]
    n, rows = sum(splits), refs[0].shape[1]
    parity = lax.rem(lax.axis_index("col"), 2)
    for side in range(2):
        parts = refs[side * n : (side + 1) * n]
        first = (parity if side == 0 else 1 - parity) * rows
        for b in range(rows // 128):
            lanes = pl.ds(b * 128, 128)
            found = []
            for r in range(n_row):
                place, used = owner_at(r, n_row), 0
                for piece, split in zip(pieces, splits):
                    per_part = n_row // split
                    part = parts[used + place // per_part]
                    found.append(part[pl.ds(place % per_part * piece, piece), lanes])
                    used += split
            block = jnp.concatenate(found, axis=0)
            out[pl.ds(pl.multiple_of(first + b * 128, 128), 128), :] = block.T
    done[...] = jnp.zeros_like(done)


def swap(x, axis, size, bit):
    return lax.ppermute(x, axis, [(i, i ^ bit) for i in range(size)])


def shards(n_row, n_col, delta, omega):
    rows, d = delta.shape
    k = omega.shape[1]
    half = rows // 2
    per_owner = k // n_row
    pieces = [per_owner * part // sum(EIGHTHS) for part in EIGHTHS] if per_owner % 8 == 0 else [1] * per_owner
    widths = [piece * n_row for piece in pieces]
    n = len(pieces)
    splits = SPLITS if len(SPLITS) == n else (2,) * n
    bits = [1 << i for i in range(n_row.bit_length() - 1)]

    in_hbm = pltpu.with_memory_space_constraint(delta, pltpu.HBM)
    sems = pltpu.SemaphoreType.DMA((half // BLOCK,))
    held_other, omega_t, to_send, ahead = call(
        functools.partial(first_half_body, n_row, pieces),
        (in_hbm, pltpu.with_memory_space_constraint(omega, pltpu.HBM)),
        [((half, d), BF16), ((k, d), BF16), ((k, half), F32), ((BLOCK, d), BF16)],
        "aa",
        scratch=[pltpu.VMEM((d, k), BF16), sems, pltpu.SemaphoreType.DMA, pltpu.SemaphoreType.DMA((1,))],
    )
    received = swap(to_send, "col", n_col, 1)
    held_own, kept = call(second_half_body, (in_hbm, omega_t, ahead), [((half - BLOCK, d), BF16), ((k, half), F32)], "avv", scratch=[sems])
    partial = call(add_chunks_body, (kept, received), [((width, half), F32) for width in widths])
    bit = 2
    while bit < n_col // 2:
        moved = [swap(x, "col", n_col, bit) for x in partial]
        partial = [call(add_body, pair, [(pair[0].shape, F32)])[0] for pair in zip(partial, moved)]
        bit *= 2
    moved = [swap(x, "col", n_col, bit) for x in partial]

    owns, others, befores, pending = {}, {}, {}, {}
    sketch = None
    last = ()
    planned = len(bits) == 3 and n == sum(len(group) for group in GROUPS)
    groups = GROUPS if planned else tuple((c,) for c in range(n))
    modes = MODES if planned else ("pairs",) * n
    steps = ORDER if planned else ()
    if not steps:
        found = []
        for c in range(n):
            found += [(10 * c, f"own{c}"), (10 * c + 1, f"before{c}"), (10 * c + 2, f"send{c}")]
        for g, group in enumerate(groups):
            stages = 2 if modes[g] == "direct" else len(bits)
            found += [(10 * group[-1] + 9.5 + 10 * s, f"add{g}.{s}") for s in range(1, stages)]
        steps = [step for _, step in sorted(found)] + ["sketch"]
    for step in steps:
        weight = WEIGHTS.get(step, 0)
        if step.startswith("own"):
            c = int(step[3:])
            outs = [((widths[c] // splits[c], half), F32)] * splits[c]
            owns[c] = call(add_body, (partial[c], moved[c]), outs, after=last, weight=weight)
            others[c] = [swap(x, "col", n_col, 1) for x in owns[c]]
            last = (owns[c][0],)
        elif step.startswith("before"):
            c = int(step[6:])
            befores[c] = call(product_body, (*owns[c], ahead, held_own), [((widths[c], d), F32)], after=last, weight=weight)[0]
            last = (befores[c],)
        elif step.startswith("send"):
            c = int(step[4:])
            outs = [((widths[c] // 2, d), F32)] * 2
            total = pltpu.VMEM((widths[c], d), F32)
            args = (*others[c], held_other, befores[c])
            send, keep = call(product_send_body, args, outs, after=last, scratch=[total], weight=weight)
            pending[(c,)] = keep, swap(send, "row", n_row, bits[0])
            last = (keep,)
        elif step.startswith("add"):
            g, s = (int(x) for x in step[3:].split("."))
            group = groups[g]
            if modes[g] == "direct":
                outs = [((pieces[group[0]], d), F32)] * (n_row // 2)
                body = functools.partial(add_spread_body, n_row // 2)
                own, *sends = call(body, pending[group], outs, after=last, weight=weight)
                flips = [2 * owner_at(flip, n_row // 2) for flip in range(1, n_row // 2)]
                pending[group] = own, *[swap(x, "row", n_row, flip) for x, flip in zip(sends, flips)]
                last = (own,)
                continue
            if s == 1:
                pending[group] = [x for c in group for x in pending[(c,)]]
            segments = [widths[c] >> s for c in group]
            body = functools.partial(add_send_body, bits[s], segments)
            outs = [((sum(segments) // 2, d), F32)] * 2
            send, keep = call(body, pending[group], outs, after=last, weight=weight)
            pending[group] = keep, swap(send, "row", n_row, bits[s])
            last = (keep,)
        else:
            parts = [[x for found in halves.values() for x in found] for halves in (owns, others)]
            sketch, done = finish_sketch(n_row, k, pieces, splits, *parts, last)
            last = (done,)
    flat = [x for group in groups for x in pending[group]]
    if per_owner % 8 == 0:
        body = functools.partial(final_corange_body, [len(pending[group]) for group in groups], [sum(pieces[c] for c in group) for group in groups])
        corange = call(body, flat, [((per_owner, d), F32)], after=last, results=1, weight=WEIGHTS.get("F", 0))[0]
    else:
        corange = jnp.concatenate([functools.reduce(jnp.add, pending[group]) for group in groups], axis=0)
    return sketch, corange.T


def finish_sketch(n_row, k, pieces, splits, owns, others, after):
    half = owns[0].shape[1]
    if k // n_row % 8 == 0:
        body = functools.partial(final_sketch_body, n_row, pieces, splits)
        return call(body, (*owns, *others), [((2 * half, k), F32), ((8, 128), F32)], after=after, results=1)
    places = jnp.array([owner_at(r, n_row) for r in range(n_row)])

    def columns(parts):
        starts = [sum(splits[:c]) for c in range(len(splits))]
        parts = [jnp.concatenate(parts[start : start + split], axis=0) for start, split in zip(starts, splits)]
        found = [part.reshape(n_row, piece, half)[places] for part, piece in zip(parts, pieces)]
        return jnp.concatenate(found, axis=1).reshape(k, half).T

    own, other = columns(owns), columns(others)
    first = lax.rem(lax.axis_index("col"), 2) == 0
    return jnp.where(first, jnp.concatenate([own, other]), jnp.concatenate([other, own])), after[0]


def solution(mesh):
    body = functools.partial(shards, mesh.shape["row"], mesh.shape["col"])
    in_specs = (P("row", "col"), P("col", None))
    out_specs = (P("row", None), P("col", "row"))
    return jax.shard_map(body, mesh=mesh, in_specs=in_specs, out_specs=out_specs, check_vma=False)
```

```python
import functools

import jax
import jax.numpy as jnp
from jax import lax
from jax.experimental import pallas as pl
from jax.experimental.pallas import tpu as pltpu
from jax.sharding import PartitionSpec as P

EIGHTHS = (2,2,2,2)
BLOCK = 512
F32 = jnp.float32
BF16 = jnp.bfloat16
NT = (((1,), (1,)), ((), ()))
SPECS = {"v": pl.BlockSpec(memory_space=pltpu.VMEM), "a": pl.BlockSpec(memory_space=pl.ANY)}
ORDER = ('own0', 'before0', 'send0', 'own1', 'before1', 'send1', 'add0.1', 'own2', 'before2', 'send2', 'add1.1', 'own3', 'before3', 'send3', 'add2.1', 'add1.2', 'add0.2', 'add2.2', 'add3.1', 'sketch')
WEIGHTS = {'add2.1': 500000000, 'F': 500000000, 'send1': 0, 'send0': 0, 'send3': 0, 'add2.2': 200000000, 'add0.2': 1000000000, 'own2': 500000000, 'before1': 500000000, 'add0.1': 500000000, 'before3': 2000000000, 'sketch': 500000000, 'send2': 0, 'add1.2': 200000000}
SPLITS = (2,2,2,2)
GROUPS = ((0,),(1,),(2,),(3,))
MODES = ('pairs','pairs','pairs','direct')


def call(body, args, outs, kinds=None, after=(), scratch=(), results=0, weight=0):
    n = len(args)
    kinds = (kinds or "v" * n) + "a" * len(after)

    def run(*refs):
        body(*refs[:n], *refs[len(kinds) :])

    return pl.pallas_call(
        run,
        out_shape=[pltpu.VMEM(*o) if i >= results else jax.ShapeDtypeStruct(*o) for i, o in enumerate(outs)],
        in_specs=[SPECS[kind] for kind in kinds],
        out_specs=[SPECS["v"]] * len(outs),
        scratch_shapes=list(scratch),
        cost_estimate=pl.CostEstimate(flops=weight, bytes_accessed=0, transcendentals=0),
        compiler_params=pltpu.CompilerParams(vmem_limit_bytes=16 << 20),
    )(*args, *after)


def owner_at(index, n_row):
    owner, bit = index * 0, 1
    while bit < n_row:
        owner = 2 * owner + index % 2
        index = index // 2
        bit *= 2
    return owner


def column_of(position, k, n_row, pieces):
    column, first, done = position * 0, 0, 0
    for piece in pieces:
        rest = position - first
        found = owner_at(rest // piece, n_row) * (k // n_row) + done + rest % piece
        column = jnp.where((rest >= 0) & (rest < piece * n_row), found, column)
        first += piece * n_row
        done += piece
    return column


def stream_half(delta, held, sem, mine, skipped=0):
    rows = delta.shape[0] // 2
    parity = lax.rem(lax.axis_index("col"), 2)
    first = (parity if mine else 1 - parity) * rows + skipped
    copies = []
    for b in range(held.shape[0] // BLOCK):
        source = delta.at[pl.ds(pl.multiple_of(first + b * BLOCK, BLOCK), BLOCK), :]
        copies.append(pltpu.make_async_copy(source, held.at[pl.ds(b * BLOCK, BLOCK), :], sem.at[b]))
        copies[-1].start()
    return copies


def sketch_half(omega_t, held, copies, out, skipped=0):
    for b, copy in enumerate(copies):
        copy.wait()
        rows, lanes = pl.ds(b * BLOCK, BLOCK), pl.ds(skipped + b * BLOCK, BLOCK)
        out[:, lanes] = lax.dot_general(omega_t[...], held[rows, :], NT, preferred_element_type=F32)


def first_half_body(n_row, pieces, delta, omega, held, omega_t, out, ahead, head, omega_v, sem, omega_sem, ahead_sem):
    k = out.shape[0]
    fetch = pltpu.make_async_copy(omega, omega_v, omega_sem)
    fetch.start()
    copies = stream_half(delta, held, sem, False)
    early = stream_half(delta, ahead, ahead_sem, True)
    position = lax.broadcasted_iota(jnp.int32, (k, k), 0)
    column = lax.broadcasted_iota(jnp.int32, (k, k), 1)
    pick = jnp.where(column_of(position, k, n_row, pieces) == column, 1.0, 0.0).astype(BF16)
    fetch.wait()
    omega_t[...] = lax.dot_general(pick, omega_v[...], NT, preferred_element_type=F32).astype(BF16)
    sketch_half(omega_t, held, copies, out)
    head[...] = out[pl.ds(0, head.shape[0]), :]
    for copy in early:
        copy.wait()


def second_half_body(delta, omega_t, ahead, held, out, sem):
    copies = stream_half(delta, held, sem, True, BLOCK)
    out[:, pl.ds(0, BLOCK)] = lax.dot_general(omega_t[...], ahead[...], NT, preferred_element_type=F32)
    sketch_half(omega_t, held, copies, out, BLOCK)


def add_head_body(kept, received, out):
    out[...] = kept[pl.ds(0, out.shape[0]), :] + received[...]


def add_chunks_body(skipped, kept, received, *outs):
    first = 0
    for out in outs:
        rows = out.shape[0]
        out[...] = kept[pl.ds(skipped + first, rows), :] + received[pl.ds(first, rows), :]
        first += rows


def add_body(a, b, *outs):
    first = 0
    for out in outs:
        part = pl.ds(first, out.shape[0])
        out[...] = a[part, :] + b[part, :]
        first += out.shape[0]


def joined(refs):
    return jnp.concatenate([ref[...] for ref in refs], axis=0)


def product_body(*refs):
    *sketch, ahead, held, out = refs
    rounded = joined(sketch).astype(BF16)
    total = jnp.dot(rounded[:, :BLOCK], ahead[...], preferred_element_type=F32)
    out[...] = total + jnp.dot(rounded[:, BLOCK:], held[...], preferred_element_type=F32)


def split(bit, segments, refs, send, keep):
    own = lax.rem(lax.axis_index("row") // bit, 2)
    start, first = 0, 0
    for rows in segments:
        half = rows // 2
        for out, which in ((send, 1 - own), (keep, own)):
            if half % 8:
                low, high = (
                    functools.reduce(jnp.add, [ref[pl.ds(start + i * half, half), :] for ref in refs]) for i in range(2)
                )
                value = jnp.where(which == 0, low, high)
            else:
                part = pl.ds(pl.multiple_of(start + which * half, 8), half)
                value = functools.reduce(jnp.add, [ref[part, :] for ref in refs])
            out[pl.ds(first, half), :] = value
        start += rows
        first += half


def product_send_body(*refs):
    *sketch, held, before, send, keep, total = refs
    total[...] = before[...] + jnp.dot(joined(sketch).astype(BF16), held[...], preferred_element_type=F32)
    split(1, [total.shape[0]], [total], send, keep)


def add_send_body(bit, segments, *refs):
    *pairs, send, keep = refs
    first = 0
    for kept, got in zip(pairs[::2], pairs[1::2]):
        mine = segments if len(pairs) == 2 else [kept.shape[0]]
        half = kept.shape[0] // 2
        part = pl.ds(first, half)
        split(bit, mine, [kept, got], send.at[part, :], keep.at[part, :])
        first += half


def add_spread_body(n_high, kept, received, *outs):
    piece = outs[0].shape[0]
    place = owner_at(lax.axis_index("row") // 2, n_high)
    for flip, out in enumerate(outs):
        which = lax.bitwise_xor(place, flip)
        if piece % 8 == 0:
            part = pl.ds(pl.multiple_of(which * piece, piece), piece)
            out[...] = kept[part, :] + received[part, :]
            continue
        found = jnp.zeros(out.shape, F32)
        for i in range(n_high):
            part = pl.ds(i * piece, piece)
            found = jnp.where(which == i, kept[part, :] + received[part, :], found)
        out[...] = found


def final_corange_body(counts, rows, *refs):
    out = refs[-1]
    first, used = 0, 0
    for count, piece in zip(counts, rows):
        terms = refs[used : used + count]
        parts = [term[pl.ds(i, piece), :] for term in terms for i in range(0, term.shape[0], piece)]
        out[pl.ds(first, piece), :] = functools.reduce(jnp.add, parts)
        first += piece
        used += count


def final_sketch_body(n_row, pieces, splits, *refs):
    out, done = refs[-2:]
    n, rows = sum(splits), refs[0].shape[1]
    parity = lax.rem(lax.axis_index("col"), 2)
    for side in range(2):
        parts = refs[side * n : (side + 1) * n]
        first = (parity if side == 0 else 1 - parity) * rows
        for b in range(rows // 128):
            lanes = pl.ds(b * 128, 128)
            found = []
            for r in range(n_row):
                place, used = owner_at(r, n_row), 0
                for piece, split in zip(pieces, splits):
                    per_part = n_row // split
                    part = parts[used + place // per_part]
                    found.append(part[pl.ds(place % per_part * piece, piece), lanes])
                    used += split
            block = jnp.concatenate(found, axis=0)
            out[pl.ds(pl.multiple_of(first + b * 128, 128), 128), :] = block.T
    done[...] = jnp.zeros_like(done)


def swap(x, axis, size, bit):
    return lax.ppermute(x, axis, [(i, i ^ bit) for i in range(size)])


def shards(n_row, n_col, delta, omega):
    rows, d = delta.shape
    k = omega.shape[1]
    half = rows // 2
    per_owner = k // n_row
    pieces = [per_owner * part // sum(EIGHTHS) for part in EIGHTHS] if per_owner % 8 == 0 else [1] * per_owner
    widths = [piece * n_row for piece in pieces]
    n = len(pieces)
    splits = SPLITS if len(SPLITS) == n else (2,) * n
    bits = [1 << i for i in range(n_row.bit_length() - 1)]

    in_hbm = pltpu.with_memory_space_constraint(delta, pltpu.HBM)
    sems = pltpu.SemaphoreType.DMA((half // BLOCK,))
    held_other, omega_t, to_send, ahead, head = call(
        functools.partial(first_half_body, n_row, pieces),
        (in_hbm, pltpu.with_memory_space_constraint(omega, pltpu.HBM)),
        [((half, d), BF16), ((k, d), BF16), ((k, half), F32), ((BLOCK, d), BF16), ((widths[0], half), F32)],
        "aa",
        scratch=[pltpu.VMEM((d, k), BF16), sems, pltpu.SemaphoreType.DMA, pltpu.SemaphoreType.DMA((1,))],
    )
    received_head = swap(head, "col", n_col, 1)
    received = swap(to_send[widths[0] :], "col", n_col, 1)
    held_own, kept = call(second_half_body, (in_hbm, omega_t, ahead), [((half - BLOCK, d), BF16), ((k, half), F32)], "avv", scratch=[sems])
    partial = call(add_head_body, (kept, received_head), [((widths[0], half), F32)])
    outs = [((width, half), F32) for width in widths[1:]]
    partial += call(functools.partial(add_chunks_body, widths[0]), (kept, received), outs, after=partial)
    bit = 2
    while bit < n_col // 2:
        moved = [swap(x, "col", n_col, bit) for x in partial]
        partial = [call(add_body, pair, [(pair[0].shape, F32)])[0] for pair in zip(partial, moved)]
        bit *= 2
    moved = [swap(x, "col", n_col, bit) for x in partial]

    owns, others, befores, pending = {}, {}, {}, {}
    sketch = None
    last = ()
    planned = len(bits) == 3 and n == sum(len(group) for group in GROUPS)
    groups = GROUPS if planned else tuple((c,) for c in range(n))
    modes = MODES if planned else ("pairs",) * n
    steps = ORDER if planned else ()
    if not steps:
        found = []
        for c in range(n):
            found += [(10 * c, f"own{c}"), (10 * c + 1, f"before{c}"), (10 * c + 2, f"send{c}")]
        for g, group in enumerate(groups):
            stages = 2 if modes[g] == "direct" else len(bits)
            found += [(10 * group[-1] + 9.5 + 10 * s, f"add{g}.{s}") for s in range(1, stages)]
        steps = [step for _, step in sorted(found)] + ["sketch"]
    for step in steps:
        weight = WEIGHTS.get(step, 0)
        if step.startswith("own"):
            c = int(step[3:])
            outs = [((widths[c] // splits[c], half), F32)] * splits[c]
            owns[c] = call(add_body, (partial[c], moved[c]), outs, after=last, weight=weight)
            others[c] = [swap(x, "col", n_col, 1) for x in owns[c]]
            last = (owns[c][0],)
        elif step.startswith("before"):
            c = int(step[6:])
            befores[c] = call(product_body, (*owns[c], ahead, held_own), [((widths[c], d), F32)], after=last, weight=weight)[0]
            last = (befores[c],)
        elif step.startswith("send"):
            c = int(step[4:])
            outs = [((widths[c] // 2, d), F32)] * 2
            total = pltpu.VMEM((widths[c], d), F32)
            args = (*others[c], held_other, befores[c])
            send, keep = call(product_send_body, args, outs, after=last, scratch=[total], weight=weight)
            pending[(c,)] = keep, swap(send, "row", n_row, bits[0])
            last = (keep,)
        elif step.startswith("add"):
            g, s = (int(x) for x in step[3:].split("."))
            group = groups[g]
            if modes[g] == "direct":
                outs = [((pieces[group[0]], d), F32)] * (n_row // 2)
                body = functools.partial(add_spread_body, n_row // 2)
                own, *sends = call(body, pending[group], outs, after=last, weight=weight)
                flips = [2 * owner_at(flip, n_row // 2) for flip in range(1, n_row // 2)]
                pending[group] = own, *[swap(x, "row", n_row, flip) for x, flip in zip(sends, flips)]
                last = (own,)
                continue
            if s == 1:
                pending[group] = [x for c in group for x in pending[(c,)]]
            segments = [widths[c] >> s for c in group]
            body = functools.partial(add_send_body, bits[s], segments)
            outs = [((sum(segments) // 2, d), F32)] * 2
            send, keep = call(body, pending[group], outs, after=last, weight=weight)
            pending[group] = keep, swap(send, "row", n_row, bits[s])
            last = (keep,)
        else:
            parts = [[x for found in halves.values() for x in found] for halves in (owns, others)]
            sketch, done = finish_sketch(n_row, k, pieces, splits, *parts, last)
            last = (done,)
    flat = [x for group in groups for x in pending[group]]
    if per_owner % 8 == 0:
        body = functools.partial(final_corange_body, [len(pending[group]) for group in groups], [sum(pieces[c] for c in group) for group in groups])
        corange = call(body, flat, [((per_owner, d), F32)], after=last, results=1, weight=WEIGHTS.get("F", 0))[0]
    else:
        corange = jnp.concatenate([functools.reduce(jnp.add, pending[group]) for group in groups], axis=0)
    return sketch, corange.T


def finish_sketch(n_row, k, pieces, splits, owns, others, after):
    half = owns[0].shape[1]
    if k // n_row % 8 == 0:
        body = functools.partial(final_sketch_body, n_row, pieces, splits)
        return call(body, (*owns, *others), [((2 * half, k), F32), ((8, 128), F32)], after=after, results=1)
    places = jnp.array([owner_at(r, n_row) for r in range(n_row)])

    def columns(parts):
        starts = [sum(splits[:c]) for c in range(len(splits))]
        parts = [jnp.concatenate(parts[start : start + split], axis=0) for start, split in zip(starts, splits)]
        found = [part.reshape(n_row, piece, half)[places] for part, piece in zip(parts, pieces)]
        return jnp.concatenate(found, axis=1).reshape(k, half).T

    own, other = columns(owns), columns(others)
    first = lax.rem(lax.axis_index("col"), 2) == 0
    return jnp.where(first, jnp.concatenate([own, other]), jnp.concatenate([other, own])), after[0]


def solution(mesh):
    body = functools.partial(shards, mesh.shape["row"], mesh.shape["col"])
    in_specs = (P("row", "col"), P("col", None))
    out_specs = (P("row", None), P("col", "row"))
    return jax.shard_map(body, mesh=mesh, in_specs=in_specs, out_specs=out_specs, check_vma=False)
```
